32 devices in a mesh: seq: 8 (over y, x, core), head: 4 (over z).
Axes of the slice: x: 2, y: 2, z: 4, core: 2. Of those that a mesh axis runs over, the one named last changes fastest.
Arguments:
- queries: bfloat16 [8192, 32, 128], P('seq', 'head'), may hold values from -6 to 6
- keys: bfloat16 [8192, 32, 128], P('seq', 'head'), may hold values from -6 to 6
- values: bfloat16 [8192, 32, 128], P('seq', 'head'), may hold values from -6 to 6
- out_grad: bfloat16 [8192, 32, 128], P('seq', 'head'), may hold values from -6 to 6
- level_codes: int32 [21, 8192], P(None, ('seq', 'head')), may hold values from 1 to 16
Outputs:
- query_grad: bfloat16 [8192, 32, 128], P('seq', 'head')
- key_grad: bfloat16 [8192, 32, 128], P('seq', 'head')
- value_grad: bfloat16 [8192, 32, 128], P('seq', 'head')
The draws below stay inside these ranges and needn't reach their ends.
Inputs may be any that keep to these rules, and one draw needn't show every extreme that they name: `level_codes`: level codes are whole numbers.
All inputs are finite; a program needn't handle non-finite values.
Results may differ from the reference program's by a relative error of at most 0.0052.
Values sent between devices are 32-bit elements; how exact they have to be, the bound alone decides.
No kernel may reach another device: no remote copies, remote signals or barrier semaphores. Data moves between devices by JAX's collectives and lax.ppermute only.
A program may use at most 128 MiB of HBM per device.

```python
import jax
import jax.numpy as jnp
from jax import lax

H = 32
HD = 128
LEVELS = 21
TOK_DEV = 1024
TOKENS = 8192


def set_ends(array, key, least, largest):
    shape = array.shape
    spot = [jax.random.randint(jax.random.fold_in(key, axis), (), 0, shape[axis]) for axis in range(len(shape))]
    array = array.at[tuple(spot)].set(least)
    longest = shape.index(max(shape))
    spot[longest] = (spot[longest] + 1) % shape[longest]
    return array.at[tuple(spot)].set(largest)


def levels(stream_key, extent, pieces, low, largest):
    def one(position, shards_of):
        steps = jax.random.uniform(jax.random.fold_in(jax.random.fold_in(stream_key, 6), position), (shards_of,), jnp.float32, low / len(pieces), largest / len(pieces))
        return jnp.repeat(jnp.exp(steps), extent[position] // shards_of).reshape((-1,) + (1,) * (len(extent) - position - 1))

    loudness = one(*pieces[0])
    for cut in pieces[1:]:
        loudness = loudness * one(*cut)
    return loudness


def noise(rng, extent, scale, most, cuts=(), kind=jnp.bfloat16):
    entries = scale * jax.random.normal(rng, extent, jnp.float32)
    if cuts:
        entries = entries * levels(rng, extent, cuts, -0.22, 0.18)
    return jnp.clip(entries, -most, most).astype(kind)


def setup_inputs(seed: int = 0) -> dict:
    arg_keys = jax.random.split(jax.random.key(seed), 6)
    return {
        "queries": noise(arg_keys[0], (TOKENS, H, HD), 1.0, 6.0, ((0, 8), (1, 4))),
        "keys": noise(arg_keys[1], (TOKENS, H, HD), 1.0, 6.0, ((0, 8), (1, 4))),
        "values": noise(arg_keys[2], (TOKENS, H, HD), 1.0, 6.0, ((0, 8), (1, 4))),
        "out_grad": noise(arg_keys[3], (TOKENS, H, HD), 1.0, 6.0, ((0, 8), (1, 4))),
        "level_codes": set_ends(jax.random.randint(arg_keys[4], (LEVELS, TOKENS), 1, 17), jax.random.fold_in(arg_keys[4], 1), 1, 16).astype(jnp.int32),
    }


def level_weights(codes):
    order = jnp.arange(codes.shape[0], dtype=jnp.float32)
    factor = jnp.exp2(-0.5 * jnp.maximum(order - 1.0, 0.0)) / 16.0
    return codes.astype(jnp.float32) * factor[:, None]


def level_matrix(count, bits):
    rows = jnp.arange(count, dtype=jnp.int32)[:, None]
    cols = jnp.arange(count, dtype=jnp.int32)[None, :]
    differ = jnp.bitwise_xor(rows, cols)
    depth = jnp.zeros((count, count), jnp.int32)
    for power in range(bits):
        depth = depth + (differ >= (1 << power)).astype(jnp.int32)
    return jnp.where(cols <= rows, depth, -1)


def level_mask(depth, lam, bits):
    mask = jnp.zeros(depth.shape, jnp.float32)
    for level in range(bits + 1):
        mask = mask + jnp.where(depth == level, lam[level][:, None], 0.0)
    return mask


def local_head(mask, scale, query, key, value, grad):
    inner = (((1,), (1,)), ((), ()))
    outer = (((0,), (0,)), ((), ()))
    scores = lax.dot_general(query, key, inner, preferred_element_type=jnp.float32)
    dprob = lax.dot_general(grad, value, inner, preferred_element_type=jnp.float32)
    weight_q = (mask * (scale * dprob)).astype(jnp.bfloat16)
    weight_v = (mask * (scale * scores)).astype(jnp.bfloat16)
    dquery = jnp.dot(weight_q, key, preferred_element_type=jnp.float32)
    dkey = lax.dot_general(weight_q, query, outer, preferred_element_type=jnp.float32)
    dvalue = lax.dot_general(weight_v, grad, outer, preferred_element_type=jnp.float32)
    return dquery, dkey, dvalue


def reference(queries, keys, values, out_grad, level_codes):
    tokens, heads, width = queries.shape
    scale = width ** -0.5
    groups = tokens // TOK_DEV
    local_bits = TOK_DEV.bit_length() - 1
    tree_bits = groups.bit_length() - 1
    highest = lax.Precision.HIGHEST
    lam = level_weights(level_codes)
    lam_blocks = jnp.swapaxes(lam.reshape(lam.shape[0], groups, TOK_DEV), 0, 1)
    depth = level_matrix(TOK_DEV, local_bits)
    owners = jnp.arange(groups, dtype=jnp.int32)
    bit_rows = [jnp.bitwise_and(jnp.right_shift(owners, b), 1) for b in range(tree_bits)]
    on_bits = jnp.stack(bit_rows, axis=1).astype(jnp.float32)
    partner_rows = [(jnp.right_shift(owners[None, :], b) == jnp.bitwise_xor(jnp.right_shift(owners[:, None], b), 1)) for b in range(tree_bits)]
    picks = jnp.stack(partner_rows, axis=1).astype(jnp.float32)
    select = picks * on_bits[:, :, None]
    lam_cross = lam_blocks[:, local_bits + 1: local_bits + 1 + tree_bits] * on_bits[:, :, None]

    def one_head(items):
        query, key, value, grad = items
        query_blocks = query.reshape(groups, TOK_DEV, width)
        key_blocks = key.reshape(groups, TOK_DEV, width)
        value_blocks = value.reshape(groups, TOK_DEV, width)
        grad_blocks = grad.reshape(groups, TOK_DEV, width)

        def one_block(block):
            block_q, block_k, block_v, block_g, block_lam = block
            mask = level_mask(depth, block_lam, local_bits)
            return local_head(mask, scale, block_q, block_k, block_v, block_g)

        local_q, local_k, local_v = lax.map(one_block, (query_blocks, key_blocks, value_blocks, grad_blocks, lam_blocks))
        query32 = query_blocks.astype(jnp.float32)
        key32 = key_blocks.astype(jnp.float32)
        value32 = value_blocks.astype(jnp.float32)
        grad32 = grad_blocks.astype(jnp.float32)
        state = jnp.einsum("ntx,nty->nxy", key32, value32, precision=highest)
        cross = jnp.einsum("jbi,ixy->jbxy", select, state, precision=highest)
        cross_half = cross.astype(jnp.bfloat16).astype(jnp.float32)
        projected = jnp.einsum("jty,jbxy->jbtx", grad32, cross_half, precision=highest)
        cross_q = scale * jnp.einsum("jbt,jbtx->jtx", lam_cross, projected, precision=highest)
        weighted = (lam_cross[:, :, :, None] * query32[:, None]).astype(jnp.bfloat16).astype(jnp.float32)
        level_grad = scale * jnp.einsum("jbtx,jty->jbxy", weighted, grad32, precision=highest)
        key_state = jnp.einsum("jbi,jbxy->ixy", select, level_grad, precision=highest)
        key_half = key_state.astype(jnp.bfloat16).astype(jnp.float32)
        cross_k = jnp.einsum("ixy,ity->itx", key_half, value32, precision=highest)
        cross_v = jnp.einsum("ixy,itx->ity", key_half, key32, precision=highest)
        dquery = (local_q + cross_q).reshape(tokens, width).astype(jnp.bfloat16)
        dkey = (local_k + cross_k).reshape(tokens, width).astype(jnp.bfloat16)
        dvalue = (local_v + cross_v).reshape(tokens, width).astype(jnp.bfloat16)
        return dquery, dkey, dvalue

    heads_first = (jnp.swapaxes(queries, 0, 1), jnp.swapaxes(keys, 0, 1), jnp.swapaxes(values, 0, 1), jnp.swapaxes(out_grad, 0, 1))
    dquery, dkey, dvalue = lax.map(one_head, heads_first)
    return (jnp.swapaxes(dquery, 0, 1), jnp.swapaxes(dkey, 0, 1), jnp.swapaxes(dvalue, 0, 1))
```

```python
import functools

import jax
import jax.numpy as jnp
from jax import lax
from jax.experimental import pallas as pl
from jax.experimental.pallas import tpu as pltpu
from jax.sharding import PartitionSpec as P

F32 = jnp.float32
BF16 = jnp.bfloat16
MIB = 1 << 20


def bits_of(size):
    return size.bit_length() - 1


def dot(a, b):
    return jnp.dot(a, b, preferred_element_type=F32)


def dot_nt(a, b):
    return lax.dot_general(a, b, (((1,), (1,)), ((), ())), preferred_element_type=F32)


def scaled(row, x):
    return (row * x.astype(F32)).astype(BF16)


def stack_levels(parts, axis):
    return parts[0] if len(parts) == 1 else jnp.concatenate(parts, axis=axis)


def states_kernel(k_ref, v_ref, kh_ref, vh_ref, kt_ref, chunk_ref, total_ref):
    heads = k_ref.shape[1]
    kh_ref[...] = jnp.swapaxes(k_ref[...], 0, 1)
    vh_ref[...] = jnp.swapaxes(v_ref[...], 0, 1)
    first = pl.program_id(0) == 0
    for h in range(heads):
        key_t = kh_ref[h].T
        kt_ref[h] = key_t
        state = dot(key_t, vh_ref[h])
        chunk_ref[h, 0] = state
        total_ref[h] = jnp.where(first, state, total_ref[h] + state)


def grads_kernel(first_row, lam_ref, q_ref, g_ref, qh_ref, gh_ref, qt_ref, gt_ref, grad_ref):
    heads, width = q_ref.shape[1:]
    levels = grad_ref.shape[0]
    qh_ref[...] = jnp.swapaxes(q_ref[...], 0, 1)
    gh_ref[...] = jnp.swapaxes(g_ref[...], 0, 1)
    first = pl.program_id(0) == 0
    rows = [lam_ref[first_row + b : first_row + b + 1, :] for b in range(levels)]
    for h in range(heads):
        query_t = qh_ref[h].T
        qt_ref[h] = query_t
        gt_ref[h] = gh_ref[h].T
        weighted = stack_levels([scaled(row, query_t) for row in rows], 0)
        grad = dot(weighted, gh_ref[h])
        for b in range(levels):
            part = grad[b * width : (b + 1) * width]
            grad_ref[b, h] = jnp.where(first, part, grad_ref[b, h] + part)


def local_kernel(
    tile, lam_ref, k_ref, v_ref, q_ref, g_ref, kt_ref, qt_ref, gt_ref, chunk_ref, after_ref,
    dqt_ref, dk_ref, dv_ref, gin_ref, mask_ref,
):
    del after_ref
    count, width = k_ref.shape[1:]
    chunks = count // tile
    tile_bits = bits_of(tile)
    steps = bits_of(chunks)

    @pl.when(pl.program_id(0) == 0)
    def _():
        source = lax.broadcasted_iota(jnp.int32, (tile, tile), 0)
        target = lax.broadcasted_iota(jnp.int32, (tile, tile), 1)
        differ = jnp.where(source <= target, jnp.bitwise_xor(source, target), -1)
        for c in range(chunks):
            span = slice(c * tile, (c + 1) * tile)
            mask = jnp.zeros((tile, tile), F32)
            mask = jnp.where(differ >= 0, lam_ref[0:1, span], mask)
            for power in range(tile_bits):
                mask = jnp.where(differ >= 1 << power, lam_ref[power + 1 : power + 2, span], mask)
            mask_ref[c] = mask

    gin = [None] * chunks
    for c in range(chunks):
        span = slice(c * tile, (c + 1) * tile)
        key, value, query, grad = k_ref[0, span], v_ref[0, span], q_ref[0, span], g_ref[0, span]
        mask = mask_ref[c]
        weight_q = (mask * dot_nt(value, grad)).astype(BF16)
        weight_v = (mask * dot_nt(key, query)).astype(BF16)
        dk_ref[0, span] = dot(weight_q, query)
        dv_ref[0, span] = dot(weight_v, grad)
        dqt = dot(kt_ref[0, :, span], weight_q)
        states, grads = [], []
        for j in range(steps):
            if c >> j & 1:
                row = lam_ref[tile_bits + 1 + j : tile_bits + 2 + j, span]
                sources = range((c >> j ^ 1) << j, ((c >> j ^ 1) + 1) << j)
                state = functools.reduce(jnp.add, [chunk_ref[0, i] for i in sources])
                states.append(state.astype(BF16))
                grads.append(scaled(row, gt_ref[0, :, span]))
                level = dot(scaled(row, qt_ref[0, :, span]), grad)
                for i in sources:
                    gin[i] = level if gin[i] is None else gin[i] + level
        if states:
            dqt = dqt + dot(stack_levels(states, 1), stack_levels(grads, 0))
        dqt_ref[0, :, span] = dqt
    for c in range(chunks):
        gin_ref[0, c] = jnp.zeros((width, width), F32) if gin[c] is None else gin[c]


def query_kernel(first_row, lam_ref, dqt_ref, gt_ref, cross_ref, out_ref):
    heads = gt_ref.shape[0]
    levels = cross_ref.shape[0]
    rows = [lam_ref[first_row + b : first_row + b + 1, :] for b in range(levels)]
    done = []
    for h in range(heads):
        grad_t = gt_ref[h]
        weighted = stack_levels([scaled(row, grad_t) for row in rows], 0)
        states = stack_levels([cross_ref[b, h].astype(BF16) for b in range(levels)], 1)
        dqt = dqt_ref[h] + dot(states, weighted)
        done.append(dqt.astype(BF16).T)
    out_ref[...] = jnp.swapaxes(jnp.stack(done), 0, 1)


def key_value_kernel(dk_ref, dv_ref, k_ref, v_ref, gin_ref, state_ref, key_out, value_out):
    heads = k_ref.shape[0]
    keys, values = [], []
    for h in range(heads):
        half = (gin_ref[h, 0] + state_ref[h]).astype(BF16)
        keys.append((dk_ref[h] + dot_nt(v_ref[h], half)).astype(BF16))
        values.append((dv_ref[h] + dot(k_ref[h], half)).astype(BF16))
    key_out[...] = jnp.swapaxes(jnp.stack(keys), 0, 1)
    value_out[...] = jnp.swapaxes(jnp.stack(values), 0, 1)


def shape(dims, dtype):
    return jax.ShapeDtypeStruct(dims, dtype)


def params(limit):
    return pltpu.CompilerParams(vmem_limit_bytes=limit * MIB)


def cost(flops, size):
    return pl.CostEstimate(flops=int(flops), bytes_accessed=int(size), transcendentals=0)


def on_device(queries, keys, values, out_grad, level_codes):
    count, heads, width = queries.shape
    scale = width ** (-0.5)
    local_bits = bits_of(count)
    blocks = lax.axis_size("seq")
    tree_bits = bits_of(blocks)
    groups = lax.axis_size("head")
    here = lax.axis_index("seq")
    tile = min(256, count)
    chunks = count // tile
    half = heads // 2
    core = jnp.bitwise_and(here, 1)
    rows = local_bits + 1 + tree_bits

    def permute(x, apart, sends=lambda i: True):
        pairs = [(i, i ^ apart) for i in range(blocks) if sends(i)]
        return lax.ppermute(x, "seq", pairs)

    def half_of(x, which):
        return lax.dynamic_slice_in_dim(x, which * half, half, axis=x.ndim - 3)

    def both_halves(mine, other):
        low = jnp.where(core == 0, mine, other)
        high = jnp.where(core == 0, other, mine)
        return jnp.concatenate([low, high], axis=mine.ndim - 3)

    group = lax.axis_index("head")
    own = level_codes[:rows]
    pieces = [own] + [
        lax.ppermute(own, "head", [(i, (i + r) % groups) for i in range(groups)])
        for r in range(1, groups)
    ]
    pieces = jnp.stack(pieces)
    codes = jnp.concatenate(
        [
            lax.dynamic_index_in_dim(pieces, (group - j) % groups, 0, keepdims=False)
            for j in range(groups)
        ],
        axis=1,
    )
    order = jnp.arange(rows)
    factor = jnp.exp2(-0.5 * jnp.maximum(order.astype(F32) - 1.0, 0.0)) / 16.0
    on_bit = jnp.bitwise_and(jnp.right_shift(here, jnp.maximum(order - local_bits - 1, 0)), 1)
    factor = jnp.where(order > local_bits, factor * on_bit.astype(F32), factor)
    lam = codes.astype(F32) * (scale * factor)[:, None]

    token_block = pl.BlockSpec((tile, heads, width), lambda c: (c, 0, 0))
    head_block = pl.BlockSpec((heads, tile, width), lambda c: (0, c, 0))
    turned_block = pl.BlockSpec((heads, width, tile), lambda c: (0, 0, c))
    chunk_block = pl.BlockSpec((heads, 1, width, width), lambda c: (0, c, 0, 0))
    lam_block = pl.BlockSpec((rows, tile), lambda c: (0, c))
    whole = lambda *dims: pl.BlockSpec(dims, lambda c: (0,) * len(dims))
    natural = shape((heads, count, width), BF16)
    turned = shape((heads, width, count), BF16)
    size = count * heads * width

    kh, vh, kt, chunk_state, state = pl.pallas_call(
        states_kernel,
        grid=(chunks,),
        in_specs=[token_block, token_block],
        out_specs=[head_block, head_block, turned_block, chunk_block, whole(heads, width, width)],
        out_shape=[
            natural, natural, turned,
            shape((heads, chunks, width, width), F32),
            shape((heads, width, width), F32),
        ],
        compiler_params=params(24),
        cost_estimate=cost(2 * size * width, 10 * size),
        name="states",
    )(keys, values)
    found = permute(state, 1)

    qh, gh, qt, gt, level_grad = pl.pallas_call(
        functools.partial(grads_kernel, local_bits + 1),
        grid=(chunks,),
        in_specs=[lam_block, token_block, token_block],
        out_specs=[
            head_block, head_block, turned_block, turned_block,
            whole(tree_bits, heads, width, width),
        ],
        out_shape=[
            natural, natural, turned, turned,
            shape((tree_bits, heads, width, width), F32),
        ],
        compiler_params=params(32),
        cost_estimate=cost(2 * tree_bits * size * width, 12 * size),
        name="level_grads",
    )(lam, queries, out_grad)

    cross = [found]
    pair = half_of(state, core) + half_of(found, core)
    sums = []
    for b in range(1, tree_bits):
        sums.append(
            sum(permute(pair, 1 << b | m, lambda i: not i >> b & 1) for m in range(0, 1 << b, 2))
        )

    key_state = permute(level_grad[0], 1, lambda i: i & 1)
    if tree_bits > 1:
        wide = level_grad[1:]
        wide_pair = half_of(wide, core) + permute(half_of(wide, 1 - core), 1)
        arrived = []
        for b in range(1, tree_bits):
            for m in range(0, 1 << b, 2):
                arrived.append(permute(wide_pair[b - 1], 1 << b | m, lambda i: i >> b & 1))
        after = wide_pair
    else:
        after = level_grad

    head_row = pl.BlockSpec((1, count, width), lambda h: (h, 0, 0))
    head_turned = pl.BlockSpec((1, width, count), lambda h: (h, 0, 0))
    head_chunks = pl.BlockSpec((1, chunks, width, width), lambda h: (h, 0, 0, 0))
    dqt, dk, dv, gin = pl.pallas_call(
        functools.partial(local_kernel, tile),
        grid=(heads,),
        in_specs=[
            pl.BlockSpec((rows, count), lambda h: (0, 0)),
            head_row, head_row, head_row, head_row, head_turned, head_turned, head_turned,
            head_chunks,
            pl.BlockSpec(memory_space=pl.ANY),
        ],
        out_specs=[head_turned, head_row, head_row, head_chunks],
        out_shape=[
            shape((heads, width, count), F32),
            shape((heads, count, width), F32),
            shape((heads, count, width), F32),
            shape((heads, chunks, width, width), F32),
        ],
        scratch_shapes=[pltpu.VMEM((chunks, tile, tile), F32)],
        compiler_params=params(32),
        cost_estimate=cost(14 * size * tile, 26 * size),
        name="local",
    )(lam, kh, vh, qh, gh, kt, qt, gt, chunk_state, after)

    if tree_bits > 1:
        mine = jnp.stack(sums)
        rest = both_halves(mine, permute(mine, 1))
        cross = jnp.concatenate([found[None], rest])
    else:
        cross = found[None]
    query_grad = pl.pallas_call(
        functools.partial(query_kernel, local_bits + 1),
        grid=(chunks,),
        in_specs=[lam_block, turned_block, turned_block, whole(tree_bits, heads, width, width)],
        out_specs=token_block,
        out_shape=shape((count, heads, width), BF16),
        compiler_params=params(32),
        cost_estimate=cost(2 * tree_bits * size * width, 8 * size),
        name="query_grad",
    )(lam, dqt, gt, cross)

    if tree_bits > 1:
        mine = sum(arrived)
        key_state = key_state + both_halves(mine, permute(mine, 1))
    key_grad, value_grad = pl.pallas_call(
        key_value_kernel,
        grid=(chunks,),
        in_specs=[
            head_block, head_block, head_block, head_block, chunk_block,
            whole(heads, width, width),
        ],
        out_specs=[token_block, token_block],
        out_shape=[shape((count, heads, width), BF16)] * 2,
        compiler_params=params(32),
        cost_estimate=cost(4 * size * width, 16 * size),
        name="key_value_grad",
    )(dk, dv, kh, vh, gin, key_state)
    return (query_grad, key_grad, value_grad)


def solution(mesh):
    tokens = P("seq", "head", None)
    return jax.shard_map(
        on_device,
        mesh=mesh,
        in_specs=(tokens, tokens, tokens, tokens, P(None, ("seq", "head"))),
        out_specs=(tokens, tokens, tokens),
        check_vma=False,
    )
```

```python
import functools

import jax
import jax.numpy as jnp
from jax import lax
from jax.experimental import pallas as pl
from jax.experimental.pallas import tpu as pltpu
from jax.sharding import PartitionSpec as P

F32 = jnp.float32
BF16 = jnp.bfloat16
MIB = 1 << 20


def bits_of(size):
    return size.bit_length() - 1


def dot(a, b):
    return jnp.dot(a, b, preferred_element_type=F32)


def scaled(row, x):
    return (row * x.astype(F32)).astype(BF16)


def stack_levels(parts, axis):
    return parts[0] if len(parts) == 1 else jnp.concatenate(parts, axis=axis)


def states_kernel(k_ref, v_ref, kh_ref, vh_ref, kt_ref, chunk_ref, total_ref):
    heads = k_ref.shape[1]
    kh_ref[0] = jnp.swapaxes(k_ref[...], 0, 1)
    vh_ref[0] = jnp.swapaxes(v_ref[...], 0, 1)
    first = pl.program_id(0) == 0
    for h in range(heads):
        key_t = kh_ref[0, h].T
        kt_ref[0, h] = key_t
        state = dot(key_t, vh_ref[0, h])
        chunk_ref[0, h] = state
        total_ref[h] = jnp.where(first, state, total_ref[h] + state)


def grads_kernel(
    first_row, core_ref, lam_ref, q_ref, g_ref, state_ref,
    qh_ref, gh_ref, qt_ref, gt_ref, send_ref, keep_ref, grad_ref,
):
    heads, width = q_ref.shape[1:]
    half = heads // 2
    levels = grad_ref.shape[0]
    qh_ref[0] = jnp.swapaxes(q_ref[...], 0, 1)
    gh_ref[0] = jnp.swapaxes(g_ref[...], 0, 1)
    first = pl.program_id(0) == 0
    rows = [lam_ref[first_row + b : first_row + b + 1, :] for b in range(levels)]
    for h in range(heads):
        query_t = qh_ref[0, h].T
        qt_ref[0, h] = query_t
        gt_ref[0, h] = gh_ref[0, h].T
        weighted = stack_levels([scaled(row, query_t) for row in rows], 0)
        grad = dot(weighted, gh_ref[0, h])
        for b in range(levels):
            part = grad[b * width : (b + 1) * width]
            grad_ref[b, h] = jnp.where(first, part, grad_ref[b, h] + part)

    for core in range(2):

        @pl.when((pl.program_id(0) == pl.num_programs(0) - 1) & (core_ref[0] == core))
        def _():
            for h in range(heads):
                send_ref[h] = state_ref[h] if core == 0 else grad_ref[0, h]
            for level in range(levels):
                for i in range(half):
                    spot = level * half + i
                    source = state_ref if level == 0 else grad_ref.at[level]
                    keep_ref[spot] = source[core * half + i]
                    send_ref[heads + spot] = source[(1 - core) * half + i]


def make_mask(tile, lam_ref, mask_ref):
    source = lax.broadcasted_iota(jnp.int32, (tile, tile), 0)
    target = lax.broadcasted_iota(jnp.int32, (tile, tile), 1)
    differ = jnp.where(source <= target, jnp.bitwise_xor(source, target), -1)
    for c in range(mask_ref.shape[0]):
        span = slice(c * tile, (c + 1) * tile)
        mask = jnp.where(differ >= 0, lam_ref[0:1, span], 0.0)
        for power in range(bits_of(tile)):
            mask = jnp.where(differ >= 1 << power, lam_ref[power + 1 : power + 2, span], mask)
        mask_ref[c] = mask


def local_kernel(
    start, build, lam_ref, k_ref, v_ref, q_ref, g_ref, kt_ref, qt_ref, gt_ref, chunk_ref, mask_in,
    dqt_ref, dk_ref, dv_ref, gin_ref, *mask_out,
):
    chunks, _, tile, width = k_ref.shape
    tile_bits = bits_of(tile)
    steps = bits_of(chunks)
    if build:
        make_mask(tile, lam_ref, mask_out[0])
    mask_ref = mask_out[0] if build else mask_in

    @pl.loop(0, dk_ref.shape[1])
    def _(to):
        h = to + start
        gin = [None] * chunks
        for c in range(chunks):
            span = slice(c * tile, (c + 1) * tile)
            query, grad = q_ref[c, h], g_ref[c, h]
            query_t, grad_t = qt_ref[c, h], gt_ref[c, h]
            mask = mask_ref[c]
            weight_q = (mask * dot(v_ref[c, h], grad_t)).astype(BF16)
            weight_v = (mask * dot(k_ref[c, h], query_t)).astype(BF16)
            dk_ref[c, to] = dot(weight_q, query).astype(BF16)
            dv_ref[c, to] = dot(weight_v, grad).astype(BF16)
            dqt = dot(kt_ref[c, h], weight_q)
            states, grads, queries, where = [], [], [], []
            for j in range(steps):
                if c >> j & 1:
                    row = lam_ref[tile_bits + 1 + j : tile_bits + 2 + j, span]
                    sources = range((c >> j ^ 1) << j, ((c >> j ^ 1) + 1) << j)
                    state = functools.reduce(jnp.add, [chunk_ref[i, h] for i in sources])
                    states.append(state.astype(BF16))
                    grads.append(scaled(row, grad_t))
                    queries.append(scaled(row, query_t))
                    where.append(sources)
            if states:
                dqt = dqt + dot(stack_levels(states, 1), stack_levels(grads, 0))
                level = dot(stack_levels(queries, 0), grad)
                for n, sources in enumerate(where):
                    part = level[n * width : (n + 1) * width]
                    for i in sources:
                        gin[i] = part if gin[i] is None else gin[i] + part
            dqt_ref[c, to] = dqt.astype(BF16)
        for c in range(chunks):
            gin_ref[c, to] = jnp.zeros((width, width), F32) if gin[c] is None else gin[c]


def final_kernel(
    first_row, pieces, lam_ref, k_ref, v_ref, gt_ref, cross_ref, state_ref, *refs
):
    local, (dq_ref, dk_ref, dv_ref, turned_ref) = refs[: 4 * pieces], refs[4 * pieces :]
    heads, width = state_ref.shape[:2]
    levels = cross_ref.shape[0]

    @pl.when(pl.program_id(0) == 0)
    def _():
        for h in range(heads):
            for b in range(levels):
                turned_ref[h, :, b * width : (b + 1) * width] = cross_ref[b, h].astype(BF16)

    rows = [lam_ref[first_row + b : first_row + b + 1, :] for b in range(levels)]
    none = jnp.zeros((width, width), BF16)
    queries, keys, values = [], [], []
    h = 0
    for piece in range(pieces):
        dqt_in, dk_in, dv_in, gin_ref = local[4 * piece : 4 * piece + 4]
        for at in range(dk_in.shape[1]):
            weighted = stack_levels([scaled(row, gt_ref[0, h]) for row in rows], 0)
            dqt = dqt_in[0, at].astype(F32) + dot(turned_ref[h], weighted)
            queries.append(dqt.astype(BF16).T)
            state = (gin_ref[0, at] + state_ref[h]).astype(BF16)
            both = jnp.concatenate([v_ref[0, h], k_ref[0, h]], axis=1)
            right = jnp.concatenate(
                [
                    jnp.concatenate([state.T, none], axis=1),
                    jnp.concatenate([none, state], axis=1),
                ],
                axis=0,
            )
            product = dot(both, right)
            keys.append((dk_in[0, at].astype(F32) + product[:, :width]).astype(BF16))
            values.append((dv_in[0, at].astype(F32) + product[:, width:]).astype(BF16))
            h += 1
    dq_ref[...] = jnp.swapaxes(jnp.stack(queries), 0, 1)
    dk_ref[...] = jnp.swapaxes(jnp.stack(keys), 0, 1)
    dv_ref[...] = jnp.swapaxes(jnp.stack(values), 0, 1)


def shape(dims, dtype):
    return jax.ShapeDtypeStruct(dims, dtype)


def params(limit):
    return pltpu.CompilerParams(vmem_limit_bytes=limit * MIB)


def cost(flops, size):
    return pl.CostEstimate(flops=int(flops), bytes_accessed=int(size), transcendentals=0)


def on_device(queries, keys, values, out_grad, level_codes):
    count, heads, width = queries.shape
    scale = width ** (-0.5)
    local_bits = bits_of(count)
    blocks = lax.axis_size("seq")
    tree_bits = bits_of(blocks)
    groups = lax.axis_size("head")
    here = lax.axis_index("seq")
    tile = min(256, count)
    chunks = count // tile
    half = heads // 2
    core = jnp.bitwise_and(here, 1)
    rows = local_bits + 1 + tree_bits
    is_on = [jnp.bitwise_and(jnp.right_shift(here, b), 1) == 1 for b in range(tree_bits)]

    def permute(x, apart):
        return lax.ppermute(x, "seq", [(i, i ^ apart) for i in range(blocks)])

    def in_order(mine, other, is_high, axis):
        low = jnp.where(is_high, other, mine)
        high = jnp.where(is_high, mine, other)
        return jnp.concatenate([low, high], axis=axis)

    group = lax.axis_index("head")
    codes = level_codes[:rows]
    for b in range(bits_of(groups)):
        other = lax.ppermute(codes, "head", [(i, i ^ 1 << b) for i in range(groups)])
        codes = in_order(codes, other, jnp.bitwise_and(jnp.right_shift(group, b), 1) == 1, 1)
    order = jnp.arange(rows)
    factor = jnp.exp2(-0.5 * jnp.maximum(order.astype(F32) - 1.0, 0.0)) / 16.0
    on_bit = jnp.bitwise_and(jnp.right_shift(here, jnp.maximum(order - local_bits - 1, 0)), 1)
    factor = jnp.where(order > local_bits, factor * on_bit.astype(F32), factor)
    lam = codes.astype(F32) * (scale * factor)[:, None]

    queries, keys, values, out_grad = [
        pltpu.with_memory_space_constraint(x, pltpu.HBM) for x in (queries, keys, values, out_grad)
    ]
    token_block = pl.BlockSpec((tile, heads, width), lambda c: (c, 0, 0))
    lam_block = pl.BlockSpec((rows, tile), lambda c: (0, c))
    on_core = pl.BlockSpec(memory_space=pltpu.VMEM)

    def chunk_block(*dims):
        return pl.BlockSpec((1,) + dims, lambda c: (c,) + (0,) * len(dims))

    def whole(*dims):
        return pl.BlockSpec(dims, lambda c: (0,) * len(dims))

    head_block = chunk_block(heads, tile, width)
    turned_block = chunk_block(heads, width, tile)
    natural = shape((chunks, heads, tile, width), BF16)
    turned = shape((chunks, heads, width, tile), BF16)
    square = (width, width)
    size = count * heads * width

    kh, vh, kt, chunk_state, state = pl.pallas_call(
        states_kernel,
        grid=(chunks,),
        in_specs=[token_block, token_block],
        out_specs=[
            head_block, head_block, turned_block, chunk_block(heads, *square),
            whole(heads, *square),
        ],
        out_shape=[
            natural, natural, turned, shape((chunks, heads, *square), F32),
            shape((heads, *square), F32),
        ],
        compiler_params=params(12),
        cost_estimate=cost(2 * size * width, 10 * size),
        name="states",
    )(keys, values)

    qh, gh, qt, gt, send, keep = pl.pallas_call(
        functools.partial(grads_kernel, local_bits + 1),
        grid=(chunks,),
        in_specs=[
            pl.BlockSpec(memory_space=pltpu.SMEM), lam_block, token_block, token_block,
            whole(heads, *square),
        ],
        out_specs=[
            head_block, head_block, turned_block, turned_block,
            whole(heads + tree_bits * half, *square), whole(tree_bits * half, *square),
        ],
        out_shape=[
            natural, natural, turned, turned,
            shape((heads + tree_bits * half, *square), F32),
            shape((tree_bits * half, *square), F32),
        ],
        scratch_shapes=[pltpu.VMEM((tree_bits, heads, *square), F32)],
        compiler_params=params(14),
        cost_estimate=cost(2 * tree_bits * size * width, 12 * size),
        name="level_grads",
    )(core.astype(jnp.int32)[None], lam, queries, out_grad, state)
    found = permute(send, 1)

    def local(start, stop, mask):
        some = stop - start
        outs = [
            shape((chunks, some, width, tile), BF16),
            shape((chunks, some, tile, width), BF16),
            shape((chunks, some, tile, width), BF16),
            shape((chunks, some, *square), F32),
        ]
        build = start == 0
        operands = [lam, kh, vh, qh, gh, kt, qt, gt, chunk_state]
        if build:
            outs.append(shape((chunks, tile, tile), F32))
            specs = [on_core] * 9 + [pl.BlockSpec(memory_space=pl.ANY)]
            operands.append(lam)
        else:
            specs = [on_core] * 10
            operands.append(mask)
        return pl.pallas_call(
            functools.partial(local_kernel, start, build),
            in_specs=specs,
            out_specs=[on_core] * len(outs),
            out_shape=outs,
            compiler_params=params(14),
            cost_estimate=cost(14 * size * tile * some / heads, 20 * size * some / heads),
            name="local",
        )(*operands)

    early = max(heads // 4, 1)
    *first_part, mask = local(0, early, None)
    pair = keep + found[heads:]
    pair = pair.reshape(tree_bits, half, *square)
    messages = [jnp.where(is_on[b], pair[b], pair[0]) for b in range(1, tree_bits)]
    if messages:
        mask, *messages = lax.optimization_barrier((mask, *messages))
    arrived = []
    for b in range(1, tree_bits):
        arrived.append(
            sum(permute(messages[b - 1], 1 << b | m) for m in range(0, 1 << b, 2))
        )
    second_part = local(early, heads, mask)

    cross = found[None, :heads]
    key_state = jnp.where(is_on[0], 0.0, found[:heads])
    if arrived:
        mine = jnp.stack(arrived)
        rest = in_order(mine, permute(mine, 1), is_on[0], 1)
        cross = jnp.concatenate([cross, rest])
        for b in range(1, tree_bits):
            key_state = key_state + jnp.where(is_on[b], 0.0, rest[b - 1])

    local_parts = [*first_part, *second_part]
    return pl.pallas_call(
        functools.partial(final_kernel, local_bits + 1, 2),
        grid=(chunks,),
        in_specs=[
            lam_block, head_block, head_block, turned_block,
            whole(tree_bits, heads, *square), whole(heads, *square),
        ]
        + [chunk_block(*x.shape[1:]) for x in local_parts],
        out_specs=[token_block] * 3,
        out_shape=[shape((count, heads, width), BF16)] * 3,
        scratch_shapes=[pltpu.VMEM((heads, width, tree_bits * width), BF16)],
        compiler_params=params(16),
        cost_estimate=cost(2 * (tree_bits + 2) * size * width, 16 * size),
        name="final",
    )(lam, kh, vh, gt, cross, key_state, *local_parts)


def solution(mesh):
    tokens = P("seq", "head", None)
    return jax.shard_map(
        on_device,
        mesh=mesh,
        in_specs=(tokens, tokens, tokens, tokens, P(None, ("seq", "head"))),
        out_specs=(tokens, tokens, tokens),
        check_vma=False,
    )
```

```python
import functools

import jax
import jax.numpy as jnp
from jax import lax
from jax.experimental import pallas as pl
from jax.experimental.pallas import tpu as pltpu
from jax.sharding import PartitionSpec as P

F32 = jnp.float32
BF16 = jnp.bfloat16
MIB = 1 << 20


def bits_of(size):
    return size.bit_length() - 1


def dot(a, b):
    return jnp.dot(a, b, preferred_element_type=F32)


def dot_nt(a, b):
    return lax.dot_general(a, b, (((1,), (1,)), ((), ())), preferred_element_type=F32)


def scaled(row, x):
    return (row * x.astype(F32)).astype(BF16)


def stack_levels(parts, axis):
    return parts[0] if len(parts) == 1 else jnp.concatenate(parts, axis=axis)


def level_sources(chunks):
    found = []
    for j in range(bits_of(chunks)):
        for first in range(0, chunks, 2 << j):
            found.append(range(first, first + (1 << j)))
    return found


def states_kernel(k_ref, v_ref, kh_ref, vh_ref, level_ref, total_ref, chunk_ref):
    heads = k_ref.shape[1]
    chunks = chunk_ref.shape[0]
    step = pl.program_id(0)
    kh_ref[0] = jnp.swapaxes(k_ref[...], 0, 1)
    vh_ref[0] = jnp.swapaxes(v_ref[...], 0, 1)
    for h in range(heads):
        chunk_ref[step, h] = dot(kh_ref[0, h].T, vh_ref[0, h])

    @pl.when(step == chunks - 1)
    def _():
        for h in range(heads):
            tiles = [chunk_ref[i, h] for i in range(chunks)]
            total_ref[h] = functools.reduce(jnp.add, tiles)
            for n, sources in enumerate(level_sources(chunks)):
                state = functools.reduce(jnp.add, [tiles[i] for i in sources])
                level_ref[n, h] = state.astype(BF16)


def grads_kernel(
    first_row, core_ref, lam_ref, q_ref, g_ref, state_ref,
    qh_ref, gh_ref, send_ref, keep_ref, grad_ref,
):
    heads, width = q_ref.shape[1:]
    half = heads // 2
    levels = grad_ref.shape[0]
    qh_ref[0] = jnp.swapaxes(q_ref[...], 0, 1)
    gh_ref[0] = jnp.swapaxes(g_ref[...], 0, 1)
    first = pl.program_id(0) == 0
    rows = [lam_ref[first_row + b : first_row + b + 1, :] for b in range(levels)]
    for h in range(heads):
        query_t = qh_ref[0, h].T
        weighted = stack_levels([scaled(row, query_t) for row in rows], 0)
        grad = dot(weighted, gh_ref[0, h])
        for b in range(levels):
            part = grad[b * width : (b + 1) * width]
            grad_ref[b, h] = jnp.where(first, part, grad_ref[b, h] + part)

    for core in range(2):

        @pl.when((pl.program_id(0) == pl.num_programs(0) - 1) & (core_ref[0] == core))
        def _():
            for h in range(heads):
                send_ref[h] = state_ref[h] if core == 0 else grad_ref[0, h]
            for level in range(levels):
                for i in range(half):
                    spot = level * half + i
                    source = state_ref if level == 0 else grad_ref.at[level]
                    keep_ref[spot] = source[core * half + i]
                    send_ref[heads + spot] = source[(1 - core) * half + i]


def make_mask(tile, lam_ref, mask_ref):
    source = lax.broadcasted_iota(jnp.int32, (tile, tile), 0)
    target = lax.broadcasted_iota(jnp.int32, (tile, tile), 1)
    differ = jnp.where(source <= target, jnp.bitwise_xor(source, target), -1)
    for c in range(mask_ref.shape[0]):
        span = slice(c * tile, (c + 1) * tile)
        mask = jnp.where(differ >= 0, lam_ref[0:1, span], 0.0)
        for power in range(bits_of(tile)):
            mask = jnp.where(differ >= 1 << power, lam_ref[power + 1 : power + 2, span], mask)
        mask_ref[c] = mask


def local_kernel(
    build, lam_ref, k_ref, v_ref, q_ref, g_ref, level_ref, mask_in,
    dq_ref, dk_ref, dv_ref, gin_ref, *mask_out,
):
    chunks, _, tile, width = k_ref.shape
    tile_bits = bits_of(tile)
    if build:
        pl.when(pl.program_id(0) == 0)(lambda: make_mask(tile, lam_ref, mask_out[0]))
    mask_ref = mask_out[0] if build else mask_in

    groups = level_sources(chunks)
    gin = [None] * chunks
    for c in range(chunks):
        span = slice(c * tile, (c + 1) * tile)
        key, value, query, grad = k_ref[c, 0], v_ref[c, 0], q_ref[c, 0], g_ref[c, 0]
        mask = mask_ref[c]
        weight_q = (mask * dot_nt(value, grad)).astype(BF16)
        weight_v = (mask * dot_nt(key, query)).astype(BF16)
        dk_ref[c, 0] = dot(weight_q, query).astype(BF16)
        dv_ref[c, 0] = dot(weight_v, grad).astype(BF16)
        dqt = dot(key.T, weight_q)
        query_t = query.T if c else None
        for j in range(bits_of(chunks)):
            if c >> j & 1:
                row = lam_ref[tile_bits + 1 + j : tile_bits + 2 + j, span]
                first = (c >> j ^ 1) << j
                sources = range(first, first + (1 << j))
                dqt = dqt + row * dot_nt(level_ref[groups.index(sources), 0], grad)
                part = dot(scaled(row, query_t), grad)
                for i in sources:
                    gin[i] = part if gin[i] is None else gin[i] + part
        dq_ref[c, 0] = dqt.astype(BF16).T
    for c in range(chunks):
        gin_ref[c, 0] = jnp.zeros((width, width), F32) if gin[c] is None else gin[c]


def final_kernel(first_row, pieces, lam_ref, k_ref, v_ref, g_ref, cross_ref, state_ref, *refs):
    local, (dq_ref, dk_ref, dv_ref, half_ref, lam_wide_ref) = refs[: 4 * pieces], refs[4 * pieces :]
    heads, width = state_ref.shape[:2]
    levels = cross_ref.shape[0]
    tile = lam_ref.shape[1]

    @pl.when(pl.program_id(0) == 0)
    def _():
        for h in range(heads):
            for b in range(levels):
                half_ref[h, b * width : (b + 1) * width] = cross_ref[b, h].astype(BF16)

    for b in range(levels):
        row = lam_ref[first_row + b : first_row + b + 1, :]
        lam_wide_ref[b] = jnp.broadcast_to(row, (width, tile)).T
    none = jnp.zeros((width, width), BF16)
    queries, keys, values = [], [], []
    h = 0
    for piece in range(pieces):
        dq_in, dk_in, dv_in, gin_ref = local[4 * piece : 4 * piece + 4]
        for at in range(dk_in.shape[1]):
            dq = dq_in[0, at].astype(F32)
            projected = dot_nt(g_ref[0, h], half_ref[h])
            for b in range(levels):
                dq = dq + lam_wide_ref[b] * projected[:, b * width : (b + 1) * width]
            queries.append(dq.astype(BF16))
            state = (gin_ref[0, at] + state_ref[h]).astype(BF16)
            both = jnp.concatenate([v_ref[0, h], k_ref[0, h]], axis=1)
            right = jnp.concatenate(
                [
                    jnp.concatenate([state.T, none], axis=1),
                    jnp.concatenate([none, state], axis=1),
                ],
                axis=0,
            )
            product = dot(both, right)
            keys.append((dk_in[0, at].astype(F32) + product[:, :width]).astype(BF16))
            values.append((dv_in[0, at].astype(F32) + product[:, width:]).astype(BF16))
            h += 1
    dq_ref[...] = jnp.swapaxes(jnp.stack(queries), 0, 1)
    dk_ref[...] = jnp.swapaxes(jnp.stack(keys), 0, 1)
    dv_ref[...] = jnp.swapaxes(jnp.stack(values), 0, 1)


def shape(dims, dtype):
    return jax.ShapeDtypeStruct(dims, dtype)


def params(limit):
    return pltpu.CompilerParams(vmem_limit_bytes=limit * MIB)


def cost(flops, size):
    return pl.CostEstimate(flops=int(flops), bytes_accessed=int(size), transcendentals=0)


def on_device(queries, keys, values, out_grad, level_codes):
    count, heads, width = queries.shape
    scale = width ** (-0.5)
    local_bits = bits_of(count)
    blocks = lax.axis_size("seq")
    tree_bits = bits_of(blocks)
    groups = lax.axis_size("head")
    here = lax.axis_index("seq")
    tile = min(256, count)
    chunks = count // tile
    half = heads // 2
    core = jnp.bitwise_and(here, 1)
    rows = local_bits + 1 + tree_bits
    is_on = [jnp.bitwise_and(jnp.right_shift(here, b), 1) == 1 for b in range(tree_bits)]

    def permute(x, apart):
        return lax.ppermute(x, "seq", [(i, i ^ apart) for i in range(blocks)])

    def in_order(mine, other, is_high, axis):
        low = jnp.where(is_high, other, mine)
        high = jnp.where(is_high, mine, other)
        return jnp.concatenate([low, high], axis=axis)

    def in_hbm(*arrays):
        return [pltpu.with_memory_space_constraint(x, pltpu.HBM) for x in arrays]

    token_block = pl.BlockSpec((tile, heads, width), lambda c: (c, 0, 0))
    lam_block = pl.BlockSpec((rows, tile), lambda c: (0, c))

    def chunk_block(*dims):
        return pl.BlockSpec((1,) + dims, lambda c: (c,) + (0,) * len(dims))

    def whole(*dims):
        return pl.BlockSpec(dims, lambda c: (0,) * len(dims))

    head_block = chunk_block(heads, tile, width)
    natural = pltpu.HBM((chunks, heads, tile, width), BF16)
    square = (width, width)
    size = count * heads * width
    groups_in = len(level_sources(chunks))
    queries, keys, values, out_grad = in_hbm(queries, keys, values, out_grad)

    kh, vh, level_state, state = pl.pallas_call(
        states_kernel,
        grid=(chunks,),
        in_specs=[token_block, token_block],
        out_specs=[
            head_block, head_block, whole(groups_in, heads, *square), whole(heads, *square),
        ],
        out_shape=[
            natural, natural, shape((groups_in, heads, *square), BF16),
            shape((heads, *square), F32),
        ],
        scratch_shapes=[pltpu.VMEM((chunks, heads, *square), F32)],
        compiler_params=params(12),
        cost_estimate=cost(2 * size * width, 8 * size),
        name="states",
    )(keys, values)

    group = lax.axis_index("head")
    codes = level_codes[:rows]
    for b in range(bits_of(groups)):
        other = lax.ppermute(codes, "head", [(i, i ^ 1 << b) for i in range(groups)])
        if b == 0:
            other, state = lax.optimization_barrier((other, state))
        codes = in_order(codes, other, jnp.bitwise_and(jnp.right_shift(group, b), 1) == 1, 1)
    order = jnp.arange(rows)
    factor = jnp.exp2(-0.5 * jnp.maximum(order.astype(F32) - 1.0, 0.0)) / 16.0
    on_bit = jnp.bitwise_and(jnp.right_shift(here, jnp.maximum(order - local_bits - 1, 0)), 1)
    factor = jnp.where(order > local_bits, factor * on_bit.astype(F32), factor)
    lam = codes.astype(F32) * (scale * factor)[:, None]

    qh, gh, send, keep = pl.pallas_call(
        functools.partial(grads_kernel, local_bits + 1),
        grid=(chunks,),
        in_specs=[
            pl.BlockSpec(memory_space=pltpu.SMEM), lam_block, token_block, token_block,
            whole(heads, *square),
        ],
        out_specs=[
            head_block, head_block,
            whole(heads + tree_bits * half, *square), whole(tree_bits * half, *square),
        ],
        out_shape=[
            natural, natural,
            shape((heads + tree_bits * half, *square), F32),
            shape((tree_bits * half, *square), F32),
        ],
        scratch_shapes=[pltpu.VMEM((tree_bits, heads, *square), F32)],
        compiler_params=params(14),
        cost_estimate=cost(2 * tree_bits * size * width, 8 * size),
        name="level_grads",
    )(core.astype(jnp.int32)[None], lam, queries, out_grad, state)
    found = permute(send, 1)
    kh, vh, qh, gh = in_hbm(kh, vh, qh, gh)

    def local(start, stop, mask):
        some = stop - start
        build = start == 0

        def head_in(n, *dims):
            return pl.BlockSpec((n, 1) + dims, lambda h: (0, h + start, 0, 0))

        def head_out(*dims):
            return pl.BlockSpec((chunks, 1) + dims, lambda h: (0, h, 0, 0))

        place = pltpu.HBM if build else shape
        outs = [place((chunks, some, tile, width), BF16)] * 3
        outs.append(place((chunks, some, *square), F32))
        out_specs = [head_out(tile, width)] * 3 + [head_out(*square)]
        mask_spec = whole(chunks, tile, tile)
        if build:
            outs.append(shape((chunks, tile, tile), F32))
            out_specs.append(mask_spec)
            mask_spec = pl.BlockSpec(memory_space=pl.ANY)
            mask = lam
        return pl.pallas_call(
            functools.partial(local_kernel, build),
            grid=(some,),
            in_specs=[
                whole(rows, count), *[head_in(chunks, tile, width)] * 4,
                head_in(groups_in, *square), mask_spec,
            ],
            out_specs=out_specs,
            out_shape=outs,
            compiler_params=params(14),
            cost_estimate=cost(14 * size * tile * some / heads, 16 * size * some / heads),
            name="local",
        )(lam, kh, vh, qh, gh, level_state, mask)

    early = max(heads // 4, 1)
    *first_part, mask = local(0, early, None)
    first_part = in_hbm(*first_part)
    pair = keep + found[heads:]
    pair = pair.reshape(tree_bits, half, *square)
    messages = [jnp.where(is_on[b], pair[b], pair[0]) for b in range(1, tree_bits)]
    if messages:
        mask, *messages = lax.optimization_barrier((mask, *messages))
    received = [
        [permute(messages[b - 1], 1 << b | m) for m in range(0, 1 << b, 2)]
        for b in range(1, tree_bits)
    ]
    second_part = local(early, heads, mask)
    received, second_part = lax.optimization_barrier((received, second_part))
    arrived = [functools.reduce(jnp.add, parts) for parts in received]

    cross = found[None, :heads]
    key_state = jnp.where(is_on[0], 0.0, found[:heads])
    if arrived:
        mine = jnp.stack(arrived)
        rest = in_order(mine, permute(mine, 1), is_on[0], 1)
        cross = jnp.concatenate([cross, rest])
        for b in range(1, tree_bits):
            key_state = key_state + jnp.where(is_on[b], 0.0, rest[b - 1])

    local_parts = [*first_part, *second_part]
    return pl.pallas_call(
        functools.partial(final_kernel, local_bits + 1, 2),
        grid=(chunks,),
        in_specs=[
            lam_block, head_block, head_block, head_block,
            whole(tree_bits, heads, *square), whole(heads, *square),
        ]
        + [chunk_block(*x.shape[1:]) for x in local_parts],
        out_specs=[token_block] * 3,
        out_shape=[shape((count, heads, width), BF16)] * 3,
        scratch_shapes=[
            pltpu.VMEM((heads, tree_bits * width, width), BF16),
            pltpu.VMEM((tree_bits, tile, width), F32),
        ],
        compiler_params=params(20),
        cost_estimate=cost(2 * (tree_bits + 2) * size * width, 16 * size),
        name="final",
    )(lam, kh, vh, gh, cross, key_state, *local_parts)


def solution(mesh):
    tokens = P("seq", "head", None)
    return jax.shard_map(
        on_device,
        mesh=mesh,
        in_specs=(tokens, tokens, tokens, tokens, P(None, ("seq", "head"))),
        out_specs=(tokens, tokens, tokens),
        check_vma=False,
    )
```

```python
import functools

import jax
import jax.numpy as jnp
from jax import lax
from jax.experimental import pallas as pl
from jax.experimental.pallas import tpu as pltpu
from jax.sharding import PartitionSpec as P

F32 = jnp.float32
BF16 = jnp.bfloat16
MIB = 1 << 20


def bits_of(size):
    return size.bit_length() - 1


def dot(a, b):
    return jnp.dot(a, b, preferred_element_type=F32)


def dot_nt(a, b):
    return lax.dot_general(a, b, (((1,), (1,)), ((), ())), preferred_element_type=F32)


def scaled(row, x):
    return (row * x.astype(F32)).astype(BF16)


def stack_levels(parts, axis):
    return parts[0] if len(parts) == 1 else jnp.concatenate(parts, axis=axis)


def level_sources(chunks):
    found = []
    for j in range(bits_of(chunks)):
        for first in range(0, chunks, 2 << j):
            found.append(range(first, first + (1 << j)))
    return found


def states_kernel(k_ref, v_ref, kh_ref, vh_ref, level_ref, total_ref, chunk_ref):
    heads = k_ref.shape[1]
    chunks = chunk_ref.shape[0]
    step = pl.program_id(0)
    kh_ref[0] = jnp.swapaxes(k_ref[...], 0, 1)
    vh_ref[0] = jnp.swapaxes(v_ref[...], 0, 1)
    for h in range(heads):
        chunk_ref[step, h] = dot(kh_ref[0, h].T, vh_ref[0, h])

    @pl.when(step == chunks - 1)
    def _():
        for h in range(heads):
            tiles = [chunk_ref[i, h] for i in range(chunks)]
            total_ref[h] = functools.reduce(jnp.add, tiles)
            for n, sources in enumerate(level_sources(chunks)):
                state = functools.reduce(jnp.add, [tiles[i] for i in sources])
                level_ref[n, h] = state.astype(BF16)


def grads_kernel(
    first_row, core_ref, lam_ref, q_ref, g_ref, state_ref,
    qh_ref, gh_ref, send_ref, keep_ref, grad_ref,
):
    heads, width = q_ref.shape[1:]
    half = heads // 2
    levels = grad_ref.shape[0]
    qh_ref[0] = jnp.swapaxes(q_ref[...], 0, 1)
    gh_ref[0] = jnp.swapaxes(g_ref[...], 0, 1)
    first = pl.program_id(0) == 0
    rows = [lam_ref[first_row + b : first_row + b + 1, :] for b in range(levels)]
    for h in range(heads):
        query_t = qh_ref[0, h].T
        weighted = stack_levels([scaled(row, query_t) for row in rows], 0)
        grad = dot(weighted, gh_ref[0, h])
        for b in range(levels):
            part = grad[b * width : (b + 1) * width]
            grad_ref[b, h] = jnp.where(first, part, grad_ref[b, h] + part)

    for core in range(2):

        @pl.when((pl.program_id(0) == pl.num_programs(0) - 1) & (core_ref[0] == core))
        def _():
            for h in range(heads):
                send_ref[h] = state_ref[h] if core == 0 else grad_ref[0, h]
            for level in range(levels):
                for i in range(half):
                    spot = level * half + i
                    source = state_ref if level == 0 else grad_ref.at[level]
                    keep_ref[spot] = source[core * half + i]
                    send_ref[heads + spot] = source[(1 - core) * half + i]


def make_mask(lam_ref, span, mask_ref):
    tile = mask_ref.shape[0]
    part = min(128, tile)
    source = lax.broadcasted_iota(jnp.int32, (part, part), 0)
    target = lax.broadcasted_iota(jnp.int32, (part, part), 1)
    differ = jnp.where(source <= target, jnp.bitwise_xor(source, target), -1)
    for to in range(0, tile, part):
        lanes = slice(span.start + to, span.start + to + part)
        mask = jnp.where(differ >= 0, lam_ref[0:1, lanes], 0.0)
        for power in range(bits_of(part)):
            mask = jnp.where(differ >= 1 << power, lam_ref[power + 1 : power + 2, lanes], mask)
        mask_ref[to : to + part, to : to + part] = mask
        for at in range(0, tile, part):
            if at < to:
                level = bits_of(at ^ to) + 1
                row = lam_ref[level : level + 1, lanes]
                mask_ref[at : at + part, to : to + part] = jnp.broadcast_to(row, (part, part))
            elif at > to:
                mask_ref[at : at + part, to : to + part] = jnp.zeros((part, part), F32)


def local_kernel(only, lam_ref, k_ref, v_ref, q_ref, g_ref, level_ref, *refs):
    dq_ref, dk_ref, dv_ref, gin_ref, mask_ref = refs[-5:]
    chunks, heads, tile, width = k_ref.shape
    tile_bits = bits_of(tile)
    groups = level_sources(chunks)
    if 0 in only:
        gin_ref[...] = jnp.zeros(gin_ref.shape, F32)
    for c in only:
        span = slice(c * tile, (c + 1) * tile)
        make_mask(lam_ref, span, mask_ref)

        @pl.loop(0, heads, unroll=4)
        def _(h):
            key, value, query, grad = k_ref[c, h], v_ref[c, h], q_ref[c, h], g_ref[c, h]
            mask = mask_ref[...]
            weight_q = (mask * dot_nt(value, grad)).astype(BF16)
            weight_v = (mask * dot_nt(key, query)).astype(BF16)
            dk_ref[c, h] = dot(weight_q, query).astype(BF16)
            dv_ref[c, h] = dot(weight_v, grad).astype(BF16)
            dqt = dot(key.T, weight_q)
            query_t = query.T if c else None
            for j in range(bits_of(chunks)):
                if c >> j & 1:
                    row = lam_ref[tile_bits + 1 + j : tile_bits + 2 + j, span]
                    first = (c >> j ^ 1) << j
                    sources = range(first, first + (1 << j))
                    dqt = dqt + row * dot_nt(level_ref[groups.index(sources), h], grad)
                    part = dot(scaled(row, query_t), grad)
                    for i in sources:
                        gin_ref[i, h] = gin_ref[i, h] + part
            dq_ref[c, h] = dqt.astype(BF16).T


def pair_kernel(flag_ref, keep_ref, found_ref, *out_refs):
    half = out_refs[0].shape[0]
    heads = found_ref.shape[0] - keep_ref.shape[0]

    def pair(level, i):
        return keep_ref[level * half + i] + found_ref[heads + level * half + i]

    for n, out_ref in enumerate(out_refs):
        for on in range(2):

            @pl.when(flag_ref[n + 1] == on)
            def _():
                for i in range(half):
                    out_ref[i] = pair((n + 1) * on, i)


def sum_kernel(counts, *refs):
    out_ref = refs[-1]
    at = 0
    for n, count in enumerate(counts):
        for i in range(out_ref.shape[1]):
            out_ref[n, i] = functools.reduce(jnp.add, [r[i] for r in refs[at : at + count]])
        at += count


def final_kernel(
    first_row, flag_ref, lam_ref, k_ref, v_ref, g_ref, dq_in, dk_in, dv_in, gin_ref, found_ref,
    *refs,
):
    sums, (dq_ref, dk_ref, dv_ref, half_ref, state_ref, lam_wide_ref) = refs[:-6], refs[-6:]
    heads, width = state_ref.shape[:2]
    half = heads // 2
    levels = lam_wide_ref.shape[0]
    tile = lam_ref.shape[1]

    for core in range(2):

        @pl.when((pl.program_id(0) == 0) & (flag_ref[0] == core))
        def _():
            off = [(1 - flag_ref[b]).astype(F32) for b in range(levels)]
            for h in range(heads):
                first = found_ref[h]
                half_ref[h, :width] = first.astype(BF16)
                state = off[0] * first
                for b in range(1, levels):
                    part = sums[0 if h // half == core else 1][b - 1, h % half]
                    half_ref[h, b * width : (b + 1) * width] = part.astype(BF16)
                    state = state + off[b] * part
                state_ref[h] = state

    for b in range(levels):
        row = lam_ref[first_row + b : first_row + b + 1, :]
        lam_wide_ref[b] = jnp.broadcast_to(row, (width, tile)).T
    none = jnp.zeros((width, width), BF16)
    queries, keys, values = [], [], []
    for h in range(heads):
        dq = dq_in[0, h].astype(F32)
        projected = dot_nt(g_ref[0, h], half_ref[h])
        for b in range(levels):
            dq = dq + lam_wide_ref[b] * projected[:, b * width : (b + 1) * width]
        queries.append(dq.astype(BF16))
        state = (gin_ref[0, h] + state_ref[h]).astype(BF16)
        both = jnp.concatenate([v_ref[0, h], k_ref[0, h]], axis=1)
        right = jnp.concatenate(
            [
                jnp.concatenate([state.T, none], axis=1),
                jnp.concatenate([none, state], axis=1),
            ],
            axis=0,
        )
        product = dot(both, right)
        keys.append((dk_in[0, h].astype(F32) + product[:, :width]).astype(BF16))
        values.append((dv_in[0, h].astype(F32) + product[:, width:]).astype(BF16))
    dq_ref[...] = jnp.swapaxes(jnp.stack(queries), 0, 1)
    dk_ref[...] = jnp.swapaxes(jnp.stack(keys), 0, 1)
    dv_ref[...] = jnp.swapaxes(jnp.stack(values), 0, 1)


def shape(dims, dtype):
    return jax.ShapeDtypeStruct(dims, dtype)


def params(limit):
    return pltpu.CompilerParams(vmem_limit_bytes=limit * MIB)


def cost(flops, size):
    return pl.CostEstimate(flops=int(flops), bytes_accessed=int(size), transcendentals=0)


def on_device(queries, keys, values, out_grad, level_codes):
    count, heads, width = queries.shape
    scale = width ** (-0.5)
    local_bits = bits_of(count)
    blocks = lax.axis_size("seq")
    tree_bits = bits_of(blocks)
    groups = lax.axis_size("head")
    here = lax.axis_index("seq")
    tile = min(256, count)
    chunks = count // tile
    half = heads // 2
    rows = local_bits + 1 + tree_bits
    flags = jnp.bitwise_and(jnp.right_shift(here, jnp.arange(max(tree_bits, 1))), 1)

    def permute(x, apart):
        return lax.ppermute(x, "seq", [(i, i ^ apart) for i in range(blocks)])

    def in_hbm(*arrays):
        return [pltpu.with_memory_space_constraint(x, pltpu.HBM) for x in arrays]

    def near(*arrays):
        return [pltpu.with_memory_space_constraint(x, pltpu.VMEM) for x in arrays]

    token_block = pl.BlockSpec((tile, heads, width), lambda c: (c, 0, 0))
    lam_block = pl.BlockSpec((rows, tile), lambda c: (0, c))
    in_smem = pl.BlockSpec(memory_space=pltpu.SMEM)
    in_vmem = pl.BlockSpec(memory_space=pltpu.VMEM)
    anywhere = pl.BlockSpec(memory_space=pl.ANY)

    def chunk_block(*dims):
        return pl.BlockSpec((1,) + dims, lambda c: (c,) + (0,) * len(dims))

    def whole(*dims):
        return pl.BlockSpec(dims, lambda c: (0,) * len(dims))

    head_block = chunk_block(heads, tile, width)
    natural = pltpu.VMEM((chunks, heads, tile, width), BF16)
    square = (width, width)
    size = count * heads * width
    groups_in = len(level_sources(chunks))
    queries, keys, values, out_grad = in_hbm(queries, keys, values, out_grad)

    kh, vh, level_state, state = pl.pallas_call(
        states_kernel,
        grid=(chunks,),
        in_specs=[token_block, token_block],
        out_specs=[
            head_block, head_block, whole(groups_in, heads, *square), whole(heads, *square),
        ],
        out_shape=[
            natural, natural, pltpu.VMEM((groups_in, heads, *square), BF16),
            pltpu.VMEM((heads, *square), F32),
        ],
        scratch_shapes=[pltpu.VMEM((chunks, heads, *square), F32)],
        compiler_params=params(10),
        cost_estimate=cost(2 * size * width, 8 * size),
        name="states",
    )(keys, values)

    group = lax.axis_index("head")
    pieces = [
        lax.ppermute(level_codes, "head", [(i, (i + r) % groups) for i in range(groups)])
        for r in range(1, groups)
    ]
    pieces, state = lax.optimization_barrier((pieces, state))
    pieces = jnp.stack([level_codes, *pieces])
    codes = jnp.concatenate(
        [
            lax.dynamic_index_in_dim(pieces, (group - j) % groups, 0, keepdims=False)[:rows]
            for j in range(groups)
        ],
        axis=1,
    )
    order = jnp.arange(rows)
    factor = jnp.exp2(-0.5 * jnp.maximum(order.astype(F32) - 1.0, 0.0)) / 16.0
    on_bit = jnp.bitwise_and(jnp.right_shift(here, jnp.maximum(order - local_bits - 1, 0)), 1)
    factor = jnp.where(order > local_bits, factor * on_bit.astype(F32), factor)
    lam = codes.astype(F32) * (scale * factor)[:, None]

    qh, gh, send, keep = pl.pallas_call(
        functools.partial(grads_kernel, local_bits + 1),
        grid=(chunks,),
        in_specs=[in_smem, lam_block, token_block, token_block, whole(heads, *square)],
        out_specs=[
            head_block, head_block,
            whole(heads + tree_bits * half, *square), whole(tree_bits * half, *square),
        ],
        out_shape=[
            natural, natural,
            pltpu.VMEM((heads + tree_bits * half, *square), F32),
            pltpu.VMEM((tree_bits * half, *square), F32),
        ],
        scratch_shapes=[pltpu.VMEM((tree_bits, heads, *square), F32)],
        compiler_params=params(10),
        cost_estimate=cost(2 * tree_bits * size * width, 8 * size),
        name="level_grads",
    )(flags, lam, queries, out_grad, *near(state))
    found = permute(send, 1)
    kh, vh, qh, gh, level_state, keep = near(kh, vh, qh, gh, level_state, keep)

    def local(only, before):
        inputs = [lam, kh, vh, qh, gh, level_state]
        return pl.pallas_call(
            functools.partial(local_kernel, only),
            in_specs=[in_vmem] * len(inputs) + [anywhere] * len(before),
            out_specs=[in_vmem] * 4,
            out_shape=[natural] * 3 + [pltpu.VMEM((chunks, heads, *square), F32)],
            input_output_aliases={len(inputs) + i: i for i in range(len(before))},
            scratch_shapes=[pltpu.VMEM((tile, tile), F32)],
            compiler_params=params(6),
            cost_estimate=cost(14 * size * tile * len(only) / chunks, 4 * size),
            name="local",
        )(*inputs, *before)

    parts = local([0], [])
    mine = []
    if tree_bits > 1:
        messages = pl.pallas_call(
            pair_kernel,
            in_specs=[in_smem, in_vmem, in_vmem],
            out_specs=[in_vmem] * (tree_bits - 1),
            out_shape=[pltpu.VMEM((half, *square), F32)] * (tree_bits - 1),
            compiler_params=params(4),
            cost_estimate=cost(size, size),
            name="pair",
        )(flags, keep, found)
        *messages, parts = lax.optimization_barrier((*messages, parts))
        received = [
            [permute(messages[b - 1], 1 << b | m) for m in range(0, 1 << b, 2)]
            for b in range(1, tree_bits)
        ]
    if chunks > 1:
        parts = local(list(range(1, chunks)), near(*parts))
    if tree_bits > 1:
        received, parts = lax.optimization_barrier((received, parts))
        flat = [x for some in received for x in some]
        mine = pl.pallas_call(
            functools.partial(sum_kernel, [len(some) for some in received]),
            in_specs=[in_vmem] * len(flat),
            out_specs=in_vmem,
            out_shape=pltpu.VMEM((tree_bits - 1, half, *square), F32),
            compiler_params=params(6),
            cost_estimate=cost(size, size),
            name="sums",
        )(*flat)
        mine = [mine, permute(mine, 1)]

    return pl.pallas_call(
        functools.partial(final_kernel, local_bits + 1),
        grid=(chunks,),
        in_specs=[in_smem, lam_block, *[head_block] * 6, chunk_block(heads, *square)]
        + [whole(*found.shape)]
        + [whole(*x.shape) for x in mine],
        out_specs=[token_block] * 3,
        out_shape=[shape((count, heads, width), BF16)] * 3,
        scratch_shapes=[
            pltpu.VMEM((heads, tree_bits * width, width), BF16),
            pltpu.VMEM((heads, *square), F32),
            pltpu.VMEM((tree_bits, tile, width), F32),
        ],
        compiler_params=params(14),
        cost_estimate=cost(2 * (tree_bits + 2) * size * width, 16 * size),
        name="final",
    )(flags, lam, kh, vh, gh, *near(*parts), found, *mine)


def solution(mesh):
    tokens = P("seq", "head", None)
    return jax.shard_map(
        on_device,
        mesh=mesh,
        in_specs=(tokens, tokens, tokens, tokens, P(None, ("seq", "head"))),
        out_specs=(tokens, tokens, tokens),
        check_vma=False,
    )
```

```python
import functools

import jax
import jax.numpy as jnp
from jax import lax
from jax.experimental import pallas as pl
from jax.experimental.pallas import tpu as pltpu
from jax.sharding import PartitionSpec as P

F32 = jnp.float32
BF16 = jnp.bfloat16
MIB = 1 << 20


def bits_of(size):
    return size.bit_length() - 1


def dot(a, b):
    return jnp.dot(a, b, preferred_element_type=F32)


def dot_nt(a, b):
    return lax.dot_general(a, b, (((1,), (1,)), ((), ())), preferred_element_type=F32)


def scaled(row, x):
    return (row * x.astype(F32)).astype(BF16)


def stack_levels(parts, axis):
    return parts[0] if len(parts) == 1 else jnp.concatenate(parts, axis=axis)


def level_sources(chunks):
    found = []
    for j in range(bits_of(chunks)):
        for first in range(0, chunks, 2 << j):
            found.append(range(first, first + (1 << j)))
    return found


def states_kernel(
    k_ref, v_ref, q_far, g_far, kh_ref, vh_ref, level_ref, total_ref, q_near, g_near,
    chunk_ref, sems,
):
    heads = k_ref.shape[1]
    chunks = chunk_ref.shape[0]
    step = pl.program_id(0)

    def fetches(i):
        return [
            pltpu.make_async_copy(q_far.at[i], q_near.at[i], sems.at[0, i]),
            pltpu.make_async_copy(g_far.at[i], g_near.at[i], sems.at[1, i]),
        ]

    for fetch in fetches(step):
        fetch.start()
    kh_ref[0] = jnp.swapaxes(k_ref[...], 0, 1)
    vh_ref[0] = jnp.swapaxes(v_ref[...], 0, 1)
    for h in range(heads):
        chunk_ref[step, h] = dot(kh_ref[0, h].T, vh_ref[0, h])

    @pl.when(step == chunks - 1)
    def _():
        for h in range(heads):
            tiles = [chunk_ref[i, h] for i in range(chunks)]
            total_ref[h] = functools.reduce(jnp.add, tiles)
            for n, sources in enumerate(level_sources(chunks)):
                state = functools.reduce(jnp.add, [tiles[i] for i in sources])
                level_ref[n, h] = state.astype(BF16)
        for i in range(chunks):
            for fetch in fetches(i):
                fetch.wait()


def grads_kernel(
    first_row, core_ref, lam_ref, q_ref, g_ref, state_ref,
    qh_ref, gh_ref, send_ref, keep_ref, grad_ref,
):
    heads, width = q_ref.shape[2:]
    half = heads // 2
    levels = grad_ref.shape[0]
    qh_ref[0] = jnp.swapaxes(q_ref[0], 0, 1)
    gh_ref[0] = jnp.swapaxes(g_ref[0], 0, 1)
    first = pl.program_id(0) == 0
    rows = [lam_ref[first_row + b : first_row + b + 1, :] for b in range(levels)]
    for h in range(heads):
        query_t = qh_ref[0, h].T
        weighted = stack_levels([scaled(row, query_t) for row in rows], 0)
        grad = dot(weighted, gh_ref[0, h])
        for b in range(levels):
            part = grad[b * width : (b + 1) * width]
            grad_ref[b, h] = jnp.where(first, part, grad_ref[b, h] + part)

    for core in range(2):

        @pl.when((pl.program_id(0) == pl.num_programs(0) - 1) & (core_ref[0] == core))
        def _():
            for h in range(heads):
                send_ref[h] = state_ref[h] if core == 0 else grad_ref[0, h]
            for level in range(levels):
                for i in range(half):
                    spot = level * half + i
                    source = state_ref if level == 0 else grad_ref.at[level]
                    keep_ref[spot] = source[core * half + i]
                    send_ref[heads + spot] = source[(1 - core) * half + i]


def make_mask(lam_ref, span, mask_ref):
    tile = mask_ref.shape[0]
    part = min(128, tile)
    source = lax.broadcasted_iota(jnp.int32, (part, part), 0)
    target = lax.broadcasted_iota(jnp.int32, (part, part), 1)
    differ = jnp.where(source <= target, jnp.bitwise_xor(source, target), -1)
    for to in range(0, tile, part):
        lanes = slice(span.start + to, span.start + to + part)
        mask = jnp.where(differ >= 0, lam_ref[0:1, lanes], 0.0)
        for power in range(bits_of(part)):
            mask = jnp.where(differ >= 1 << power, lam_ref[power + 1 : power + 2, lanes], mask)
        mask_ref[to : to + part, to : to + part] = mask
        for at in range(0, tile, part):
            if at < to:
                level = bits_of(at ^ to) + 1
                row = lam_ref[level : level + 1, lanes]
                mask_ref[at : at + part, to : to + part] = jnp.broadcast_to(row, (part, part))
            elif at > to:
                mask_ref[at : at + part, to : to + part] = jnp.zeros((part, part), F32)


def diagonal_tile(key, value, query, grad, mask):
    weight_q = (mask * dot_nt(value, grad)).astype(BF16)
    weight_v = (mask * dot_nt(key, query)).astype(BF16)
    dk = dot(weight_q, query).astype(BF16)
    dv = dot(weight_v, grad).astype(BF16)
    return dot(key.T, weight_q), dk, dv


def first_tile_kernel(
    lam_ref, k_ref, v_ref, q_ref, g_ref, dqt_ref, dq_ref, dk_ref, dv_ref, mask_ref
):
    del dq_ref
    make_mask(lam_ref, slice(0, mask_ref.shape[0]), mask_ref)

    @pl.loop(0, k_ref.shape[1], unroll=4)
    def _(h):
        dqt_ref[h], dk_ref[0, h], dv_ref[0, h] = diagonal_tile(
            k_ref[0, h], v_ref[0, h], q_ref[0, h], g_ref[0, h], mask_ref[...]
        )


def local_kernel(
    flag_ref, lam_ref, k_ref, v_ref, q_ref, g_ref, level_ref, found_ref, dqt_ref, dq_in, dk_in, dv_in,
    dq_ref, dk_ref, dv_ref, gin_ref, mask_ref, half_ref,
):
    del dq_in, dk_in, dv_in
    chunks, heads, tile, width = k_ref.shape
    tile_bits = bits_of(tile)
    first_row = tile_bits + bits_of(chunks) + 1
    groups = level_sources(chunks)
    off = (1 - flag_ref[0]).astype(F32)

    @pl.loop(0, heads, unroll=4)
    def _(h):
        found = found_ref[h]
        half_ref[h] = found.astype(BF16)
        for i in range(chunks):
            gin_ref[i, h] = off * found
        row = lam_ref[first_row : first_row + 1, :tile]
        dqt = dqt_ref[h] + row * dot_nt(half_ref[h], g_ref[0, h])
        dq_ref[0, h] = dqt.astype(BF16).T

    for c in range(1, chunks):
        span = slice(c * tile, (c + 1) * tile)
        make_mask(lam_ref, span, mask_ref)

        @pl.loop(0, heads, unroll=4)
        def _(h):
            query, grad = q_ref[c, h], g_ref[c, h]
            dqt, dk_ref[c, h], dv_ref[c, h] = diagonal_tile(
                k_ref[c, h], v_ref[c, h], query, grad, mask_ref[...]
            )
            dqt = dqt + lam_ref[first_row : first_row + 1, span] * dot_nt(half_ref[h], grad)
            query_t = query.T
            for j in range(bits_of(chunks)):
                if c >> j & 1:
                    row = lam_ref[tile_bits + 1 + j : tile_bits + 2 + j, span]
                    first = (c >> j ^ 1) << j
                    sources = range(first, first + (1 << j))
                    dqt = dqt + row * dot_nt(level_ref[groups.index(sources), h], grad)
                    part = dot(scaled(row, query_t), grad)
                    for i in sources:
                        gin_ref[i, h] = gin_ref[i, h] + part
            dq_ref[c, h] = dqt.astype(BF16).T


def pair_kernel(flag_ref, keep_ref, found_ref, *out_refs):
    half = out_refs[0].shape[0]
    heads = found_ref.shape[0] - keep_ref.shape[0]

    def pair(level, i):
        return keep_ref[level * half + i] + found_ref[heads + level * half + i]

    for n, out_ref in enumerate(out_refs):
        for on in range(2):

            @pl.when(flag_ref[n + 1] == on)
            def _():
                for i in range(half):
                    out_ref[i] = pair((n + 1) * on, i)


def sum_kernel(counts, *refs):
    out_ref = refs[-1]
    at = 0
    for n, count in enumerate(counts):
        for i in range(out_ref.shape[1]):
            out_ref[n, i] = functools.reduce(jnp.add, [r[i] for r in refs[at : at + count]])
        at += count


def widen(lam_ref, first_row, lanes, wide_ref):
    for b in range(wide_ref.shape[0]):
        row = lam_ref[first_row + b : first_row + b + 1, lanes]
        wide_ref[b] = jnp.broadcast_to(row, wide_ref.shape[:0:-1]).T


def received(flag_ref, sums_ref, i):
    parts = [sums_ref[b, i] for b in range(sums_ref.shape[0])]
    off = [(1 - flag_ref[b + 1]).astype(F32) for b in range(len(parts))]
    state = functools.reduce(jnp.add, [w * part for w, part in zip(off, parts)])
    return stack_levels([part.astype(BF16) for part in parts], 0), state


def add_received(half, state, wide_ref, key, value, grad, dq, dk, dv):
    width = key.shape[1]
    dq = dq.astype(F32)
    projected = dot_nt(grad, half)
    for b in range(wide_ref.shape[0]):
        dq = dq + wide_ref[b] * projected[:, b * width : (b + 1) * width]
    state = state.astype(BF16)
    none = jnp.zeros((width, width), BF16)
    right = jnp.concatenate(
        [
            jnp.concatenate([state.T, none], axis=1),
            jnp.concatenate([none, state], axis=1),
        ],
        axis=0,
    )
    product = dot(jnp.concatenate([value, key], axis=1), right)
    dk = dk.astype(F32) + product[:, :width]
    dv = dv.astype(F32) + product[:, width:]
    return dq.astype(BF16), dk.astype(BF16), dv.astype(BF16)


def own_half_kernel(
    first_row, flag_ref, lam_ref, k_ref, v_ref, g_ref, gin_ref, sums_ref, dq_in, dk_in, dv_in,
    dq_ref, dk_ref, dv_ref, wide_ref, half_ref, state_ref,
):
    chunks, _, tile, _ = k_ref.shape
    half = half_ref.shape[0]
    start = flag_ref[0] * half
    for i in range(half):
        half_ref[i], state_ref[i] = received(flag_ref, sums_ref, i)
    for c in range(chunks):
        widen(lam_ref, first_row, slice(c * tile, (c + 1) * tile), wide_ref)
        for i in range(half):
            h = start + i
            dq_ref[c, h], dk_ref[c, h], dv_ref[c, h] = add_received(
                half_ref[i], gin_ref[c, h] + state_ref[i], wide_ref,
                k_ref[c, h], v_ref[c, h], g_ref[c, h],
                dq_in[c, h], dk_in[c, h], dv_in[c, h],
            )


def final_kernel(
    first_row, flag_ref, lam_ref, k_ref, v_ref, g_ref, dq_in, dk_in, dv_in, gin_ref, sums_ref,
    dq_ref, dk_ref, dv_ref, wide_ref, half_ref, state_ref,
):
    heads = k_ref.shape[1]
    half = half_ref.shape[0]

    @pl.when(pl.program_id(0) == 0)
    def _():
        for i in range(half):
            half_ref[i], state_ref[i] = received(flag_ref, sums_ref, i)

    widen(lam_ref, first_row, slice(None), wide_ref)
    for core in range(2):

        @pl.when(flag_ref[0] == core)
        def _():
            done = []
            for h in range(heads):
                parts = [x[0, h] for x in (dq_in, dk_in, dv_in)]
                if h // half != core:
                    i = h % half
                    parts = add_received(
                        half_ref[i], gin_ref[0, h] + state_ref[i], wide_ref,
                        k_ref[0, h], v_ref[0, h], g_ref[0, h], *parts,
                    )
                done.append(parts)
            for out_ref, parts in zip((dq_ref, dk_ref, dv_ref), zip(*done)):
                out_ref[...] = jnp.swapaxes(jnp.stack(parts), 0, 1)


def shape(dims, dtype):
    return jax.ShapeDtypeStruct(dims, dtype)


def params(limit):
    return pltpu.CompilerParams(vmem_limit_bytes=limit * MIB)


def cost(flops, size):
    return pl.CostEstimate(flops=int(flops), bytes_accessed=int(size), transcendentals=0)


def on_device(queries, keys, values, out_grad, level_codes):
    count, heads, width = queries.shape
    scale = width ** (-0.5)
    local_bits = bits_of(count)
    blocks = lax.axis_size("seq")
    tree_bits = bits_of(blocks)
    groups = lax.axis_size("head")
    here = lax.axis_index("seq")
    tile = min(256, count)
    chunks = count // tile
    half = heads // 2
    rows = local_bits + 1 + tree_bits
    flags = jnp.bitwise_and(jnp.right_shift(here, jnp.arange(max(tree_bits, 1))), 1)

    def permute(x, apart):
        return lax.ppermute(x, "seq", [(i, i ^ apart) for i in range(blocks)])

    def in_hbm(*arrays):
        return [pltpu.with_memory_space_constraint(x, pltpu.HBM) for x in arrays]

    def near(*arrays):
        return [pltpu.with_memory_space_constraint(x, pltpu.VMEM) for x in arrays]

    token_block = pl.BlockSpec((tile, heads, width), lambda c: (c, 0, 0))
    lam_block = pl.BlockSpec((rows, tile), lambda c: (0, c))
    in_smem = pl.BlockSpec(memory_space=pltpu.SMEM)
    in_vmem = pl.BlockSpec(memory_space=pltpu.VMEM)
    anywhere = pl.BlockSpec(memory_space=pl.ANY)

    def chunk_block(*dims):
        return pl.BlockSpec((1,) + dims, lambda c: (c,) + (0,) * len(dims))

    def whole(*dims):
        return pl.BlockSpec(dims, lambda c: (0,) * len(dims))

    head_block = chunk_block(heads, tile, width)
    natural = pltpu.VMEM((chunks, heads, tile, width), BF16)
    square = (width, width)
    size = count * heads * width
    groups_in = len(level_sources(chunks))
    queries, out_grad = [x.reshape(chunks, tile, heads, width) for x in (queries, out_grad)]
    queries, keys, values, out_grad = in_hbm(queries, keys, values, out_grad)

    kh, vh, level_state, state, queries, out_grad = pl.pallas_call(
        states_kernel,
        grid=(chunks,),
        in_specs=[token_block, token_block, anywhere, anywhere],
        out_specs=[
            head_block, head_block, whole(groups_in, heads, *square), whole(heads, *square),
            in_vmem, in_vmem,
        ],
        out_shape=[
            natural, natural, pltpu.VMEM((groups_in, heads, *square), BF16),
            pltpu.VMEM((heads, *square), F32),
            *[pltpu.VMEM((chunks, tile, heads, width), BF16)] * 2,
        ],
        scratch_shapes=[
            pltpu.VMEM((chunks, heads, *square), F32),
            pltpu.SemaphoreType.DMA((2, chunks)),
        ],
        compiler_params=params(10),
        cost_estimate=cost(2 * size * width, 8 * size),
        name="states",
    )(keys, values, queries, out_grad)

    group = lax.axis_index("head")
    pieces = [
        lax.ppermute(level_codes, "head", [(i, (i + r) % groups) for i in range(groups)])
        for r in range(1, groups)
    ]
    pieces, state = lax.optimization_barrier((pieces, state))
    pieces = jnp.stack([level_codes, *pieces])
    codes = jnp.concatenate(
        [
            lax.dynamic_index_in_dim(pieces, (group - j) % groups, 0, keepdims=False)[:rows]
            for j in range(groups)
        ],
        axis=1,
    )
    order = jnp.arange(rows)
    factor = jnp.exp2(-0.5 * jnp.maximum(order.astype(F32) - 1.0, 0.0)) / 16.0
    on_bit = jnp.bitwise_and(jnp.right_shift(here, jnp.maximum(order - local_bits - 1, 0)), 1)
    factor = jnp.where(order > local_bits, factor * on_bit.astype(F32), factor)
    lam = codes.astype(F32) * (scale * factor)[:, None]

    qh, gh, send, keep = pl.pallas_call(
        functools.partial(grads_kernel, local_bits + 1),
        grid=(chunks,),
        in_specs=[in_smem, lam_block, *[chunk_block(tile, heads, width)] * 2, whole(heads, *square)],
        out_specs=[
            head_block, head_block,
            whole(heads + tree_bits * half, *square), whole(tree_bits * half, *square),
        ],
        out_shape=[
            natural, natural,
            pltpu.VMEM((heads + tree_bits * half, *square), F32),
            pltpu.VMEM((tree_bits * half, *square), F32),
        ],
        scratch_shapes=[pltpu.VMEM((tree_bits, heads, *square), F32)],
        compiler_params=params(10),
        cost_estimate=cost(2 * tree_bits * size * width, 8 * size),
        name="level_grads",
    )(flags, lam, *near(queries, out_grad, state))
    found = permute(send, 1)
    kh, vh, qh, gh, level_state, keep = near(kh, vh, qh, gh, level_state, keep)

    dqt, *parts = pl.pallas_call(
        first_tile_kernel,
        in_specs=[in_vmem] * 5,
        out_specs=[in_vmem] * 4,
        out_shape=[pltpu.VMEM((heads, width, tile), F32)] + [natural] * 3,
        scratch_shapes=[pltpu.VMEM((tile, tile), F32)],
        compiler_params=params(6),
        cost_estimate=cost(14 * size * tile / chunks, 4 * size),
        name="first_tile",
    )(lam, kh, vh, qh, gh)
    messages = pl.pallas_call(
        pair_kernel,
        in_specs=[in_smem, in_vmem, in_vmem],
        out_specs=[in_vmem] * (tree_bits - 1),
        out_shape=[pltpu.VMEM((half, *square), F32)] * (tree_bits - 1),
        compiler_params=params(4),
        cost_estimate=cost(size, size),
        name="pair",
    )(flags, keep, found)
    *messages, parts = lax.optimization_barrier((*messages, parts))
    arrived = [
        [permute(messages[b - 1], 1 << b | m) for m in range(0, 1 << b, 2)]
        for b in range(1, tree_bits)
    ]
    *parts, gin = pl.pallas_call(
        local_kernel,
        in_specs=[in_smem] + [in_vmem] * 8 + [anywhere] * 3,
        out_specs=[in_vmem] * 4,
        out_shape=[natural] * 3 + [pltpu.VMEM((chunks, heads, *square), F32)],
        input_output_aliases={9: 0, 10: 1, 11: 2},
        scratch_shapes=[pltpu.VMEM((tile, tile), F32), pltpu.VMEM((heads, *square), BF16)],
        compiler_params=params(6),
        cost_estimate=cost(14 * size * tile, 4 * size),
        name="local",
    )(flags, lam, kh, vh, qh, gh, level_state, found, *near(dqt, *parts))
    arrived, parts = lax.optimization_barrier((arrived, parts))
    flat = [x for some in arrived for x in some]
    sums_shape = (tree_bits - 1, half, *square)
    mine = pl.pallas_call(
        functools.partial(sum_kernel, [len(some) for some in arrived]),
        in_specs=[in_vmem] * len(flat),
        out_specs=in_vmem,
        out_shape=pltpu.VMEM(sums_shape, F32),
        compiler_params=params(6),
        cost_estimate=cost(size, size),
        name="sums",
    )(*flat)
    others = permute(mine, 1)

    kept = [
        pltpu.VMEM((tree_bits - 1, tile, width), F32),
        pltpu.VMEM((half, (tree_bits - 1) * width, width), BF16),
        pltpu.VMEM((half, *square), F32),
    ]
    gin, mine = near(gin, mine)
    parts = pl.pallas_call(
        functools.partial(own_half_kernel, local_bits + 2),
        in_specs=[in_smem] + [in_vmem] * 9,
        out_specs=[in_vmem] * 3,
        out_shape=[natural] * 3,
        input_output_aliases={7: 0, 8: 1, 9: 2},
        scratch_shapes=kept,
        compiler_params=params(6),
        cost_estimate=cost((tree_bits + 2) * size * width, 8 * size),
        name="own_half",
    )(flags, lam, kh, vh, gh, gin, mine, *near(*parts))
    others, parts = lax.optimization_barrier((others, parts))
    return pl.pallas_call(
        functools.partial(final_kernel, local_bits + 2),
        grid=(chunks,),
        in_specs=[
            in_smem, lam_block, *[head_block] * 6, chunk_block(heads, *square), whole(*sums_shape),
        ],
        out_specs=[token_block] * 3,
        out_shape=[shape((count, heads, width), BF16)] * 3,
        scratch_shapes=kept,
        compiler_params=params(12),
        cost_estimate=cost((tree_bits + 2) * size * width, 16 * size),
        name="final",
    )(flags, lam, kh, vh, gh, *near(*parts), gin, others)


def solution(mesh):
    tokens = P("seq", "head", None)
    return jax.shard_map(
        on_device,
        mesh=mesh,
        in_specs=(tokens, tokens, tokens, tokens, P(None, ("seq", "head"))),
        out_specs=(tokens, tokens, tokens),
        check_vma=False,
    )
```

```python
import functools

import jax
import jax.numpy as jnp
from jax import lax
from jax.experimental import pallas as pl
from jax.experimental.pallas import tpu as pltpu
from jax.sharding import PartitionSpec as P

F32 = jnp.float32
BF16 = jnp.bfloat16
MIB = 1 << 20


def bits_of(size):
    return size.bit_length() - 1


def dot(a, b):
    return jnp.dot(a, b, preferred_element_type=F32)


def dot_nt(a, b):
    return lax.dot_general(a, b, (((1,), (1,)), ((), ())), preferred_element_type=F32)


def scaled(row, x):
    return (row * x.astype(F32)).astype(BF16)


def stack_levels(parts, axis):
    return parts[0] if len(parts) == 1 else jnp.concatenate(parts, axis=axis)


def level_sources(chunks):
    found = []
    for j in range(bits_of(chunks)):
        for first in range(0, chunks, 2 << j):
            found.append(range(first, first + (1 << j)))
    return found


def states_kernel(k_ref, v_ref, kh_ref, vh_ref, level_ref, total_ref, chunk_ref):
    heads = k_ref.shape[1]
    chunks = chunk_ref.shape[0]
    step = pl.program_id(0)
    kh_ref[0] = jnp.swapaxes(k_ref[...], 0, 1)
    vh_ref[0] = jnp.swapaxes(v_ref[...], 0, 1)
    for h in range(heads):
        chunk_ref[step, h] = dot(kh_ref[0, h].T, vh_ref[0, h])

    @pl.when(step == chunks - 1)
    def _():
        for h in range(heads):
            tiles = [chunk_ref[i, h] for i in range(chunks)]
            total_ref[h] = functools.reduce(jnp.add, tiles)
            for n, sources in enumerate(level_sources(chunks)):
                state = functools.reduce(jnp.add, [tiles[i] for i in sources])
                level_ref[n, h] = state.astype(BF16)


def grads_kernel(
    flag_ref, factor_ref, codes_ref, q_ref, g_ref, state_ref,
    qh_ref, gh_ref, send_ref, keep_ref, grad_ref,
):
    heads, width = q_ref.shape[1:]
    half = heads // 2
    levels, tile = codes_ref.shape
    qh_ref[0] = jnp.swapaxes(q_ref[...], 0, 1)
    gh_ref[0] = jnp.swapaxes(g_ref[...], 0, 1)
    first = pl.program_id(0) == 0
    rows = [
        jnp.broadcast_to(codes_ref[b : b + 1, :], (width, tile)).astype(BF16) for b in range(levels)
    ]
    for h in range(heads):
        query_t = qh_ref[0, h].T
        weighted = stack_levels([row * query_t for row in rows], 0)
        grad = dot(weighted, gh_ref[0, h])
        for b in range(levels):
            part = grad[b * width : (b + 1) * width]
            grad_ref[b, h] = jnp.where(first, part, grad_ref[b, h] + part)

    for core in range(2):

        @pl.when((pl.program_id(0) == pl.num_programs(0) - 1) & (flag_ref[0] == core))
        def _():
            for h in range(heads):
                send_ref[h] = state_ref[h] if core == 0 else factor_ref[0] * grad_ref[0, h]
            for level in range(levels):
                for i in range(half):
                    spot = level * half + i
                    mine, other = core * half + i, (1 - core) * half + i
                    if level == 0:
                        keep_ref[spot] = state_ref[mine]
                        send_ref[heads + spot] = state_ref[other]
                    else:
                        keep_ref[spot] = factor_ref[level] * grad_ref[level, mine]
                        send_ref[heads + spot] = factor_ref[level] * grad_ref[level, other]


def make_mask(lam_ref, span, mask_ref):
    tile = mask_ref.shape[0]
    part = min(128, tile)
    source = lax.broadcasted_iota(jnp.int32, (part, part), 0)
    target = lax.broadcasted_iota(jnp.int32, (part, part), 1)
    differ = jnp.where(source <= target, jnp.bitwise_xor(source, target), -1)
    for to in range(0, tile, part):
        lanes = slice(span.start + to, span.start + to + part)
        mask = jnp.where(differ >= 0, lam_ref[0:1, lanes], 0.0)
        for power in range(bits_of(part)):
            mask = jnp.where(differ >= 1 << power, lam_ref[power + 1 : power + 2, lanes], mask)
        mask_ref[to : to + part, to : to + part] = mask
        for at in range(0, tile, part):
            if at < to:
                level = bits_of(at ^ to) + 1
                row = lam_ref[level : level + 1, lanes]
                mask_ref[at : at + part, to : to + part] = jnp.broadcast_to(row, (part, part))
            elif at > to:
                mask_ref[at : at + part, to : to + part] = jnp.zeros((part, part), F32)


def diagonal_tile(key, value, query, grad, mask):
    weight_q = (mask * dot_nt(value, grad)).astype(BF16)
    weight_v = (mask * dot_nt(key, query)).astype(BF16)
    dk = dot(weight_q, query).astype(BF16)
    dv = dot(weight_v, grad).astype(BF16)
    return dot(key.T, weight_q), dk, dv


def first_tile_kernel(
    lam_ref, k_ref, v_ref, q_ref, g_ref, dqt_ref, dq_ref, dk_ref, dv_ref, mask_ref
):
    del dq_ref
    make_mask(lam_ref, slice(0, mask_ref.shape[0]), mask_ref)

    @pl.loop(0, k_ref.shape[1], unroll=4)
    def _(h):
        dqt_ref[h], dk_ref[0, h], dv_ref[0, h] = diagonal_tile(
            k_ref[0, h], v_ref[0, h], q_ref[0, h], g_ref[0, h], mask_ref[...]
        )


def local_kernel(
    flag_ref, lam_ref, k_ref, v_ref, q_ref, g_ref, level_ref, found_ref, dqt_ref, dq_in, dk_in, dv_in,
    dq_ref, dk_ref, dv_ref, gin_ref, mask_ref, half_ref,
):
    del dq_in, dk_in, dv_in
    chunks, heads, tile, width = k_ref.shape
    tile_bits = bits_of(tile)
    first_row = tile_bits + bits_of(chunks) + 1
    groups = level_sources(chunks)
    off = (1 - flag_ref[0]).astype(F32)

    @pl.loop(0, heads, unroll=4)
    def _(h):
        found = found_ref[h]
        half_ref[h] = found.astype(BF16)
        for i in range(chunks):
            gin_ref[i, h] = off * found
        row = lam_ref[first_row : first_row + 1, :tile]
        dqt = dqt_ref[h] + row * dot_nt(half_ref[h], g_ref[0, h])
        dq_ref[0, h] = dqt.astype(BF16).T

    for c in range(1, chunks):
        span = slice(c * tile, (c + 1) * tile)
        make_mask(lam_ref, span, mask_ref)

        @pl.loop(0, heads, unroll=4)
        def _(h):
            query, grad = q_ref[c, h], g_ref[c, h]
            dqt, dk_ref[c, h], dv_ref[c, h] = diagonal_tile(
                k_ref[c, h], v_ref[c, h], query, grad, mask_ref[...]
            )
            dqt = dqt + lam_ref[first_row : first_row + 1, span] * dot_nt(half_ref[h], grad)
            query_t = query.T
            for j in range(bits_of(chunks)):
                if c >> j & 1:
                    row = lam_ref[tile_bits + 1 + j : tile_bits + 2 + j, span]
                    first = (c >> j ^ 1) << j
                    sources = range(first, first + (1 << j))
                    dqt = dqt + row * dot_nt(level_ref[groups.index(sources), h], grad)
                    part = dot(scaled(row, query_t), grad)
                    for i in sources:
                        gin_ref[i, h] = gin_ref[i, h] + part
            dq_ref[c, h] = dqt.astype(BF16).T


def pair_kernel(levels, flag_ref, keep_ref, found_ref, *out_refs):
    half = out_refs[0].shape[0]
    heads = found_ref.shape[0] - keep_ref.shape[0]

    def pair(level, i):
        return keep_ref[level * half + i] + found_ref[heads + level * half + i]

    for b, out_ref in zip(levels, out_refs):
        for on in range(2):

            @pl.when(flag_ref[b] == on)
            def _():
                for i in range(half):
                    out_ref[i] = pair(b * on, i)


def sum_kernel(levels, *refs):
    out_ref = refs[-1]
    for n in range(out_ref.shape[0]):
        for i in range(out_ref.shape[1]):
            parts = [ref[i] for b, ref in zip(levels, refs) if b == n + 1]
            out_ref[n, i] = functools.reduce(jnp.add, parts)


def widen(lam_ref, first_row, lanes, wide_ref):
    for b in range(wide_ref.shape[0]):
        row = lam_ref[first_row + b : first_row + b + 1, lanes]
        wide_ref[b] = jnp.broadcast_to(row, wide_ref.shape[:0:-1]).T


def received(flag_ref, sums_ref, i):
    parts = [sums_ref[b, i] for b in range(sums_ref.shape[0])]
    off = [(1 - flag_ref[b + 1]).astype(F32) for b in range(len(parts))]
    state = functools.reduce(jnp.add, [w * part for w, part in zip(off, parts)])
    return stack_levels([part.astype(BF16) for part in parts], 0), state


def add_to_query(half, wide_ref, grad, dq):
    width = grad.shape[1]
    dq = dq.astype(F32)
    projected = dot_nt(grad, half)
    for b in range(wide_ref.shape[0]):
        dq = dq + wide_ref[b] * projected[:, b * width : (b + 1) * width]
    return dq.astype(BF16)


def add_to_key_value(state, key, value, dk, dv):
    width = key.shape[1]
    state = state.astype(BF16)
    none = jnp.zeros((width, width), BF16)
    right = jnp.concatenate(
        [
            jnp.concatenate([state.T, none], axis=1),
            jnp.concatenate([none, state], axis=1),
        ],
        axis=0,
    )
    product = dot(jnp.concatenate([value, key], axis=1), right)
    dk = dk.astype(F32) + product[:, :width]
    dv = dv.astype(F32) + product[:, width:]
    return dk.astype(BF16), dv.astype(BF16)


def own_half_kernel(
    first_row, flag_ref, lam_ref, k_ref, v_ref, g_ref, gin_ref, sums_ref, dq_in, dk_in, dv_in,
    dq_ref, dk_ref, dv_ref, wide_ref, half_ref, state_ref,
):
    chunks, _, tile, _ = k_ref.shape
    half = half_ref.shape[0]
    start = flag_ref[0] * half
    for i in range(half):
        half_ref[i], state_ref[i] = received(flag_ref, sums_ref, i)
    for c in range(chunks):
        widen(lam_ref, first_row, slice(c * tile, (c + 1) * tile), wide_ref)
        for i in range(half):
            h = start + i
            dq_ref[c, h] = add_to_query(half_ref[i], wide_ref, g_ref[c, h], dq_in[c, h])
            dk_ref[c, h], dv_ref[c, h] = add_to_key_value(
                gin_ref[c, h] + state_ref[i], k_ref[c, h], v_ref[c, h], dk_in[c, h], dv_in[c, h]
            )


def final_kernel(
    first_row, flag_ref, lam_ref, k_ref, v_ref, g_ref, dq_in, dk_in, dv_in, gin_ref, sums_ref,
    dq_out, dk_out, dv_out, done_ref, wide_ref, half_ref, state_ref, sems,
):
    chunks, heads, tile, _ = k_ref.shape
    half = half_ref.shape[0]
    outs = (dq_out, dk_out, dv_out)

    def ship(n, c):
        place = pl.ds(c * tile, tile)
        return pltpu.make_async_copy(done_ref.at[n, c], outs[n].at[place], sems.at[n, c])

    for i in range(half):
        half_ref[i], state_ref[i] = received(flag_ref, sums_ref, i)
    for core in range(2):

        @pl.when(flag_ref[0] == core)
        def _():
            for c in range(chunks):
                widen(lam_ref, first_row, slice(c * tile, (c + 1) * tile), wide_ref)
                queries, keys, values = [], [], []
                for h in range(heads):
                    query, key, value = dq_in[c, h], dk_in[c, h], dv_in[c, h]
                    if h // half != core:
                        i = h % half
                        query = add_to_query(half_ref[i], wide_ref, g_ref[c, h], query)
                        key, value = add_to_key_value(
                            gin_ref[c, h] + state_ref[i], k_ref[c, h], v_ref[c, h], key, value
                        )
                    queries.append(query)
                    keys.append(key)
                    values.append(value)
                for n, parts in enumerate((queries, keys, values)):
                    done_ref[n, c] = jnp.swapaxes(jnp.stack(parts), 0, 1)
                    ship(n, c).start()

    for c in range(chunks):
        for n in range(3):
            ship(n, c).wait()


def shape(dims, dtype):
    return jax.ShapeDtypeStruct(dims, dtype)


def params(limit):
    return pltpu.CompilerParams(vmem_limit_bytes=limit * MIB)


def cost(flops, size):
    return pl.CostEstimate(flops=int(flops), bytes_accessed=int(size), transcendentals=0)


def on_device(queries, keys, values, out_grad, level_codes):
    count, heads, width = queries.shape
    scale = width ** (-0.5)
    local_bits = bits_of(count)
    blocks = lax.axis_size("seq")
    tree_bits = bits_of(blocks)
    groups = lax.axis_size("head")
    here = lax.axis_index("seq")
    tile = min(256, count)
    chunks = count // tile
    half = heads // 2
    rows = local_bits + 1 + tree_bits
    flags = jnp.bitwise_and(jnp.right_shift(here, jnp.arange(max(tree_bits, 1))), 1)

    def permute(x, apart):
        return lax.ppermute(x, "seq", [(i, i ^ apart) for i in range(blocks)])

    def in_hbm(*arrays):
        return [pltpu.with_memory_space_constraint(x, pltpu.HBM) for x in arrays]

    def near(*arrays):
        return [pltpu.with_memory_space_constraint(x, pltpu.VMEM) for x in arrays]

    token_block = pl.BlockSpec((tile, heads, width), lambda c: (c, 0, 0))
    lam_block = pl.BlockSpec((rows, tile), lambda c: (0, c))
    in_smem = pl.BlockSpec(memory_space=pltpu.SMEM)
    in_vmem = pl.BlockSpec(memory_space=pltpu.VMEM)
    anywhere = pl.BlockSpec(memory_space=pl.ANY)

    def chunk_block(*dims):
        return pl.BlockSpec((1,) + dims, lambda c: (c,) + (0,) * len(dims))

    def whole(*dims):
        return pl.BlockSpec(dims, lambda c: (0,) * len(dims))

    head_block = chunk_block(heads, tile, width)
    natural = pltpu.VMEM((chunks, heads, tile, width), BF16)
    square = (width, width)
    size = count * heads * width
    groups_in = len(level_sources(chunks))
    queries, keys, values, out_grad = in_hbm(queries, keys, values, out_grad)

    kh, vh, level_state, state = pl.pallas_call(
        states_kernel,
        grid=(chunks,),
        in_specs=[token_block, token_block],
        out_specs=[
            head_block, head_block, whole(groups_in, heads, *square), whole(heads, *square),
        ],
        out_shape=[
            natural, natural, pltpu.VMEM((groups_in, heads, *square), BF16),
            pltpu.VMEM((heads, *square), F32),
        ],
        scratch_shapes=[pltpu.VMEM((chunks, heads, *square), F32)],
        compiler_params=params(10),
        cost_estimate=cost(2 * size * width, 8 * size),
        name="states",
    )(keys, values)

    group = lax.axis_index("head")
    pieces = [
        lax.ppermute(level_codes, "head", [(i, (i + r) % groups) for i in range(groups)])
        for r in range(1, groups)
    ]
    pieces, state = lax.optimization_barrier((pieces, state))
    pieces = jnp.stack([level_codes, *pieces])
    codes = jnp.concatenate(
        [
            lax.dynamic_index_in_dim(pieces, (group - j) % groups, 0, keepdims=False)[:rows]
            for j in range(groups)
        ],
        axis=1,
    )
    order = jnp.arange(rows)
    factor = jnp.exp2(-0.5 * jnp.maximum(order.astype(F32) - 1.0, 0.0)) / 16.0
    on_bit = jnp.bitwise_and(jnp.right_shift(here, jnp.maximum(order - local_bits - 1, 0)), 1)
    factor = jnp.where(order > local_bits, factor * on_bit.astype(F32), factor)
    codes, factor = codes.astype(F32), scale * factor
    lam = codes * factor[:, None]

    qh, gh, send, keep = pl.pallas_call(
        grads_kernel,
        grid=(chunks,),
        in_specs=[
            in_smem, in_smem, pl.BlockSpec((tree_bits, tile), lambda c: (0, c)),
            token_block, token_block, whole(heads, *square),
        ],
        out_specs=[
            head_block, head_block,
            whole(heads + tree_bits * half, *square), whole(tree_bits * half, *square),
        ],
        out_shape=[
            natural, natural,
            pltpu.VMEM((heads + tree_bits * half, *square), F32),
            pltpu.VMEM((tree_bits * half, *square), F32),
        ],
        scratch_shapes=[pltpu.VMEM((tree_bits, heads, *square), F32)],
        compiler_params=params(10),
        cost_estimate=cost(2 * tree_bits * size * width, 8 * size),
        name="level_grads",
    )(flags, factor[local_bits + 1 :], codes[local_bits + 1 :], queries, out_grad, *near(state))
    found = permute(send, 1)
    kh, vh, qh, gh, level_state, keep = near(kh, vh, qh, gh, level_state, keep)

    dqt, *parts = pl.pallas_call(
        first_tile_kernel,
        in_specs=[in_vmem] * 5,
        out_specs=[in_vmem] * 4,
        out_shape=[pltpu.VMEM((heads, width, tile), F32)] + [natural] * 3,
        scratch_shapes=[pltpu.VMEM((tile, tile), F32)],
        compiler_params=params(6),
        cost_estimate=cost(14 * size * tile / chunks, 4 * size),
        name="first_tile",
    )(lam, kh, vh, qh, gh)
    hops = [1 << b | m for b in range(1, tree_bits) for m in range(0, 1 << b, 2)]
    hops.sort(key=lambda hop: (hop & hop - 1) == 0)
    messages = pl.pallas_call(
        functools.partial(pair_kernel, [bits_of(hop) for hop in hops]),
        in_specs=[in_smem, in_vmem, in_vmem],
        out_specs=[in_vmem] * len(hops),
        out_shape=[pltpu.VMEM((half, *square), F32)] * len(hops),
        compiler_params=params(4),
        cost_estimate=cost(size, size),
        name="pair",
    )(flags, keep, found)
    *messages, parts = lax.optimization_barrier((*messages, parts))
    arrived = [permute(x, hop) for hop, x in zip(hops, messages)]
    *parts, gin = pl.pallas_call(
        local_kernel,
        in_specs=[in_smem] + [in_vmem] * 8 + [anywhere] * 3,
        out_specs=[in_vmem] * 4,
        out_shape=[natural] * 3 + [pltpu.VMEM((chunks, heads, *square), F32)],
        input_output_aliases={9: 0, 10: 1, 11: 2},
        scratch_shapes=[pltpu.VMEM((tile, tile), F32), pltpu.VMEM((heads, *square), BF16)],
        compiler_params=params(6),
        cost_estimate=cost(14 * size * tile, 4 * size),
        name="local",
    )(flags, lam, kh, vh, qh, gh, level_state, found, *near(dqt, *parts))
    arrived, parts = lax.optimization_barrier((arrived, parts))
    sums_shape = (tree_bits - 1, half, *square)
    mine = pl.pallas_call(
        functools.partial(sum_kernel, [bits_of(hop) for hop in hops]),
        in_specs=[in_vmem] * len(hops),
        out_specs=in_vmem,
        out_shape=pltpu.VMEM(sums_shape, F32),
        compiler_params=params(6),
        cost_estimate=cost(size, size),
        name="sums",
    )(*arrived)
    others = permute(mine, 1)

    kept = [
        pltpu.VMEM((tree_bits - 1, tile, width), F32),
        pltpu.VMEM((half, (tree_bits - 1) * width, width), BF16),
        pltpu.VMEM((half, *square), F32),
    ]
    gin, mine = near(gin, mine)
    parts = pl.pallas_call(
        functools.partial(own_half_kernel, local_bits + 2),
        in_specs=[in_smem] + [in_vmem] * 9,
        out_specs=[in_vmem] * 3,
        out_shape=[natural] * 3,
        input_output_aliases={7: 0, 8: 1, 9: 2},
        scratch_shapes=kept,
        compiler_params=params(6),
        cost_estimate=cost((tree_bits + 2) * size * width, 8 * size),
        name="own_half",
    )(flags, lam, kh, vh, gh, gin, mine, *near(*parts))
    others, parts = lax.optimization_barrier((others, parts))
    return pl.pallas_call(
        functools.partial(final_kernel, local_bits + 2),
        in_specs=[in_smem] + [in_vmem] * 9,
        out_specs=[anywhere] * 3,
        out_shape=[pltpu.HBM((count, heads, width), BF16)] * 3,
        scratch_shapes=[
            pltpu.VMEM((3, chunks, tile, heads, width), BF16), *kept,
            pltpu.SemaphoreType.DMA((3, chunks)),
        ],
        compiler_params=params(12),
        cost_estimate=cost((tree_bits + 2) * size * width, 16 * size),
        name="final",
    )(flags, lam, kh, vh, gh, *near(*parts), gin, others)


def solution(mesh):
    tokens = P("seq", "head", None)
    return jax.shard_map(
        on_device,
        mesh=mesh,
        in_specs=(tokens, tokens, tokens, tokens, P(None, ("seq", "head"))),
        out_specs=(tokens, tokens, tokens),
        check_vma=False,
    )
```

```python
import functools

import jax
import jax.numpy as jnp
from jax import lax
from jax.experimental import pallas as pl
from jax.experimental.pallas import tpu as pltpu
from jax.sharding import PartitionSpec as P

F32 = jnp.float32
BF16 = jnp.bfloat16
MIB = 1 << 20


def bits_of(size):
    return size.bit_length() - 1


def dot(a, b):
    return jnp.dot(a, b, preferred_element_type=F32)


def dot_nt(a, b):
    return lax.dot_general(a, b, (((1,), (1,)), ((), ())), preferred_element_type=F32)


def scaled(row, x):
    return (row * x.astype(F32)).astype(BF16)


def stack_levels(parts, axis):
    return parts[0] if len(parts) == 1 else jnp.concatenate(parts, axis=axis)


def level_sources(chunks):
    found = []
    for j in range(bits_of(chunks)):
        for first in range(0, chunks, 2 << j):
            found.append(range(first, first + (1 << j)))
    return found


def bit_of_block(b):
    return jnp.bitwise_and(jnp.right_shift(lax.axis_index("seq"), b), 1)


def states_kernel(
    k_ref, v_ref, q_ref, g_ref,
    kh_ref, vh_ref, qh_ref, gh_ref, qt_ref, level_ref, total_ref, chunk_ref,
):
    heads = k_ref.shape[1]
    chunks = chunk_ref.shape[0]
    step = pl.program_id(0)
    kh_ref[0] = jnp.swapaxes(k_ref[...], 0, 1)
    vh_ref[0] = jnp.swapaxes(v_ref[...], 0, 1)
    qh_ref[0] = jnp.swapaxes(q_ref[...], 0, 1)
    gh_ref[0] = jnp.swapaxes(g_ref[...], 0, 1)
    for h in range(heads):
        chunk_ref[step, h] = dot(kh_ref[0, h].T, vh_ref[0, h])
        qt_ref[0, h] = qh_ref[0, h].T

    @pl.when(step == chunks - 1)
    def _():
        for h in range(heads):
            tiles = [chunk_ref[i, h] for i in range(chunks)]
            total_ref[h] = functools.reduce(jnp.add, tiles)
            for n, sources in enumerate(level_sources(chunks)):
                state = functools.reduce(jnp.add, [tiles[i] for i in sources])
                level_ref[n, h] = state.astype(BF16)


def grads_kernel(first_row, lam_ref, qt_ref, g_ref, send_ref, keep_ref):
    chunks, heads, tile, width = g_ref.shape
    half = heads // 2
    levels = lam_ref.shape[0] - first_row

    for core in range(2):

        @pl.when(bit_of_block(0) == core)
        def _():
            for h in range(heads):
                weighted = [
                    stack_levels(
                        [
                            scaled(
                                lam_ref[first_row + b : first_row + b + 1, c * tile : (c + 1) * tile],
                                qt_ref[c, h],
                            )
                            for b in range(levels)
                        ],
                        0,
                    )
                    for c in range(chunks)
                ]
                grad = dot(stack_levels(weighted, 1), g_ref[:, h].reshape(chunks * tile, width))
                send_ref[h] = grad[:width]
                for b in range(1, levels):
                    part = grad[b * width : (b + 1) * width]
                    spot = (b - 1) * half + h % half
                    if h // half == core:
                        keep_ref[spot] = part
                    else:
                        send_ref[heads + spot] = part


def make_mask(lam_ref, span, mask_ref):
    tile = mask_ref.shape[0]
    part = min(128, tile)
    source = lax.broadcasted_iota(jnp.int32, (part, part), 0)
    target = lax.broadcasted_iota(jnp.int32, (part, part), 1)
    differ = jnp.where(source <= target, jnp.bitwise_xor(source, target), -1)
    for to in range(0, tile, part):
        lanes = slice(span.start + to, span.start + to + part)
        mask = jnp.where(differ >= 0, lam_ref[0:1, lanes], 0.0)
        for power in range(bits_of(part)):
            mask = jnp.where(differ >= 1 << power, lam_ref[power + 1 : power + 2, lanes], mask)
        mask_ref[to : to + part, to : to + part] = mask
        for at in range(0, tile, part):
            if at < to:
                level = bits_of(at ^ to) + 1
                row = lam_ref[level : level + 1, lanes]
                mask_ref[at : at + part, to : to + part] = jnp.broadcast_to(row, (part, part))
            elif at > to:
                mask_ref[at : at + part, to : to + part] = jnp.zeros((part, part), F32)


def diagonal_tile(key, value, query, grad, mask):
    weight_q = (mask * dot_nt(value, grad)).astype(BF16)
    weight_v = (mask * dot_nt(key, query)).astype(BF16)
    dk = dot(weight_q, query).astype(BF16)
    dv = dot(weight_v, grad).astype(BF16)
    return dot(key.T, weight_q), dk, dv


def first_tile_kernel(
    lam_ref, k_ref, v_ref, q_ref, g_ref, dqt_ref, dq_ref, dk_ref, dv_ref, mask_ref
):
    del dq_ref
    make_mask(lam_ref, slice(0, mask_ref.shape[0]), mask_ref)

    @pl.loop(0, k_ref.shape[1], unroll=4)
    def _(h):
        dqt_ref[h], dk_ref[0, h], dv_ref[0, h] = diagonal_tile(
            k_ref[0, h], v_ref[0, h], q_ref[0, h], g_ref[0, h], mask_ref[...]
        )


def local_kernel(
    lam_ref, k_ref, v_ref, q_ref, g_ref, qt_ref, level_ref, state_ref, grad_ref, dqt_ref,
    dq_in, dk_in, dv_in,
    dq_ref, dk_ref, dv_ref, gin_ref, mask_ref, half_ref,
):
    del dq_in, dk_in, dv_in
    chunks, heads, tile, width = k_ref.shape
    tile_bits = bits_of(tile)
    first_row = tile_bits + bits_of(chunks) + 1
    groups = level_sources(chunks)
    off = (1 - bit_of_block(0)).astype(F32)

    @pl.loop(0, heads, unroll=4)
    def _(h):
        half_ref[h] = state_ref[h].astype(BF16)
        for i in range(chunks):
            gin_ref[i, h] = off * grad_ref[h]
        row = lam_ref[first_row : first_row + 1, :tile]
        dqt = dqt_ref[h] + row * dot_nt(half_ref[h], g_ref[0, h])
        dq_ref[0, h] = dqt.astype(BF16).T

    for c in range(1, chunks):
        span = slice(c * tile, (c + 1) * tile)
        make_mask(lam_ref, span, mask_ref)

        @pl.loop(0, heads, unroll=4)
        def _(h):
            query, grad = q_ref[c, h], g_ref[c, h]
            dqt, dk_ref[c, h], dv_ref[c, h] = diagonal_tile(
                k_ref[c, h], v_ref[c, h], query, grad, mask_ref[...]
            )
            dqt = dqt + lam_ref[first_row : first_row + 1, span] * dot_nt(half_ref[h], grad)
            query_t = qt_ref[c, h]
            for j in range(bits_of(chunks)):
                if c >> j & 1:
                    row = lam_ref[tile_bits + 1 + j : tile_bits + 2 + j, span]
                    first = (c >> j ^ 1) << j
                    sources = range(first, first + (1 << j))
                    dqt = dqt + row * dot_nt(level_ref[groups.index(sources), h], grad)
                    part = dot(scaled(row, query_t), grad)
                    for i in sources:
                        gin_ref[i, h] = gin_ref[i, h] + part
            dq_ref[c, h] = dqt.astype(BF16).T


def pair_kernel(levels, state_ref, other_state_ref, keep_ref, found_ref, *out_refs):
    heads = state_ref.shape[0]
    half = heads // 2
    start = bit_of_block(0) * half
    for b, out_ref in zip(levels, out_refs):
        for on in range(2):

            @pl.when(bit_of_block(b) == on)
            def _():
                for i in range(half):
                    if on:
                        spot = (b - 1) * half + i
                        out_ref[i] = keep_ref[spot] + found_ref[heads + spot]
                    else:
                        out_ref[i] = state_ref[start + i] + other_state_ref[start + i]


def sum_kernel(levels, *refs):
    out_ref = refs[-1]
    for n in range(out_ref.shape[0]):
        for i in range(out_ref.shape[1]):
            parts = [ref[i] for b, ref in zip(levels, refs) if b == n + 1]
            out_ref[n, i] = functools.reduce(jnp.add, parts)


def widen(lam_ref, first_row, lanes, wide_ref):
    for b in range(wide_ref.shape[0]):
        row = lam_ref[first_row + b : first_row + b + 1, lanes]
        wide_ref[b] = jnp.broadcast_to(row, wide_ref.shape[:0:-1]).T


def received(sums_ref, i):
    parts = [sums_ref[b, i] for b in range(sums_ref.shape[0])]
    off = [(1 - bit_of_block(b + 1)).astype(F32) for b in range(len(parts))]
    state = functools.reduce(jnp.add, [w * part for w, part in zip(off, parts)])
    return stack_levels([part.astype(BF16) for part in parts], 0), state


def add_to_query(half, wide_ref, grad, dq):
    width = grad.shape[1]
    dq = dq.astype(F32)
    projected = dot_nt(grad, half)
    for b in range(wide_ref.shape[0]):
        dq = dq + wide_ref[b] * projected[:, b * width : (b + 1) * width]
    return dq.astype(BF16)


def add_to_key_value(state, key, value, dk, dv):
    width = key.shape[1]
    state = state.astype(BF16)
    none = jnp.zeros((width, width), BF16)
    right = jnp.concatenate(
        [
            jnp.concatenate([state.T, none], axis=1),
            jnp.concatenate([none, state], axis=1),
        ],
        axis=0,
    )
    product = dot(jnp.concatenate([value, key], axis=1), right)
    dk = dk.astype(F32) + product[:, :width]
    dv = dv.astype(F32) + product[:, width:]
    return dk.astype(BF16), dv.astype(BF16)


def own_half_kernel(
    first_row, lam_ref, k_ref, v_ref, g_ref, gin_ref, sums_ref, dq_in, dk_in, dv_in,
    dq_ref, dk_ref, dv_ref, wide_ref, half_ref, state_ref,
):
    chunks, _, tile, _ = k_ref.shape
    half = half_ref.shape[0]
    start = bit_of_block(0) * half
    for i in range(half):
        half_ref[i], state_ref[i] = received(sums_ref, i)
    for c in range(chunks):
        widen(lam_ref, first_row, slice(c * tile, (c + 1) * tile), wide_ref)
        for i in range(half):
            h = start + i
            dq_ref[c, h] = add_to_query(half_ref[i], wide_ref, g_ref[c, h], dq_in[c, h])
            dk_ref[c, h], dv_ref[c, h] = add_to_key_value(
                gin_ref[c, h] + state_ref[i], k_ref[c, h], v_ref[c, h], dk_in[c, h], dv_in[c, h]
            )


def final_kernel(
    first_row, lam_ref, k_ref, v_ref, g_ref, dq_in, dk_in, dv_in, gin_ref, sums_ref,
    dq_out, dk_out, dv_out, done_ref, wide_ref, half_ref, state_ref, sems,
):
    chunks, heads, tile, _ = k_ref.shape
    half = half_ref.shape[0]
    outs = (dq_out, dk_out, dv_out)

    def ship(n, c):
        place = pl.ds(c * tile, tile)
        return pltpu.make_async_copy(done_ref.at[n, c], outs[n].at[place], sems.at[n, c])

    for i in range(half):
        half_ref[i], state_ref[i] = received(sums_ref, i)
    for core in range(2):

        @pl.when(bit_of_block(0) == core)
        def _():
            for c in range(chunks):
                widen(lam_ref, first_row, slice(c * tile, (c + 1) * tile), wide_ref)
                queries, keys, values = [], [], []
                for h in range(heads):
                    query, key, value = dq_in[c, h], dk_in[c, h], dv_in[c, h]
                    if h // half != core:
                        i = h % half
                        query = add_to_query(half_ref[i], wide_ref, g_ref[c, h], query)
                        key, value = add_to_key_value(
                            gin_ref[c, h] + state_ref[i], k_ref[c, h], v_ref[c, h], key, value
                        )
                    queries.append(query)
                    keys.append(key)
                    values.append(value)
                for n, parts in enumerate((queries, keys, values)):
                    done_ref[n, c] = jnp.swapaxes(jnp.stack(parts), 0, 1)
                    ship(n, c).start()

    for c in range(chunks):
        for n in range(3):
            ship(n, c).wait()


def shape(dims, dtype):
    return jax.ShapeDtypeStruct(dims, dtype)


def params(limit):
    return pltpu.CompilerParams(vmem_limit_bytes=limit * MIB)


def cost(flops, size):
    return pl.CostEstimate(flops=int(flops), bytes_accessed=int(size), transcendentals=0)


def on_device(queries, keys, values, out_grad, level_codes):
    count, heads, width = queries.shape
    scale = width ** (-0.5)
    local_bits = bits_of(count)
    blocks = lax.axis_size("seq")
    tree_bits = bits_of(blocks)
    groups = lax.axis_size("head")
    here = lax.axis_index("seq")
    tile = min(256, count)
    chunks = count // tile
    half = heads // 2
    rows = local_bits + 1 + tree_bits

    def permute(x, apart):
        return lax.ppermute(x, "seq", [(i, i ^ apart) for i in range(blocks)])

    def in_hbm(*arrays):
        return [pltpu.with_memory_space_constraint(x, pltpu.HBM) for x in arrays]

    def near(*arrays):
        return [pltpu.with_memory_space_constraint(x, pltpu.VMEM) for x in arrays]

    token_block = pl.BlockSpec((tile, heads, width), lambda c: (c, 0, 0))
    in_vmem = pl.BlockSpec(memory_space=pltpu.VMEM)
    anywhere = pl.BlockSpec(memory_space=pl.ANY)

    def chunk_block(*dims):
        return pl.BlockSpec((1,) + dims, lambda c: (c,) + (0,) * len(dims))

    def whole(*dims):
        return pl.BlockSpec(dims, lambda c: (0,) * len(dims))

    head_block = chunk_block(heads, tile, width)
    natural = pltpu.VMEM((chunks, heads, tile, width), BF16)
    square = (width, width)
    size = count * heads * width
    groups_in = len(level_sources(chunks))
    queries, keys, values, out_grad = in_hbm(queries, keys, values, out_grad)

    kh, vh, qh, gh, qt, level_state, state = near(
        *pl.pallas_call(
            states_kernel,
            grid=(chunks,),
            in_specs=[token_block] * 4,
            out_specs=[
                *[head_block] * 4, chunk_block(heads, width, tile),
                whole(groups_in, heads, *square), whole(heads, *square),
            ],
            out_shape=[
                *[natural] * 4, pltpu.VMEM((chunks, heads, width, tile), BF16),
                pltpu.VMEM((groups_in, heads, *square), BF16), pltpu.VMEM((heads, *square), F32),
            ],
            scratch_shapes=[pltpu.VMEM((chunks, heads, *square), F32)],
            compiler_params=params(10),
            cost_estimate=cost(2 * size * width, 8 * size),
            name="states",
        )(keys, values, queries, out_grad)
    )
    other_state = permute(state, 1)

    codes = jnp.broadcast_to(level_codes, (groups, *level_codes.shape))
    codes = lax.all_to_all(codes, "head", 0, 0)
    codes, qt = lax.optimization_barrier((codes, qt))
    (qt,) = near(qt)
    codes = jnp.concatenate([codes[j, :rows] for j in range(groups)], axis=1)
    order = jnp.arange(rows)
    factor = jnp.exp2(-0.5 * jnp.maximum(order.astype(F32) - 1.0, 0.0)) / 16.0
    on_bit = jnp.bitwise_and(jnp.right_shift(here, jnp.maximum(order - local_bits - 1, 0)), 1)
    factor = jnp.where(order > local_bits, factor * on_bit.astype(F32), factor)
    lam = codes.astype(F32) * (scale * factor)[:, None]

    wide = (tree_bits - 1) * half
    send, keep = pl.pallas_call(
        functools.partial(grads_kernel, local_bits + 1),
        in_specs=[in_vmem] * 3,
        out_specs=[in_vmem] * 2,
        out_shape=[
            pltpu.VMEM((heads + wide, *square), F32), pltpu.VMEM((wide, *square), F32),
        ],
        compiler_params=params(8),
        cost_estimate=cost(2 * tree_bits * size * width, 8 * size),
        name="level_grads",
    )(lam, qt, gh)
    send, other_state = lax.optimization_barrier((send, other_state))
    found = permute(send, 1)
    (keep,) = near(keep)

    dqt, *parts = pl.pallas_call(
        first_tile_kernel,
        in_specs=[in_vmem] * 5,
        out_specs=[in_vmem] * 4,
        out_shape=[pltpu.VMEM((heads, width, tile), F32)] + [natural] * 3,
        scratch_shapes=[pltpu.VMEM((tile, tile), F32)],
        compiler_params=params(6),
        cost_estimate=cost(14 * size * tile / chunks, 4 * size),
        name="first_tile",
    )(lam, kh, vh, qh, gh)
    hops = [1 << b | m for b in range(1, tree_bits) for m in range(0, 1 << b, 2)]
    hops.sort(key=lambda hop: (hop & hop - 1) == 0)
    messages = pl.pallas_call(
        functools.partial(pair_kernel, [bits_of(hop) for hop in hops]),
        in_specs=[in_vmem] * 4,
        out_specs=[in_vmem] * len(hops),
        out_shape=[pltpu.VMEM((half, *square), F32)] * len(hops),
        compiler_params=params(4),
        cost_estimate=cost(size, size),
        name="pair",
    )(state, other_state, keep, found)
    *messages, parts = lax.optimization_barrier((*messages, parts))
    arrived = [permute(x, hop) for hop, x in zip(hops, messages)]
    *parts, gin = pl.pallas_call(
        local_kernel,
        in_specs=[in_vmem] * 10 + [anywhere] * 3,
        out_specs=[in_vmem] * 4,
        out_shape=[natural] * 3 + [pltpu.VMEM((chunks, heads, *square), F32)],
        input_output_aliases={10: 0, 11: 1, 12: 2},
        scratch_shapes=[pltpu.VMEM((tile, tile), F32), pltpu.VMEM((heads, *square), BF16)],
        compiler_params=params(6),
        cost_estimate=cost(14 * size * tile, 4 * size),
        name="local",
    )(lam, kh, vh, qh, gh, qt, level_state, other_state, found, *near(dqt, *parts))
    arrived, parts = lax.optimization_barrier((arrived, parts))
    sums_shape = (tree_bits - 1, half, *square)
    mine = pl.pallas_call(
        functools.partial(sum_kernel, [bits_of(hop) for hop in hops]),
        in_specs=[in_vmem] * len(hops),
        out_specs=in_vmem,
        out_shape=pltpu.VMEM(sums_shape, F32),
        compiler_params=params(6),
        cost_estimate=cost(size, size),
        name="sums",
    )(*arrived)
    others = permute(mine, 1)

    kept = [
        pltpu.VMEM((tree_bits - 1, tile, width), F32),
        pltpu.VMEM((half, (tree_bits - 1) * width, width), BF16),
        pltpu.VMEM((half, *square), F32),
    ]
    gin, mine = near(gin, mine)
    parts = pl.pallas_call(
        functools.partial(own_half_kernel, local_bits + 2),
        in_specs=[in_vmem] * 9,
        out_specs=[in_vmem] * 3,
        out_shape=[natural] * 3,
        input_output_aliases={6: 0, 7: 1, 8: 2},
        scratch_shapes=kept,
        compiler_params=params(6),
        cost_estimate=cost((tree_bits + 2) * size * width, 8 * size),
        name="own_half",
    )(lam, kh, vh, gh, gin, mine, *near(*parts))
    others, parts = lax.optimization_barrier((others, parts))
    return pl.pallas_call(
        functools.partial(final_kernel, local_bits + 2),
        in_specs=[in_vmem] * 9,
        out_specs=[anywhere] * 3,
        out_shape=[pltpu.HBM((count, heads, width), BF16)] * 3,
        scratch_shapes=[
            pltpu.VMEM((3, chunks, tile, heads, width), BF16), *kept,
            pltpu.SemaphoreType.DMA((3, chunks)),
        ],
        compiler_params=params(12),
        cost_estimate=cost((tree_bits + 2) * size * width, 16 * size),
        name="final",
    )(lam, kh, vh, gh, *near(*parts), gin, others)


def solution(mesh):
    tokens = P("seq", "head", None)
    return jax.shard_map(
        on_device,
        mesh=mesh,
        in_specs=(tokens, tokens, tokens, tokens, P(None, ("seq", "head"))),
        out_specs=(tokens, tokens, tokens),
        check_vma=False,
    )
```

```python
import functools

import jax
import jax.numpy as jnp
from jax import lax
from jax.experimental import pallas as pl
from jax.experimental.pallas import tpu as pltpu
from jax.sharding import PartitionSpec as P

F32 = jnp.float32
BF16 = jnp.bfloat16
MIB = 1 << 20


def bits_of(size):
    return size.bit_length() - 1


def dot(a, b):
    return jnp.dot(a, b, preferred_element_type=F32)


def dot_nt(a, b):
    return lax.dot_general(a, b, (((1,), (1,)), ((), ())), preferred_element_type=F32)


def scaled(row, x):
    return (row * x.astype(F32)).astype(BF16)


def stack_levels(parts, axis):
    return parts[0] if len(parts) == 1 else jnp.concatenate(parts, axis=axis)


def level_sources(chunks):
    found = []
    for j in range(bits_of(chunks)):
        for first in range(0, chunks, 2 << j):
            found.append(range(first, first + (1 << j)))
    return found


def bit_of_block(b):
    return jnp.bitwise_and(jnp.right_shift(lax.axis_index("seq"), b), 1)


def states_kernel(
    k_ref, v_ref, q_ref, g_ref,
    kh_ref, vh_ref, qh_ref, gh_ref, qt_ref, level_ref, total_ref, chunk_ref,
):
    heads = k_ref.shape[1]
    chunks = chunk_ref.shape[0]
    step = pl.program_id(0)
    kh_ref[0] = jnp.swapaxes(k_ref[...], 0, 1)
    vh_ref[0] = jnp.swapaxes(v_ref[...], 0, 1)
    qh_ref[0] = jnp.swapaxes(q_ref[...], 0, 1)
    gh_ref[0] = jnp.swapaxes(g_ref[...], 0, 1)
    for h in range(heads):
        chunk_ref[step, h] = dot(kh_ref[0, h].T, vh_ref[0, h])
        qt_ref[0, h] = qh_ref[0, h].T

    @pl.when(step == chunks - 1)
    def _():
        for h in range(heads):
            tiles = [chunk_ref[i, h] for i in range(chunks)]
            total_ref[h] = functools.reduce(jnp.add, tiles)
            for n, sources in enumerate(level_sources(chunks)):
                state = functools.reduce(jnp.add, [tiles[i] for i in sources])
                level_ref[n, h] = state.astype(BF16)


def grads_kernel(first_row, lam_ref, qt_ref, g_ref, send_ref, keep_ref):
    chunks, heads, tile, width = g_ref.shape
    half = heads // 2
    levels = lam_ref.shape[0] - first_row

    for core in range(2):

        @pl.when(bit_of_block(0) == core)
        def _():
            for h in range(heads):
                weighted = [
                    stack_levels(
                        [
                            scaled(
                                lam_ref[first_row + b : first_row + b + 1, c * tile : (c + 1) * tile],
                                qt_ref[c, h],
                            )
                            for b in range(levels)
                        ],
                        0,
                    )
                    for c in range(chunks)
                ]
                grad = dot(stack_levels(weighted, 1), g_ref[:, h].reshape(chunks * tile, width))
                send_ref[h] = grad[:width]
                for b in range(1, levels):
                    part = grad[b * width : (b + 1) * width]
                    spot = (b - 1) * half + h % half
                    if h // half == core:
                        keep_ref[spot] = part
                    else:
                        send_ref[heads + spot] = part


def make_mask(lam_ref, span, mask_ref):
    tile = mask_ref.shape[0]
    part = min(128, tile)
    source = lax.broadcasted_iota(jnp.int32, (part, part), 0)
    target = lax.broadcasted_iota(jnp.int32, (part, part), 1)
    differ = jnp.where(source <= target, jnp.bitwise_xor(source, target), -1)
    for to in range(0, tile, part):
        lanes = slice(span.start + to, span.start + to + part)
        mask = jnp.where(differ >= 0, lam_ref[0:1, lanes], 0.0)
        for power in range(bits_of(part)):
            mask = jnp.where(differ >= 1 << power, lam_ref[power + 1 : power + 2, lanes], mask)
        mask_ref[to : to + part, to : to + part] = mask
        for at in range(0, tile, part):
            if at < to:
                level = bits_of(at ^ to) + 1
                row = lam_ref[level : level + 1, lanes]
                mask_ref[at : at + part, to : to + part] = jnp.broadcast_to(row, (part, part))
            elif at > to:
                mask_ref[at : at + part, to : to + part] = jnp.zeros((part, part), F32)


def diagonal_tile(key, value, query, grad, mask):
    weight_q = (mask * dot_nt(value, grad)).astype(BF16)
    weight_v = (mask * dot_nt(key, query)).astype(BF16)
    dk = dot(weight_q, query).astype(BF16)
    dv = dot(weight_v, grad).astype(BF16)
    return dot(key.T, weight_q), dk, dv


def first_tile_kernel(
    lam_ref, k_ref, v_ref, q_ref, g_ref, dqt_ref, dq_ref, dk_ref, dv_ref, mask_ref
):
    del dq_ref
    make_mask(lam_ref, slice(0, mask_ref.shape[0]), mask_ref)

    @pl.loop(0, k_ref.shape[1], unroll=4)
    def _(h):
        dqt_ref[h], dk_ref[0, h], dv_ref[0, h] = diagonal_tile(
            k_ref[0, h], v_ref[0, h], q_ref[0, h], g_ref[0, h], mask_ref[...]
        )


def local_kernel(
    lam_ref, k_ref, v_ref, q_ref, g_ref, qt_ref, level_ref, state_ref, grad_ref, dqt_ref,
    dq_in, dk_in, dv_in,
    dq_ref, dk_ref, dv_ref, gin_ref, mask_ref, half_ref,
):
    del dq_in, dk_in, dv_in
    chunks, heads, tile, width = k_ref.shape
    tile_bits = bits_of(tile)
    first_row = tile_bits + bits_of(chunks) + 1
    groups = level_sources(chunks)
    off = (1 - bit_of_block(0)).astype(F32)

    @pl.loop(0, heads, unroll=4)
    def _(h):
        half_ref[h] = state_ref[h].astype(BF16)
        for i in range(chunks):
            gin_ref[i, h] = off * grad_ref[h]
        row = lam_ref[first_row : first_row + 1, :tile]
        dqt = dqt_ref[h] + row * dot_nt(half_ref[h], g_ref[0, h])
        dq_ref[0, h] = dqt.astype(BF16).T

    for c in range(1, chunks):
        span = slice(c * tile, (c + 1) * tile)
        make_mask(lam_ref, span, mask_ref)

        @pl.loop(0, heads, unroll=4)
        def _(h):
            query, grad = q_ref[c, h], g_ref[c, h]
            dqt, dk_ref[c, h], dv_ref[c, h] = diagonal_tile(
                k_ref[c, h], v_ref[c, h], query, grad, mask_ref[...]
            )
            dqt = dqt + lam_ref[first_row : first_row + 1, span] * dot_nt(half_ref[h], grad)
            query_t = qt_ref[c, h]
            for j in range(bits_of(chunks)):
                if c >> j & 1:
                    row = lam_ref[tile_bits + 1 + j : tile_bits + 2 + j, span]
                    first = (c >> j ^ 1) << j
                    sources = range(first, first + (1 << j))
                    dqt = dqt + row * dot_nt(level_ref[groups.index(sources), h], grad)
                    part = dot(scaled(row, query_t), grad)
                    for i in sources:
                        gin_ref[i, h] = gin_ref[i, h] + part
            dq_ref[c, h] = dqt.astype(BF16).T


def pair_kernel(levels, state_ref, other_state_ref, keep_ref, found_ref, *out_refs):
    heads = state_ref.shape[0]
    half = heads // 2
    start = bit_of_block(0) * half
    for b, out_ref in zip(levels, out_refs):
        for on in range(2):

            @pl.when(bit_of_block(b) == on)
            def _():
                for i in range(half):
                    if on:
                        spot = (b - 1) * half + i
                        out_ref[i] = keep_ref[spot] + found_ref[heads + spot]
                    else:
                        out_ref[i] = state_ref[start + i] + other_state_ref[start + i]


def sum_kernel(levels, *refs):
    out_ref = refs[-1]
    for n in range(out_ref.shape[0]):
        for i in range(out_ref.shape[1]):
            parts = [ref[i] for b, ref in zip(levels, refs) if b == n + 1]
            out_ref[n, i] = functools.reduce(jnp.add, parts)


def widen(lam_ref, first_row, lanes, wide_ref):
    for b in range(wide_ref.shape[0]):
        row = lam_ref[first_row + b : first_row + b + 1, lanes]
        wide_ref[b] = jnp.broadcast_to(row, wide_ref.shape[:0:-1]).T


def received(sums_ref, i):
    parts = [sums_ref[b, i] for b in range(sums_ref.shape[0])]
    off = [(1 - bit_of_block(b + 1)).astype(F32) for b in range(len(parts))]
    state = functools.reduce(jnp.add, [w * part for w, part in zip(off, parts)])
    return stack_levels([part.astype(BF16) for part in parts], 0), state


def add_to_query(half, wide_ref, grad, dq):
    width = grad.shape[1]
    dq = dq.astype(F32)
    projected = dot_nt(grad, half)
    for b in range(wide_ref.shape[0]):
        dq = dq + wide_ref[b] * projected[:, b * width : (b + 1) * width]
    return dq.astype(BF16)


def add_to_key_value(state, key, value, dk, dv):
    width = key.shape[1]
    state = state.astype(BF16)
    none = jnp.zeros((width, width), BF16)
    right = jnp.concatenate(
        [
            jnp.concatenate([state.T, none], axis=1),
            jnp.concatenate([none, state], axis=1),
        ],
        axis=0,
    )
    product = dot(jnp.concatenate([value, key], axis=1), right)
    dk = dk.astype(F32) + product[:, :width]
    dv = dv.astype(F32) + product[:, width:]
    return dk.astype(BF16), dv.astype(BF16)


def own_half_kernel(
    first_row, lam_ref, k_ref, v_ref, g_ref, gin_ref, sums_ref, dq_in, dk_in, dv_in,
    dq_ref, dk_ref, dv_ref, wide_ref, half_ref, state_ref,
):
    chunks, _, tile, _ = k_ref.shape
    half = half_ref.shape[0]
    start = bit_of_block(0) * half
    for i in range(half):
        half_ref[i], state_ref[i] = received(sums_ref, i)
    for c in range(chunks):
        widen(lam_ref, first_row, slice(c * tile, (c + 1) * tile), wide_ref)
        for i in range(half):
            h = start + i
            dq_ref[c, h] = add_to_query(half_ref[i], wide_ref, g_ref[c, h], dq_in[c, h])
            dk_ref[c, h], dv_ref[c, h] = add_to_key_value(
                gin_ref[c, h] + state_ref[i], k_ref[c, h], v_ref[c, h], dk_in[c, h], dv_in[c, h]
            )


def final_kernel(
    first_row, lam_ref, k_ref, v_ref, g_ref, dq_in, dk_in, dv_in, gin_ref, sums_ref,
    dq_out, dk_out, dv_out, done_ref, wide_ref, half_ref, state_ref, sems,
):
    chunks, heads, tile, _ = k_ref.shape
    half = half_ref.shape[0]
    outs = (dq_out, dk_out, dv_out)

    def ship(n, c):
        place = pl.ds(c * tile, tile)
        return pltpu.make_async_copy(done_ref.at[n, c], outs[n].at[place], sems.at[n, c])

    for i in range(half):
        half_ref[i], state_ref[i] = received(sums_ref, i)
    for core in range(2):

        @pl.when(bit_of_block(0) == core)
        def _():
            for c in range(chunks):
                widen(lam_ref, first_row, slice(c * tile, (c + 1) * tile), wide_ref)
                queries, keys, values = [], [], []
                for h in range(heads):
                    query, key, value = dq_in[c, h], dk_in[c, h], dv_in[c, h]
                    if h // half != core:
                        i = h % half
                        query = add_to_query(half_ref[i], wide_ref, g_ref[c, h], query)
                        key, value = add_to_key_value(
                            gin_ref[c, h] + state_ref[i], k_ref[c, h], v_ref[c, h], key, value
                        )
                    queries.append(query)
                    keys.append(key)
                    values.append(value)
                for n, parts in enumerate((queries, keys, values)):
                    done_ref[n, c] = jnp.swapaxes(jnp.stack(parts), 0, 1)
                    ship(n, c).start()

    for c in range(chunks):
        for n in range(3):
            ship(n, c).wait()


def shape(dims, dtype):
    return jax.ShapeDtypeStruct(dims, dtype)


def params(limit):
    return pltpu.CompilerParams(vmem_limit_bytes=limit * MIB)


def cost(flops, size):
    return pl.CostEstimate(flops=int(flops), bytes_accessed=int(size), transcendentals=0)


def on_device(queries, keys, values, out_grad, level_codes):
    count, heads, width = queries.shape
    scale = width ** (-0.5)
    local_bits = bits_of(count)
    blocks = lax.axis_size("seq")
    tree_bits = bits_of(blocks)
    groups = lax.axis_size("head")
    here = lax.axis_index("seq")
    tile = min(256, count)
    chunks = count // tile
    half = heads // 2
    rows = local_bits + 1 + tree_bits

    def permute(x, apart):
        return lax.ppermute(x, "seq", [(i, i ^ apart) for i in range(blocks)])

    def in_hbm(*arrays):
        return [pltpu.with_memory_space_constraint(x, pltpu.HBM) for x in arrays]

    def near(*arrays):
        return [pltpu.with_memory_space_constraint(x, pltpu.VMEM) for x in arrays]

    token_block = pl.BlockSpec((tile, heads, width), lambda c: (c, 0, 0))
    in_vmem = pl.BlockSpec(memory_space=pltpu.VMEM)
    anywhere = pl.BlockSpec(memory_space=pl.ANY)

    def chunk_block(*dims):
        return pl.BlockSpec((1,) + dims, lambda c: (c,) + (0,) * len(dims))

    def whole(*dims):
        return pl.BlockSpec(dims, lambda c: (0,) * len(dims))

    head_block = chunk_block(heads, tile, width)
    natural = pltpu.VMEM((chunks, heads, tile, width), BF16)
    square = (width, width)
    size = count * heads * width
    groups_in = len(level_sources(chunks))
    queries, keys, values, out_grad = in_hbm(queries, keys, values, out_grad)

    kh, vh, qh, gh, qt, level_state, state = near(
        *pl.pallas_call(
            states_kernel,
            grid=(chunks,),
            in_specs=[token_block] * 4,
            out_specs=[
                *[head_block] * 4, chunk_block(heads, width, tile),
                whole(groups_in, heads, *square), whole(heads, *square),
            ],
            out_shape=[
                *[natural] * 4, pltpu.VMEM((chunks, heads, width, tile), BF16),
                pltpu.VMEM((groups_in, heads, *square), BF16), pltpu.VMEM((heads, *square), F32),
            ],
            scratch_shapes=[pltpu.VMEM((chunks, heads, *square), F32)],
            compiler_params=params(10),
            cost_estimate=cost(2 * size * width, 8 * size),
            name="states",
        )(keys, values, queries, out_grad)
    )
    other_state = permute(state, 1)

    group = lax.axis_index("head")
    pieces = [
        lax.ppermute(level_codes, "head", [(i, (i + r) % groups) for i in range(groups)])
        for r in range(1, groups)
    ]
    pieces, state = lax.optimization_barrier((pieces, state))
    (state,) = near(state)
    pieces = jnp.stack([level_codes, *pieces])
    codes = jnp.concatenate(
        [
            lax.dynamic_index_in_dim(pieces, (group - j) % groups, 0, keepdims=False)[:rows]
            for j in range(groups)
        ],
        axis=1,
    )
    order = jnp.arange(rows)
    factor = jnp.exp2(-0.5 * jnp.maximum(order.astype(F32) - 1.0, 0.0)) / 16.0
    on_bit = jnp.bitwise_and(jnp.right_shift(here, jnp.maximum(order - local_bits - 1, 0)), 1)
    factor = jnp.where(order > local_bits, factor * on_bit.astype(F32), factor)
    lam = codes.astype(F32) * (scale * factor)[:, None]

    wide = (tree_bits - 1) * half
    send, keep = pl.pallas_call(
        functools.partial(grads_kernel, local_bits + 1),
        in_specs=[in_vmem] * 3,
        out_specs=[in_vmem] * 2,
        out_shape=[
            pltpu.VMEM((heads + wide, *square), F32), pltpu.VMEM((wide, *square), F32),
        ],
        compiler_params=params(8),
        cost_estimate=cost(2 * tree_bits * size * width, 8 * size),
        name="level_grads",
    )(lam, qt, gh)
    send, other_state = lax.optimization_barrier((send, other_state))
    found = permute(send, 1)
    (keep,) = near(keep)

    dqt, *parts = pl.pallas_call(
        first_tile_kernel,
        in_specs=[in_vmem] * 5,
        out_specs=[in_vmem] * 4,
        out_shape=[pltpu.VMEM((heads, width, tile), F32)] + [natural] * 3,
        scratch_shapes=[pltpu.VMEM((tile, tile), F32)],
        compiler_params=params(6),
        cost_estimate=cost(14 * size * tile / chunks, 4 * size),
        name="first_tile",
    )(lam, kh, vh, qh, gh)
    hops = [1 << b | m for b in range(1, tree_bits) for m in range(0, 1 << b, 2)]
    hops.sort(key=lambda hop: (hop & hop - 1) == 0)
    messages = pl.pallas_call(
        functools.partial(pair_kernel, [bits_of(hop) for hop in hops]),
        in_specs=[in_vmem] * 4,
        out_specs=[in_vmem] * len(hops),
        out_shape=[pltpu.VMEM((half, *square), F32)] * len(hops),
        compiler_params=params(4),
        cost_estimate=cost(size, size),
        name="pair",
    )(state, other_state, keep, found)
    *messages, parts = lax.optimization_barrier((*messages, parts))
    arrived = [permute(x, hop) for hop, x in zip(hops, messages)]
    *parts, gin = pl.pallas_call(
        local_kernel,
        in_specs=[in_vmem] * 10 + [anywhere] * 3,
        out_specs=[in_vmem] * 4,
        out_shape=[natural] * 3 + [pltpu.VMEM((chunks, heads, *square), F32)],
        input_output_aliases={10: 0, 11: 1, 12: 2},
        scratch_shapes=[pltpu.VMEM((tile, tile), F32), pltpu.VMEM((heads, *square), BF16)],
        compiler_params=params(6),
        cost_estimate=cost(14 * size * tile, 4 * size),
        name="local",
    )(lam, kh, vh, qh, gh, qt, level_state, other_state, found, *near(dqt, *parts))
    arrived, parts = lax.optimization_barrier((arrived, parts))
    sums_shape = (tree_bits - 1, half, *square)
    mine = pl.pallas_call(
        functools.partial(sum_kernel, [bits_of(hop) for hop in hops]),
        in_specs=[in_vmem] * len(hops),
        out_specs=in_vmem,
        out_shape=pltpu.VMEM(sums_shape, F32),
        compiler_params=params(6),
        cost_estimate=cost(size, size),
        name="sums",
    )(*arrived)
    others = permute(mine, 1)

    kept = [
        pltpu.VMEM((tree_bits - 1, tile, width), F32),
        pltpu.VMEM((half, (tree_bits - 1) * width, width), BF16),
        pltpu.VMEM((half, *square), F32),
    ]
    gin, mine = near(gin, mine)
    parts = pl.pallas_call(
        functools.partial(own_half_kernel, local_bits + 2),
        in_specs=[in_vmem] * 9,
        out_specs=[in_vmem] * 3,
        out_shape=[natural] * 3,
        input_output_aliases={6: 0, 7: 1, 8: 2},
        scratch_shapes=kept,
        compiler_params=params(6),
        cost_estimate=cost((tree_bits + 2) * size * width, 8 * size),
        name="own_half",
    )(lam, kh, vh, gh, gin, mine, *near(*parts))
    others, parts = lax.optimization_barrier((others, parts))
    return pl.pallas_call(
        functools.partial(final_kernel, local_bits + 2),
        in_specs=[in_vmem] * 9,
        out_specs=[anywhere] * 3,
        out_shape=[pltpu.HBM((count, heads, width), BF16)] * 3,
        scratch_shapes=[
            pltpu.VMEM((3, chunks, tile, heads, width), BF16), *kept,
            pltpu.SemaphoreType.DMA((3, chunks)),
        ],
        compiler_params=params(12),
        cost_estimate=cost((tree_bits + 2) * size * width, 16 * size),
        name="final",
    )(lam, kh, vh, gh, *near(*parts), gin, others)


def solution(mesh):
    tokens = P("seq", "head", None)
    return jax.shard_map(
        on_device,
        mesh=mesh,
        in_specs=(tokens, tokens, tokens, tokens, P(None, ("seq", "head"))),
        out_specs=(tokens, tokens, tokens),
        check_vma=False,
    )
```

```python
import functools

import jax
import jax.numpy as jnp
from jax import lax
from jax.experimental import pallas as pl
from jax.experimental.pallas import tpu as pltpu
from jax.sharding import PartitionSpec as P

F32 = jnp.float32
BF16 = jnp.bfloat16
MIB = 1 << 20


def bits_of(size):
    return size.bit_length() - 1


def dot(a, b):
    return jnp.dot(a, b, preferred_element_type=F32)


def dot_nt(a, b):
    return lax.dot_general(a, b, (((1,), (1,)), ((), ())), preferred_element_type=F32)


def scaled(row, x):
    return (row * x.astype(F32)).astype(BF16)


def stack_levels(parts, axis):
    return parts[0] if len(parts) == 1 else jnp.concatenate(parts, axis=axis)


def level_sources(chunks):
    found = []
    for j in range(bits_of(chunks)):
        for first in range(0, chunks, 2 << j):
            found.append(range(first, first + (1 << j)))
    return found


def bit_of_block(b):
    return jnp.bitwise_and(jnp.right_shift(lax.axis_index("seq"), b), 1)


def states_kernel(
    k_ref, v_ref, q_ref, g_ref,
    kh_ref, vh_ref, gh_ref, qt_ref, level_ref, total_ref, chunk_ref,
):
    heads = k_ref.shape[1]
    chunks = chunk_ref.shape[0]
    step = pl.program_id(0)
    kh_ref[0] = jnp.swapaxes(k_ref[...], 0, 1)
    vh_ref[0] = jnp.swapaxes(v_ref[...], 0, 1)
    queries = jnp.swapaxes(q_ref[...], 0, 1)
    gh_ref[0] = jnp.swapaxes(g_ref[...], 0, 1)
    for h in range(heads):
        chunk_ref[step, h] = dot(kh_ref[0, h].T, vh_ref[0, h])
        qt_ref[0, h] = queries[h].T

    @pl.when(step == chunks - 1)
    def _():
        for h in range(heads):
            tiles = [chunk_ref[i, h] for i in range(chunks)]
            total_ref[h] = functools.reduce(jnp.add, tiles)
            for n, sources in enumerate(level_sources(chunks)):
                state = functools.reduce(jnp.add, [tiles[i] for i in sources])
                level_ref[n, h] = state.astype(BF16)


def grads_kernel(first_row, lam_ref, qt_ref, g_ref, send_ref, keep_ref):
    chunks, heads, tile, width = g_ref.shape
    half = heads // 2
    levels = lam_ref.shape[0] - first_row

    for core in range(2):

        @pl.when(bit_of_block(0) == core)
        def _():
            for h in range(heads):
                weighted = [
                    stack_levels(
                        [
                            scaled(
                                lam_ref[first_row + b : first_row + b + 1, c * tile : (c + 1) * tile],
                                qt_ref[c, h],
                            )
                            for b in range(levels)
                        ],
                        0,
                    )
                    for c in range(chunks)
                ]
                grad = dot(stack_levels(weighted, 1), g_ref[:, h].reshape(chunks * tile, width))
                send_ref[h] = grad[:width]
                for b in range(1, levels):
                    part = grad[b * width : (b + 1) * width]
                    spot = (b - 1) * half + h % half
                    if h // half == core:
                        keep_ref[spot] = part
                    else:
                        send_ref[heads + spot] = part


def make_mask(lam_ref, span, mask_ref):
    tile = mask_ref.shape[0]
    part = min(128, tile)
    source = lax.broadcasted_iota(jnp.int32, (part, part), 0)
    target = lax.broadcasted_iota(jnp.int32, (part, part), 1)
    differ = jnp.where(source <= target, jnp.bitwise_xor(source, target), -1)
    for to in range(0, tile, part):
        lanes = slice(span.start + to, span.start + to + part)
        mask = jnp.where(differ >= 0, lam_ref[0:1, lanes], 0.0)
        for power in range(bits_of(part)):
            mask = jnp.where(differ >= 1 << power, lam_ref[power + 1 : power + 2, lanes], mask)
        mask_ref[to : to + part, to : to + part] = mask
        for at in range(0, tile, part):
            if at < to:
                level = bits_of(at ^ to) + 1
                row = lam_ref[level : level + 1, lanes]
                mask_ref[at : at + part, to : to + part] = jnp.broadcast_to(row, (part, part))
            elif at > to:
                mask_ref[at : at + part, to : to + part] = jnp.zeros((part, part), F32)


def diagonal_tile(key, value, query_t, grad, mask):
    weight_q = (mask * dot_nt(value, grad)).astype(BF16)
    weight_v = (mask * dot(key, query_t)).astype(BF16)
    dk = dot_nt(weight_q, query_t).astype(BF16)
    dv = dot(weight_v, grad).astype(BF16)
    return dot(key.T, weight_q), dk, dv


def first_tile_kernel(
    lam_ref, k_ref, v_ref, qt_ref, g_ref, dqt_ref, dq_ref, dk_ref, dv_ref, mask_ref
):
    del dq_ref
    make_mask(lam_ref, slice(0, mask_ref.shape[0]), mask_ref)

    @pl.loop(0, k_ref.shape[1], unroll=4)
    def _(h):
        dqt_ref[h], dk_ref[0, h], dv_ref[0, h] = diagonal_tile(
            k_ref[0, h], v_ref[0, h], qt_ref[0, h], g_ref[0, h], mask_ref[...]
        )


def local_kernel(
    lam_ref, k_ref, v_ref, qt_ref, g_ref, level_ref, state_ref, grad_ref, dqt_ref,
    dq_in, dk_in, dv_in,
    dq_ref, dk_ref, dv_ref, gin_ref, mask_ref, half_ref,
):
    del dq_in, dk_in, dv_in
    chunks, heads, tile, width = k_ref.shape
    tile_bits = bits_of(tile)
    first_row = tile_bits + bits_of(chunks) + 1
    groups = level_sources(chunks)
    off = (1 - bit_of_block(0)).astype(F32)

    @pl.loop(0, heads, unroll=4)
    def _(h):
        half_ref[h] = state_ref[h].astype(BF16)
        for i in range(chunks):
            gin_ref[i, h] = off * grad_ref[h]
        row = lam_ref[first_row : first_row + 1, :tile]
        dqt = dqt_ref[h] + row * dot_nt(half_ref[h], g_ref[0, h])
        dq_ref[0, h] = dqt.astype(BF16).T

    for c in range(1, chunks):
        span = slice(c * tile, (c + 1) * tile)
        make_mask(lam_ref, span, mask_ref)

        @pl.loop(0, heads, unroll=4)
        def _(h):
            query_t, grad = qt_ref[c, h], g_ref[c, h]
            dqt, dk_ref[c, h], dv_ref[c, h] = diagonal_tile(
                k_ref[c, h], v_ref[c, h], query_t, grad, mask_ref[...]
            )
            dqt = dqt + lam_ref[first_row : first_row + 1, span] * dot_nt(half_ref[h], grad)
            for j in range(bits_of(chunks)):
                if c >> j & 1:
                    row = lam_ref[tile_bits + 1 + j : tile_bits + 2 + j, span]
                    first = (c >> j ^ 1) << j
                    sources = range(first, first + (1 << j))
                    dqt = dqt + row * dot_nt(level_ref[groups.index(sources), h], grad)
                    part = dot(scaled(row, query_t), grad)
                    for i in sources:
                        gin_ref[i, h] = gin_ref[i, h] + part
            dq_ref[c, h] = dqt.astype(BF16).T


def pair_kernel(levels, state_ref, other_state_ref, keep_ref, found_ref, *out_refs):
    heads = state_ref.shape[0]
    half = heads // 2
    start = bit_of_block(0) * half
    for b, out_ref in zip(levels, out_refs):
        for on in range(2):

            @pl.when(bit_of_block(b) == on)
            def _():
                for i in range(half):
                    if on:
                        spot = (b - 1) * half + i
                        out_ref[i] = keep_ref[spot] + found_ref[heads + spot]
                    else:
                        out_ref[i] = state_ref[start + i] + other_state_ref[start + i]


def sum_kernel(levels, *refs):
    out_ref = refs[-1]
    for n in range(out_ref.shape[0]):
        for i in range(out_ref.shape[1]):
            parts = [ref[i] for b, ref in zip(levels, refs) if b == n + 1]
            out_ref[n, i] = functools.reduce(jnp.add, parts)


def widen(lam_ref, first_row, lanes, wide_ref):
    for b in range(wide_ref.shape[0]):
        row = lam_ref[first_row + b : first_row + b + 1, lanes]
        wide_ref[b] = jnp.broadcast_to(row, wide_ref.shape[:0:-1]).T


def received(sums_ref, i):
    parts = [sums_ref[b, i] for b in range(sums_ref.shape[0])]
    off = [(1 - bit_of_block(b + 1)).astype(F32) for b in range(len(parts))]
    state = functools.reduce(jnp.add, [w * part for w, part in zip(off, parts)])
    return stack_levels([part.astype(BF16) for part in parts], 0), state


def add_to_query(half, wide_ref, grad, dq):
    width = grad.shape[1]
    dq = dq.astype(F32)
    projected = dot_nt(grad, half)
    for b in range(wide_ref.shape[0]):
        dq = dq + wide_ref[b] * projected[:, b * width : (b + 1) * width]
    return dq.astype(BF16)


def add_to_key_value(state, key, value, dk, dv):
    width = key.shape[1]
    state = state.astype(BF16)
    none = jnp.zeros((width, width), BF16)
    right = jnp.concatenate(
        [
            jnp.concatenate([state.T, none], axis=1),
            jnp.concatenate([none, state], axis=1),
        ],
        axis=0,
    )
    product = dot(jnp.concatenate([value, key], axis=1), right)
    dk = dk.astype(F32) + product[:, :width]
    dv = dv.astype(F32) + product[:, width:]
    return dk.astype(BF16), dv.astype(BF16)


def own_half_kernel(
    first_row, lam_ref, k_ref, v_ref, g_ref, gin_ref, sums_ref, dq_in, dk_in, dv_in,
    dq_ref, dk_ref, dv_ref, wide_ref, half_ref, state_ref,
):
    chunks, _, tile, _ = k_ref.shape
    half = half_ref.shape[0]
    start = bit_of_block(0) * half
    for i in range(half):
        half_ref[i], state_ref[i] = received(sums_ref, i)
    for c in range(chunks):
        widen(lam_ref, first_row, slice(c * tile, (c + 1) * tile), wide_ref)
        for i in range(half):
            h = start + i
            dq_ref[c, h] = add_to_query(half_ref[i], wide_ref, g_ref[c, h], dq_in[c, h])
            dk_ref[c, h], dv_ref[c, h] = add_to_key_value(
                gin_ref[c, h] + state_ref[i], k_ref[c, h], v_ref[c, h], dk_in[c, h], dv_in[c, h]
            )


def final_kernel(
    first_row, lam_ref, k_ref, v_ref, g_ref, dq_in, dk_in, dv_in, gin_ref, sums_ref,
    dq_out, dk_out, dv_out, done_ref, wide_ref, half_ref, state_ref, sems,
):
    chunks, heads, tile, _ = k_ref.shape
    half = half_ref.shape[0]
    outs = (dq_out, dk_out, dv_out)

    def ship(n, c):
        place = pl.ds(c * tile, tile)
        return pltpu.make_async_copy(done_ref.at[n, c], outs[n].at[place], sems.at[n, c])

    for i in range(half):
        half_ref[i], state_ref[i] = received(sums_ref, i)
    for core in range(2):

        @pl.when(bit_of_block(0) == core)
        def _():
            for c in range(chunks):
                widen(lam_ref, first_row, slice(c * tile, (c + 1) * tile), wide_ref)
                queries, keys, values = [], [], []
                for h in range(heads):
                    query, key, value = dq_in[c, h], dk_in[c, h], dv_in[c, h]
                    if h // half != core:
                        i = h % half
                        query = add_to_query(half_ref[i], wide_ref, g_ref[c, h], query)
                        key, value = add_to_key_value(
                            gin_ref[c, h] + state_ref[i], k_ref[c, h], v_ref[c, h], key, value
                        )
                    queries.append(query)
                    keys.append(key)
                    values.append(value)
                for n, parts in enumerate((queries, keys, values)):
                    done_ref[n, c] = jnp.swapaxes(jnp.stack(parts), 0, 1)
                    ship(n, c).start()

    for c in range(chunks):
        for n in range(3):
            ship(n, c).wait()


def shape(dims, dtype):
    return jax.ShapeDtypeStruct(dims, dtype)


def params(limit):
    return pltpu.CompilerParams(vmem_limit_bytes=limit * MIB)


def cost(flops, size):
    return pl.CostEstimate(flops=int(flops), bytes_accessed=int(size), transcendentals=0)


def on_device(queries, keys, values, out_grad, level_codes):
    count, heads, width = queries.shape
    scale = width ** (-0.5)
    local_bits = bits_of(count)
    blocks = lax.axis_size("seq")
    tree_bits = bits_of(blocks)
    groups = lax.axis_size("head")
    here = lax.axis_index("seq")
    tile = min(256, count)
    chunks = count // tile
    half = heads // 2
    rows = local_bits + 1 + tree_bits

    def permute(x, apart):
        return lax.ppermute(x, "seq", [(i, i ^ apart) for i in range(blocks)])

    def in_hbm(*arrays):
        return [pltpu.with_memory_space_constraint(x, pltpu.HBM) for x in arrays]

    def near(*arrays):
        return [pltpu.with_memory_space_constraint(x, pltpu.VMEM) for x in arrays]

    token_block = pl.BlockSpec((tile, heads, width), lambda c: (c, 0, 0))
    in_vmem = pl.BlockSpec(memory_space=pltpu.VMEM)
    anywhere = pl.BlockSpec(memory_space=pl.ANY)

    def chunk_block(*dims):
        return pl.BlockSpec((1,) + dims, lambda c: (c,) + (0,) * len(dims))

    def whole(*dims):
        return pl.BlockSpec(dims, lambda c: (0,) * len(dims))

    head_block = chunk_block(heads, tile, width)
    natural = pltpu.VMEM((chunks, heads, tile, width), BF16)
    square = (width, width)
    size = count * heads * width
    groups_in = len(level_sources(chunks))
    queries, keys, values, out_grad = in_hbm(queries, keys, values, out_grad)

    kh, vh, gh, qt, level_state, state = near(
        *pl.pallas_call(
            states_kernel,
            grid=(chunks,),
            in_specs=[token_block] * 4,
            out_specs=[
                *[head_block] * 3, chunk_block(heads, width, tile),
                whole(groups_in, heads, *square), whole(heads, *square),
            ],
            out_shape=[
                *[natural] * 3, pltpu.VMEM((chunks, heads, width, tile), BF16),
                pltpu.VMEM((groups_in, heads, *square), BF16), pltpu.VMEM((heads, *square), F32),
            ],
            scratch_shapes=[pltpu.VMEM((chunks, heads, *square), F32)],
            compiler_params=params(8),
            cost_estimate=cost(2 * size * width, 8 * size),
            name="states",
        )(keys, values, queries, out_grad)
    )
    other_state = permute(state, 1)

    group = lax.axis_index("head")
    pieces = [
        lax.ppermute(level_codes, "head", [(i, (i + r) % groups) for i in range(groups)])
        for r in range(1, groups)
    ]
    pieces, state = lax.optimization_barrier((pieces, state))
    (state,) = near(state)
    pieces = jnp.stack([level_codes, *pieces])
    codes = jnp.concatenate(
        [
            lax.dynamic_index_in_dim(pieces, (group - j) % groups, 0, keepdims=False)[:rows]
            for j in range(groups)
        ],
        axis=1,
    )
    order = jnp.arange(rows)
    factor = jnp.exp2(-0.5 * jnp.maximum(order.astype(F32) - 1.0, 0.0)) / 16.0
    on_bit = jnp.bitwise_and(jnp.right_shift(here, jnp.maximum(order - local_bits - 1, 0)), 1)
    factor = jnp.where(order > local_bits, factor * on_bit.astype(F32), factor)
    lam = codes.astype(F32) * (scale * factor)[:, None]

    wide = (tree_bits - 1) * half
    send, keep = pl.pallas_call(
        functools.partial(grads_kernel, local_bits + 1),
        in_specs=[in_vmem] * 3,
        out_specs=[in_vmem] * 2,
        out_shape=[
            pltpu.VMEM((heads + wide, *square), F32), pltpu.VMEM((wide, *square), F32),
        ],
        compiler_params=params(4),
        cost_estimate=cost(2 * tree_bits * size * width, 8 * size),
        name="level_grads",
    )(lam, qt, gh)
    send, other_state = lax.optimization_barrier((send, other_state))
    found = permute(send, 1)
    (keep,) = near(keep)

    dqt, *parts = pl.pallas_call(
        first_tile_kernel,
        in_specs=[in_vmem] * 5,
        out_specs=[in_vmem] * 4,
        out_shape=[pltpu.VMEM((heads, width, tile), F32)] + [natural] * 3,
        scratch_shapes=[pltpu.VMEM((tile, tile), F32)],
        compiler_params=params(3),
        cost_estimate=cost(14 * size * tile / chunks, 4 * size),
        name="first_tile",
    )(lam, kh, vh, qt, gh)
    hops = [1 << b | m for b in range(1, tree_bits) for m in range(0, 1 << b, 2)]
    hops.sort(key=lambda hop: (hop & hop - 1) == 0)
    messages = pl.pallas_call(
        functools.partial(pair_kernel, [bits_of(hop) for hop in hops]),
        in_specs=[in_vmem] * 4,
        out_specs=[in_vmem] * len(hops),
        out_shape=[pltpu.VMEM((half, *square), F32)] * len(hops),
        compiler_params=params(2),
        cost_estimate=cost(size, size),
        name="pair",
    )(state, other_state, keep, found)
    *messages, parts = lax.optimization_barrier((*messages, parts))
    arrived = [permute(x, hop) for hop, x in zip(hops, messages)]
    *parts, gin = pl.pallas_call(
        local_kernel,
        in_specs=[in_vmem] * 9 + [anywhere] * 3,
        out_specs=[in_vmem] * 4,
        out_shape=[natural] * 3 + [pltpu.VMEM((chunks, heads, *square), F32)],
        input_output_aliases={9: 0, 10: 1, 11: 2},
        scratch_shapes=[pltpu.VMEM((tile, tile), F32), pltpu.VMEM((heads, *square), BF16)],
        compiler_params=params(3),
        cost_estimate=cost(14 * size * tile, 4 * size),
        name="local",
    )(lam, kh, vh, qt, gh, level_state, other_state, found, *near(dqt, *parts))
    arrived, parts = lax.optimization_barrier((arrived, parts))
    sums_shape = (tree_bits - 1, half, *square)
    mine = pl.pallas_call(
        functools.partial(sum_kernel, [bits_of(hop) for hop in hops]),
        in_specs=[in_vmem] * len(hops),
        out_specs=in_vmem,
        out_shape=pltpu.VMEM(sums_shape, F32),
        compiler_params=params(2),
        cost_estimate=cost(size, size),
        name="sums",
    )(*arrived)
    others = permute(mine, 1)

    kept = [
        pltpu.VMEM((tree_bits - 1, tile, width), F32),
        pltpu.VMEM((half, (tree_bits - 1) * width, width), BF16),
        pltpu.VMEM((half, *square), F32),
    ]
    gin, mine = near(gin, mine)
    parts = pl.pallas_call(
        functools.partial(own_half_kernel, local_bits + 2),
        in_specs=[in_vmem] * 9,
        out_specs=[in_vmem] * 3,
        out_shape=[natural] * 3,
        input_output_aliases={6: 0, 7: 1, 8: 2},
        scratch_shapes=kept,
        compiler_params=params(3),
        cost_estimate=cost((tree_bits + 2) * size * width, 8 * size),
        name="own_half",
    )(lam, kh, vh, gh, gin, mine, *near(*parts))
    others, parts = lax.optimization_barrier((others, parts))
    return pl.pallas_call(
        functools.partial(final_kernel, local_bits + 2),
        in_specs=[in_vmem] * 9,
        out_specs=[anywhere] * 3,
        out_shape=[pltpu.HBM((count, heads, width), BF16)] * 3,
        scratch_shapes=[
            pltpu.VMEM((3, chunks, tile, heads, width), BF16), *kept,
            pltpu.SemaphoreType.DMA((3, chunks)),
        ],
        compiler_params=params(10),
        cost_estimate=cost((tree_bits + 2) * size * width, 16 * size),
        name="final",
    )(lam, kh, vh, gh, *near(*parts), gin, others)


def solution(mesh):
    tokens = P("seq", "head", None)
    return jax.shard_map(
        on_device,
        mesh=mesh,
        in_specs=(tokens, tokens, tokens, tokens, P(None, ("seq", "head"))),
        out_specs=(tokens, tokens, tokens),
        check_vma=False,
    )
```

```python
import functools

import jax
import jax.numpy as jnp
from jax import lax
from jax.experimental import pallas as pl
from jax.experimental.pallas import tpu as pltpu
from jax.sharding import PartitionSpec as P

F32 = jnp.float32
BF16 = jnp.bfloat16
MIB = 1 << 20


def bits_of(size):
    return size.bit_length() - 1


def dot(a, b):
    return jnp.dot(a, b, preferred_element_type=F32)


def dot_nt(a, b):
    return lax.dot_general(a, b, (((1,), (1,)), ((), ())), preferred_element_type=F32)


def scaled(row, x):
    return (row * x.astype(F32)).astype(BF16)


def stack_levels(parts, axis):
    return parts[0] if len(parts) == 1 else jnp.concatenate(parts, axis=axis)


def level_sources(chunks):
    found = []
    for j in range(bits_of(chunks)):
        for first in range(0, chunks, 2 << j):
            found.append(range(first, first + (1 << j)))
    return found


def bit_of_block(b):
    return jnp.bitwise_and(jnp.right_shift(lax.axis_index("seq"), b), 1)


def states_kernel(k_ref, v_ref, kh_ref, vh_ref, level_ref, total_ref, chunk_ref):
    heads = k_ref.shape[1]
    chunks = chunk_ref.shape[0]
    step = pl.program_id(0)
    kh_ref[0] = jnp.swapaxes(k_ref[...], 0, 1)
    vh_ref[0] = jnp.swapaxes(v_ref[...], 0, 1)
    for h in range(heads):
        chunk_ref[step, h] = dot(kh_ref[0, h].T, vh_ref[0, h])

    @pl.when(step == chunks - 1)
    def _():
        for h in range(heads):
            tiles = [chunk_ref[i, h] for i in range(chunks)]
            total_ref[h] = functools.reduce(jnp.add, tiles)
            for n, sources in enumerate(level_sources(chunks)):
                state = functools.reduce(jnp.add, [tiles[i] for i in sources])
                level_ref[n, h] = state.astype(BF16)


def grads_kernel(
    first_row, lam_ref, q_ref, g_ref, state_ref, gh_ref, qt_ref, send_ref, keep_ref, grad_ref
):
    heads, width = q_ref.shape[1:]
    half = heads // 2
    levels = grad_ref.shape[0]
    queries = jnp.swapaxes(q_ref[...], 0, 1)
    gh_ref[0] = jnp.swapaxes(g_ref[...], 0, 1)
    first = pl.program_id(0) == 0
    rows = [lam_ref[first_row + b : first_row + b + 1, :] for b in range(levels)]
    for h in range(heads):
        query_t = queries[h].T
        qt_ref[0, h] = query_t
        weighted = stack_levels([scaled(row, query_t) for row in rows], 0)
        grad = dot(weighted, gh_ref[0, h])
        for b in range(levels):
            part = grad[b * width : (b + 1) * width]
            grad_ref[b, h] = jnp.where(first, part, grad_ref[b, h] + part)

    for core in range(2):

        @pl.when((pl.program_id(0) == pl.num_programs(0) - 1) & (bit_of_block(0) == core))
        def _():
            for h in range(heads):
                send_ref[h] = state_ref[h] if core == 0 else grad_ref[0, h]
            for level in range(levels):
                for i in range(half):
                    spot = level * half + i
                    source = state_ref if level == 0 else grad_ref.at[level]
                    keep_ref[spot] = source[core * half + i]
                    send_ref[heads + spot] = source[(1 - core) * half + i]


def make_mask(lam_ref, span, mask_ref):
    tile = mask_ref.shape[0]
    part = min(128, tile)
    source = lax.broadcasted_iota(jnp.int32, (part, part), 0)
    target = lax.broadcasted_iota(jnp.int32, (part, part), 1)
    differ = jnp.where(source <= target, jnp.bitwise_xor(source, target), -1)
    for to in range(0, tile, part):
        lanes = slice(span.start + to, span.start + to + part)
        mask = jnp.where(differ >= 0, lam_ref[0:1, lanes], 0.0)
        for power in range(bits_of(part)):
            mask = jnp.where(differ >= 1 << power, lam_ref[power + 1 : power + 2, lanes], mask)
        mask_ref[to : to + part, to : to + part] = mask
        for at in range(0, tile, part):
            if at < to:
                level = bits_of(at ^ to) + 1
                row = lam_ref[level : level + 1, lanes]
                mask_ref[at : at + part, to : to + part] = jnp.broadcast_to(row, (part, part))
            elif at > to:
                mask_ref[at : at + part, to : to + part] = jnp.zeros((part, part), F32)


def diagonal_tile(key, value, query_t, grad, mask):
    weight_q = (mask * dot_nt(value, grad)).astype(BF16)
    weight_v = (mask * dot(key, query_t)).astype(BF16)
    dk = dot_nt(weight_q, query_t).astype(BF16)
    dv = dot(weight_v, grad).astype(BF16)
    return dot(key.T, weight_q), dk, dv


def first_tile_kernel(
    lam_ref, k_ref, v_ref, qt_ref, g_ref, dqt_ref, dq_ref, dk_ref, dv_ref, mask_ref
):
    del dq_ref
    make_mask(lam_ref, slice(0, mask_ref.shape[0]), mask_ref)

    @pl.loop(0, k_ref.shape[1], unroll=4)
    def _(h):
        dqt_ref[h], dk_ref[0, h], dv_ref[0, h] = diagonal_tile(
            k_ref[0, h], v_ref[0, h], qt_ref[0, h], g_ref[0, h], mask_ref[...]
        )


def local_kernel(
    lam_ref, k_ref, v_ref, qt_ref, g_ref, level_ref, found_ref, dqt_ref,
    dq_in, dk_in, dv_in,
    dq_ref, dk_ref, dv_ref, gin_ref, mask_ref, half_ref,
):
    del dq_in, dk_in, dv_in
    chunks, heads, tile, width = k_ref.shape
    tile_bits = bits_of(tile)
    first_row = tile_bits + bits_of(chunks) + 1
    groups = level_sources(chunks)
    off = (1 - bit_of_block(0)).astype(F32)

    @pl.loop(0, heads, unroll=4)
    def _(h):
        found = found_ref[h]
        half_ref[h] = found.astype(BF16)
        for i in range(chunks):
            gin_ref[i, h] = off * found
        row = lam_ref[first_row : first_row + 1, :tile]
        dqt = dqt_ref[h] + row * dot_nt(half_ref[h], g_ref[0, h])
        dq_ref[0, h] = dqt.astype(BF16).T

    for c in range(1, chunks):
        span = slice(c * tile, (c + 1) * tile)
        make_mask(lam_ref, span, mask_ref)

        @pl.loop(0, heads, unroll=4)
        def _(h):
            query_t, grad = qt_ref[c, h], g_ref[c, h]
            dqt, dk_ref[c, h], dv_ref[c, h] = diagonal_tile(
                k_ref[c, h], v_ref[c, h], query_t, grad, mask_ref[...]
            )
            dqt = dqt + lam_ref[first_row : first_row + 1, span] * dot_nt(half_ref[h], grad)
            for j in range(bits_of(chunks)):
                if c >> j & 1:
                    row = lam_ref[tile_bits + 1 + j : tile_bits + 2 + j, span]
                    first = (c >> j ^ 1) << j
                    sources = range(first, first + (1 << j))
                    dqt = dqt + row * dot_nt(level_ref[groups.index(sources), h], grad)
                    part = dot(scaled(row, query_t), grad)
                    for i in sources:
                        gin_ref[i, h] = gin_ref[i, h] + part
            dq_ref[c, h] = dqt.astype(BF16).T


def pair_kernel(levels, keep_ref, found_ref, *out_refs):
    half = out_refs[0].shape[0]
    heads = found_ref.shape[0] - keep_ref.shape[0]
    for b, out_ref in zip(levels, out_refs):
        for on in range(2):

            @pl.when(bit_of_block(b) == on)
            def _():
                for i in range(half):
                    spot = b * on * half + i
                    out_ref[i] = keep_ref[spot] + found_ref[heads + spot]


def sum_kernel(levels, *refs):
    out_ref = refs[-1]
    for n in range(out_ref.shape[0]):
        for i in range(out_ref.shape[1]):
            parts = [ref[i] for b, ref in zip(levels, refs) if b == n + 1]
            out_ref[n, i] = functools.reduce(jnp.add, parts)


def widen(lam_ref, first_row, lanes, wide_ref):
    for b in range(wide_ref.shape[0]):
        row = lam_ref[first_row + b : first_row + b + 1, lanes]
        wide_ref[b] = jnp.broadcast_to(row, wide_ref.shape[:0:-1]).T


def received(sums_ref, i):
    parts = [sums_ref[b, i] for b in range(sums_ref.shape[0])]
    off = [(1 - bit_of_block(b + 1)).astype(F32) for b in range(len(parts))]
    state = functools.reduce(jnp.add, [w * part for w, part in zip(off, parts)])
    return stack_levels([part.astype(BF16) for part in parts], 0), state


def add_to_query(half, wide_ref, grad, dq):
    width = grad.shape[1]
    dq = dq.astype(F32)
    projected = dot_nt(grad, half)
    for b in range(wide_ref.shape[0]):
        dq = dq + wide_ref[b] * projected[:, b * width : (b + 1) * width]
    return dq.astype(BF16)


def add_to_key_value(state, key, value, dk, dv):
    width = key.shape[1]
    state = state.astype(BF16)
    none = jnp.zeros((width, width), BF16)
    right = jnp.concatenate(
        [
            jnp.concatenate([state.T, none], axis=1),
            jnp.concatenate([none, state], axis=1),
        ],
        axis=0,
    )
    product = dot(jnp.concatenate([value, key], axis=1), right)
    dk = dk.astype(F32) + product[:, :width]
    dv = dv.astype(F32) + product[:, width:]
    return dk.astype(BF16), dv.astype(BF16)


def own_half_kernel(
    first_row, lam_ref, k_ref, v_ref, g_ref, gin_ref, sums_ref, dq_in, dk_in, dv_in,
    dq_ref, dk_ref, dv_ref, wide_ref, half_ref, state_ref,
):
    chunks, _, tile, _ = k_ref.shape
    half = half_ref.shape[0]
    start = bit_of_block(0) * half
    for i in range(half):
        half_ref[i], state_ref[i] = received(sums_ref, i)
    for c in range(chunks):
        widen(lam_ref, first_row, slice(c * tile, (c + 1) * tile), wide_ref)
        for i in range(half):
            h = start + i
            dq_ref[c, h] = add_to_query(half_ref[i], wide_ref, g_ref[c, h], dq_in[c, h])
            dk_ref[c, h], dv_ref[c, h] = add_to_key_value(
                gin_ref[c, h] + state_ref[i], k_ref[c, h], v_ref[c, h], dk_in[c, h], dv_in[c, h]
            )


def final_kernel(
    first_row, lam_ref, k_ref, v_ref, g_ref, dq_in, dk_in, dv_in, gin_ref, sums_ref,
    dq_out, dk_out, dv_out, done_ref, wide_ref, half_ref, state_ref, sems,
):
    chunks, heads, tile, _ = k_ref.shape
    half = half_ref.shape[0]
    outs = (dq_out, dk_out, dv_out)

    def ship(n, c):
        place = pl.ds(c * tile, tile)
        return pltpu.make_async_copy(done_ref.at[n, c], outs[n].at[place], sems.at[n, c])

    for i in range(half):
        half_ref[i], state_ref[i] = received(sums_ref, i)
    for core in range(2):

        @pl.when(bit_of_block(0) == core)
        def _():
            for c in range(chunks):
                widen(lam_ref, first_row, slice(c * tile, (c + 1) * tile), wide_ref)
                queries, keys, values = [], [], []
                for h in range(heads):
                    query, key, value = dq_in[c, h], dk_in[c, h], dv_in[c, h]
                    if h // half != core:
                        i = h % half
                        query = add_to_query(half_ref[i], wide_ref, g_ref[c, h], query)
                        key, value = add_to_key_value(
                            gin_ref[c, h] + state_ref[i], k_ref[c, h], v_ref[c, h], key, value
                        )
                    queries.append(query)
                    keys.append(key)
                    values.append(value)
                for n, parts in enumerate((queries, keys, values)):
                    done_ref[n, c] = jnp.swapaxes(jnp.stack(parts), 0, 1)
                    ship(n, c).start()

    for c in range(chunks):
        for n in range(3):
            ship(n, c).wait()


def shape(dims, dtype):
    return jax.ShapeDtypeStruct(dims, dtype)


def params(limit):
    return pltpu.CompilerParams(vmem_limit_bytes=limit * MIB)


def cost(flops, size):
    return pl.CostEstimate(flops=int(flops), bytes_accessed=int(size), transcendentals=0)


def on_device(queries, keys, values, out_grad, level_codes):
    count, heads, width = queries.shape
    scale = width ** (-0.5)
    local_bits = bits_of(count)
    blocks = lax.axis_size("seq")
    tree_bits = bits_of(blocks)
    groups = lax.axis_size("head")
    here = lax.axis_index("seq")
    tile = min(256, count)
    chunks = count // tile
    half = heads // 2
    rows = local_bits + 1 + tree_bits

    def permute(x, apart):
        return lax.ppermute(x, "seq", [(i, i ^ apart) for i in range(blocks)])

    def in_hbm(*arrays):
        return [pltpu.with_memory_space_constraint(x, pltpu.HBM) for x in arrays]

    def near(*arrays):
        return [pltpu.with_memory_space_constraint(x, pltpu.VMEM) for x in arrays]

    token_block = pl.BlockSpec((tile, heads, width), lambda c: (c, 0, 0))
    in_vmem = pl.BlockSpec(memory_space=pltpu.VMEM)
    anywhere = pl.BlockSpec(memory_space=pl.ANY)

    def chunk_block(*dims):
        return pl.BlockSpec((1,) + dims, lambda c: (c,) + (0,) * len(dims))

    def whole(*dims):
        return pl.BlockSpec(dims, lambda c: (0,) * len(dims))

    head_block = chunk_block(heads, tile, width)
    natural = pltpu.VMEM((chunks, heads, tile, width), BF16)
    square = (width, width)
    size = count * heads * width
    groups_in = len(level_sources(chunks))
    queries, keys, values, out_grad = in_hbm(queries, keys, values, out_grad)

    kh, vh, level_state, state = pl.pallas_call(
        states_kernel,
        grid=(chunks,),
        in_specs=[token_block, token_block],
        out_specs=[
            head_block, head_block, whole(groups_in, heads, *square), whole(heads, *square),
        ],
        out_shape=[
            natural, natural, pltpu.VMEM((groups_in, heads, *square), BF16),
            pltpu.VMEM((heads, *square), F32),
        ],
        scratch_shapes=[pltpu.VMEM((chunks, heads, *square), F32)],
        compiler_params=params(8),
        cost_estimate=cost(2 * size * width, 8 * size),
        name="states",
    )(keys, values)

    group = lax.axis_index("head")
    pieces = [
        lax.ppermute(level_codes, "head", [(i, i ^ r) for i in range(groups)])
        for r in range(1, groups)
    ]
    pieces, state = lax.optimization_barrier((pieces, state))
    pieces = jnp.stack([level_codes, *pieces])
    codes = jnp.concatenate(
        [
            lax.dynamic_index_in_dim(pieces, jnp.bitwise_xor(group, j), 0, keepdims=False)[:rows]
            for j in range(groups)
        ],
        axis=1,
    )
    order = jnp.arange(rows)
    factor = jnp.exp2(-0.5 * jnp.maximum(order.astype(F32) - 1.0, 0.0)) / 16.0
    on_bit = jnp.bitwise_and(jnp.right_shift(here, jnp.maximum(order - local_bits - 1, 0)), 1)
    factor = jnp.where(order > local_bits, factor * on_bit.astype(F32), factor)
    lam = codes.astype(F32) * (scale * factor)[:, None]

    gh, qt, send, keep = pl.pallas_call(
        functools.partial(grads_kernel, local_bits + 1),
        grid=(chunks,),
        in_specs=[
            pl.BlockSpec((rows, tile), lambda c: (0, c)), token_block, token_block,
            whole(heads, *square),
        ],
        out_specs=[
            head_block, chunk_block(heads, width, tile),
            whole(heads + tree_bits * half, *square), whole(tree_bits * half, *square),
        ],
        out_shape=[
            natural, pltpu.VMEM((chunks, heads, width, tile), BF16),
            pltpu.VMEM((heads + tree_bits * half, *square), F32),
            pltpu.VMEM((tree_bits * half, *square), F32),
        ],
        scratch_shapes=[pltpu.VMEM((tree_bits, heads, *square), F32)],
        compiler_params=params(8),
        cost_estimate=cost(2 * tree_bits * size * width, 8 * size),
        name="level_grads",
    )(lam, queries, out_grad, *near(state))
    found = permute(send, 1)
    kh, vh, qt, gh, level_state, keep = near(kh, vh, qt, gh, level_state, keep)

    dqt, *parts = pl.pallas_call(
        first_tile_kernel,
        in_specs=[in_vmem] * 5,
        out_specs=[in_vmem] * 4,
        out_shape=[pltpu.VMEM((heads, width, tile), F32)] + [natural] * 3,
        scratch_shapes=[pltpu.VMEM((tile, tile), F32)],
        compiler_params=params(3),
        cost_estimate=cost(14 * size * tile / chunks, 4 * size),
        name="first_tile",
    )(lam, kh, vh, qt, gh)
    hops = [1 << b | m for b in range(1, tree_bits) for m in range(0, 1 << b, 2)]
    hops.sort(key=lambda hop: (hop & hop - 1) == 0)
    messages = pl.pallas_call(
        functools.partial(pair_kernel, [bits_of(hop) for hop in hops]),
        in_specs=[in_vmem] * 2,
        out_specs=[in_vmem] * len(hops),
        out_shape=[pltpu.VMEM((half, *square), F32)] * len(hops),
        compiler_params=params(2),
        cost_estimate=cost(size, size),
        name="pair",
    )(keep, found)
    *messages, parts = lax.optimization_barrier((*messages, parts))
    arrived = [permute(x, hop) for hop, x in zip(hops, messages)]
    *parts, gin = pl.pallas_call(
        local_kernel,
        in_specs=[in_vmem] * 8 + [anywhere] * 3,
        out_specs=[in_vmem] * 4,
        out_shape=[natural] * 3 + [pltpu.VMEM((chunks, heads, *square), F32)],
        input_output_aliases={8: 0, 9: 1, 10: 2},
        scratch_shapes=[pltpu.VMEM((tile, tile), F32), pltpu.VMEM((heads, *square), BF16)],
        compiler_params=params(3),
        cost_estimate=cost(14 * size * tile, 4 * size),
        name="local",
    )(lam, kh, vh, qt, gh, level_state, found, *near(dqt, *parts))
    arrived, parts = lax.optimization_barrier((arrived, parts))
    sums_shape = (tree_bits - 1, half, *square)
    mine = pl.pallas_call(
        functools.partial(sum_kernel, [bits_of(hop) for hop in hops]),
        in_specs=[in_vmem] * len(hops),
        out_specs=in_vmem,
        out_shape=pltpu.VMEM(sums_shape, F32),
        compiler_params=params(2),
        cost_estimate=cost(size, size),
        name="sums",
    )(*arrived)
    others = permute(mine, 1)

    kept = [
        pltpu.VMEM((tree_bits - 1, tile, width), F32),
        pltpu.VMEM((half, (tree_bits - 1) * width, width), BF16),
        pltpu.VMEM((half, *square), F32),
    ]
    gin, mine = near(gin, mine)
    parts = pl.pallas_call(
        functools.partial(own_half_kernel, local_bits + 2),
        in_specs=[in_vmem] * 9,
        out_specs=[in_vmem] * 3,
        out_shape=[natural] * 3,
        input_output_aliases={6: 0, 7: 1, 8: 2},
        scratch_shapes=kept,
        compiler_params=params(3),
        cost_estimate=cost((tree_bits + 2) * size * width, 8 * size),
        name="own_half",
    )(lam, kh, vh, gh, gin, mine, *near(*parts))
    others, parts = lax.optimization_barrier((others, parts))
    return pl.pallas_call(
        functools.partial(final_kernel, local_bits + 2),
        in_specs=[in_vmem] * 9,
        out_specs=[anywhere] * 3,
        out_shape=[pltpu.HBM((count, heads, width), BF16)] * 3,
        scratch_shapes=[
            pltpu.VMEM((3, chunks, tile, heads, width), BF16), *kept,
            pltpu.SemaphoreType.DMA((3, chunks)),
        ],
        compiler_params=params(10),
        cost_estimate=cost((tree_bits + 2) * size * width, 16 * size),
        name="final",
    )(lam, kh, vh, gh, *near(*parts), gin, others)


def solution(mesh):
    tokens = P("seq", "head", None)
    return jax.shard_map(
        on_device,
        mesh=mesh,
        in_specs=(tokens, tokens, tokens, tokens, P(None, ("seq", "head"))),
        out_specs=(tokens, tokens, tokens),
        check_vma=False,
    )
```

```python
import functools

import jax
import jax.numpy as jnp
from jax import lax
from jax.experimental import pallas as pl
from jax.experimental.pallas import tpu as pltpu
from jax.sharding import PartitionSpec as P

F32 = jnp.float32
BF16 = jnp.bfloat16
MIB = 1 << 20


def bits_of(size):
    return size.bit_length() - 1


def dot(a, b):
    return jnp.dot(a, b, preferred_element_type=F32)


def dot_nt(a, b):
    return lax.dot_general(a, b, (((1,), (1,)), ((), ())), preferred_element_type=F32)


def scaled(row, x):
    return (row * x.astype(F32)).astype(BF16)


def stack_levels(parts, axis):
    return parts[0] if len(parts) == 1 else jnp.concatenate(parts, axis=axis)


def level_sources(chunks):
    found = []
    for j in range(bits_of(chunks)):
        for first in range(0, chunks, 2 << j):
            found.append(range(first, first + (1 << j)))
    return found


def bit_of_block(b):
    return jnp.bitwise_and(jnp.right_shift(lax.axis_index("seq"), b), 1)


def states_kernel(
    k_ref, v_ref, q_ref, g_ref, kh_ref, vh_ref, gh_ref, qt_ref, level_ref, total_ref, chunk_ref
):
    heads = k_ref.shape[1]
    chunks = chunk_ref.shape[0]
    step = pl.program_id(0)
    kh_ref[0] = jnp.swapaxes(k_ref[...], 0, 1)
    vh_ref[0] = jnp.swapaxes(v_ref[...], 0, 1)
    queries = jnp.swapaxes(q_ref[...], 0, 1)
    gh_ref[0] = jnp.swapaxes(g_ref[...], 0, 1)
    for h in range(heads):
        chunk_ref[step, h] = dot(kh_ref[0, h].T, vh_ref[0, h])
        qt_ref[0, h] = queries[h].T

    @pl.when(step == chunks - 1)
    def _():
        for h in range(heads):
            tiles = [chunk_ref[i, h] for i in range(chunks)]
            total_ref[h] = functools.reduce(jnp.add, tiles)
            for n, sources in enumerate(level_sources(chunks)):
                state = functools.reduce(jnp.add, [tiles[i] for i in sources])
                level_ref[n, h] = state.astype(BF16)


def grads_kernel(first_row, lam_ref, qt_ref, g_ref, state_ref, send_ref, keep_ref):
    chunks, heads, tile, width = g_ref.shape
    half = heads // 2
    levels = lam_ref.shape[0] - first_row

    for core in range(2):

        @pl.when(bit_of_block(0) == core)
        def _():
            for h in range(heads):
                weighted = [
                    stack_levels(
                        [
                            scaled(
                                lam_ref[first_row + b : first_row + b + 1, c * tile : (c + 1) * tile],
                                qt_ref[c, h],
                            )
                            for b in range(levels)
                        ],
                        0,
                    )
                    for c in range(chunks)
                ]
                grad = dot(stack_levels(weighted, 1), g_ref[:, h].reshape(chunks * tile, width))
                parts = [grad[b * width : (b + 1) * width] for b in range(levels)]
                state = state_ref[h]
                send_ref[h] = state if core == 0 else parts[0]
                for b, part in enumerate([state, *parts[1:]]):
                    spot = b * half + h % half
                    if h // half == core:
                        keep_ref[spot] = part
                    else:
                        send_ref[heads + spot] = part


def make_mask(lam_ref, span, mask_ref):
    tile = mask_ref.shape[0]
    part = min(128, tile)
    source = lax.broadcasted_iota(jnp.int32, (part, part), 0)
    target = lax.broadcasted_iota(jnp.int32, (part, part), 1)
    differ = jnp.where(source <= target, jnp.bitwise_xor(source, target), -1)
    for to in range(0, tile, part):
        lanes = slice(span.start + to, span.start + to + part)
        mask = jnp.where(differ >= 0, lam_ref[0:1, lanes], 0.0)
        for power in range(bits_of(part)):
            mask = jnp.where(differ >= 1 << power, lam_ref[power + 1 : power + 2, lanes], mask)
        mask_ref[to : to + part, to : to + part] = mask
        for at in range(0, tile, part):
            if at < to:
                level = bits_of(at ^ to) + 1
                row = lam_ref[level : level + 1, lanes]
                mask_ref[at : at + part, to : to + part] = jnp.broadcast_to(row, (part, part))
            elif at > to:
                mask_ref[at : at + part, to : to + part] = jnp.zeros((part, part), F32)


def diagonal_tile(key, value, query_t, grad, mask):
    weight_q = (mask * dot_nt(value, grad)).astype(BF16)
    weight_v = (mask * dot(key, query_t)).astype(BF16)
    dk = dot_nt(weight_q, query_t).astype(BF16)
    dv = dot(weight_v, grad).astype(BF16)
    return dot(key.T, weight_q), dk, dv


def first_tile_kernel(
    lam_ref, k_ref, v_ref, qt_ref, g_ref, dqt_ref, dq_ref, dk_ref, dv_ref, mask_ref
):
    del dq_ref
    make_mask(lam_ref, slice(0, mask_ref.shape[0]), mask_ref)

    @pl.loop(0, k_ref.shape[1], unroll=4)
    def _(h):
        dqt_ref[h], dk_ref[0, h], dv_ref[0, h] = diagonal_tile(
            k_ref[0, h], v_ref[0, h], qt_ref[0, h], g_ref[0, h], mask_ref[...]
        )


def local_kernel(
    lam_ref, k_ref, v_ref, qt_ref, g_ref, level_ref, found_ref, dqt_ref,
    dq_in, dk_in, dv_in,
    dq_ref, dk_ref, dv_ref, gin_ref, mask_ref, half_ref,
):
    del dq_in, dk_in, dv_in
    chunks, heads, tile, width = k_ref.shape
    tile_bits = bits_of(tile)
    first_row = tile_bits + bits_of(chunks) + 1
    groups = level_sources(chunks)
    off = (1 - bit_of_block(0)).astype(F32)

    @pl.loop(0, heads, unroll=4)
    def _(h):
        found = found_ref[h]
        half_ref[h] = found.astype(BF16)
        for i in range(chunks):
            gin_ref[i, h] = off * found
        row = lam_ref[first_row : first_row + 1, :tile]
        dqt = dqt_ref[h] + row * dot_nt(half_ref[h], g_ref[0, h])
        dq_ref[0, h] = dqt.astype(BF16).T

    for c in range(1, chunks):
        span = slice(c * tile, (c + 1) * tile)
        make_mask(lam_ref, span, mask_ref)

        @pl.loop(0, heads, unroll=4)
        def _(h):
            query_t, grad = qt_ref[c, h], g_ref[c, h]
            dqt, dk_ref[c, h], dv_ref[c, h] = diagonal_tile(
                k_ref[c, h], v_ref[c, h], query_t, grad, mask_ref[...]
            )
            dqt = dqt + lam_ref[first_row : first_row + 1, span] * dot_nt(half_ref[h], grad)
            for j in range(bits_of(chunks)):
                if c >> j & 1:
                    row = lam_ref[tile_bits + 1 + j : tile_bits + 2 + j, span]
                    first = (c >> j ^ 1) << j
                    sources = range(first, first + (1 << j))
                    dqt = dqt + row * dot_nt(level_ref[groups.index(sources), h], grad)
                    part = dot(scaled(row, query_t), grad)
                    for i in sources:
                        gin_ref[i, h] = gin_ref[i, h] + part
            dq_ref[c, h] = dqt.astype(BF16).T


def pair_kernel(levels, keep_ref, found_ref, *out_refs):
    half = out_refs[0].shape[0]
    heads = found_ref.shape[0] - keep_ref.shape[0]
    for b, out_ref in zip(levels, out_refs):
        for on in range(2):

            @pl.when(bit_of_block(b) == on)
            def _():
                for i in range(half):
                    spot = b * on * half + i
                    out_ref[i] = keep_ref[spot] + found_ref[heads + spot]


def sum_kernel(levels, *refs):
    out_ref = refs[-1]
    for n in range(out_ref.shape[0]):
        for i in range(out_ref.shape[1]):
            parts = [ref[i] for b, ref in zip(levels, refs) if b == n + 1]
            out_ref[n, i] = functools.reduce(jnp.add, parts)


def widen(lam_ref, first_row, lanes, wide_ref):
    for b in range(wide_ref.shape[0]):
        row = lam_ref[first_row + b : first_row + b + 1, lanes]
        wide_ref[b] = jnp.broadcast_to(row, wide_ref.shape[:0:-1]).T


def received(sums_ref, i):
    parts = [sums_ref[b, i] for b in range(sums_ref.shape[0])]
    off = [(1 - bit_of_block(b + 1)).astype(F32) for b in range(len(parts))]
    state = functools.reduce(jnp.add, [w * part for w, part in zip(off, parts)])
    return stack_levels([part.astype(BF16) for part in parts], 0), state


def add_to_query(half, wide_ref, grad, dq):
    width = grad.shape[1]
    dq = dq.astype(F32)
    projected = dot_nt(grad, half)
    for b in range(wide_ref.shape[0]):
        dq = dq + wide_ref[b] * projected[:, b * width : (b + 1) * width]
    return dq.astype(BF16)


def add_to_key_value(state, key, value, dk, dv):
    width = key.shape[1]
    state = state.astype(BF16)
    none = jnp.zeros((width, width), BF16)
    right = jnp.concatenate(
        [
            jnp.concatenate([state.T, none], axis=1),
            jnp.concatenate([none, state], axis=1),
        ],
        axis=0,
    )
    product = dot(jnp.concatenate([value, key], axis=1), right)
    dk = dk.astype(F32) + product[:, :width]
    dv = dv.astype(F32) + product[:, width:]
    return dk.astype(BF16), dv.astype(BF16)


def own_half_kernel(
    first_row, lam_ref, k_ref, v_ref, g_ref, gin_ref, sums_ref, dq_in, dk_in, dv_in,
    dq_ref, dk_ref, dv_ref, wide_ref, half_ref, state_ref,
):
    chunks, _, tile, _ = k_ref.shape
    half = half_ref.shape[0]
    start = bit_of_block(0) * half
    for i in range(half):
        half_ref[i], state_ref[i] = received(sums_ref, i)
    for c in range(chunks):
        widen(lam_ref, first_row, slice(c * tile, (c + 1) * tile), wide_ref)
        for i in range(half):
            h = start + i
            dq_ref[c, h] = add_to_query(half_ref[i], wide_ref, g_ref[c, h], dq_in[c, h])
            dk_ref[c, h], dv_ref[c, h] = add_to_key_value(
                gin_ref[c, h] + state_ref[i], k_ref[c, h], v_ref[c, h], dk_in[c, h], dv_in[c, h]
            )


def final_kernel(
    first_row, lam_ref, k_ref, v_ref, g_ref, dq_in, dk_in, dv_in, gin_ref, sums_ref,
    dq_out, dk_out, dv_out, done_ref, wide_ref, half_ref, state_ref, sems,
):
    chunks, heads, tile, _ = k_ref.shape
    half = half_ref.shape[0]
    outs = (dq_out, dk_out, dv_out)

    def ship(n, c):
        place = pl.ds(c * tile, tile)
        return pltpu.make_async_copy(done_ref.at[n, c], outs[n].at[place], sems.at[n, c])

    for i in range(half):
        half_ref[i], state_ref[i] = received(sums_ref, i)
    for core in range(2):

        @pl.when(bit_of_block(0) == core)
        def _():
            for c in range(chunks):
                widen(lam_ref, first_row, slice(c * tile, (c + 1) * tile), wide_ref)
                queries, keys, values = [], [], []
                for h in range(heads):
                    query, key, value = dq_in[c, h], dk_in[c, h], dv_in[c, h]
                    if h // half != core:
                        i = h % half
                        query = add_to_query(half_ref[i], wide_ref, g_ref[c, h], query)
                        key, value = add_to_key_value(
                            gin_ref[c, h] + state_ref[i], k_ref[c, h], v_ref[c, h], key, value
                        )
                    queries.append(query)
                    keys.append(key)
                    values.append(value)
                for n, parts in enumerate((queries, keys, values)):
                    done_ref[n, c] = jnp.swapaxes(jnp.stack(parts), 0, 1)
                    ship(n, c).start()

    for c in range(chunks):
        for n in range(3):
            ship(n, c).wait()


def shape(dims, dtype):
    return jax.ShapeDtypeStruct(dims, dtype)


def params(limit):
    return pltpu.CompilerParams(vmem_limit_bytes=limit * MIB)


def cost(flops, size):
    return pl.CostEstimate(flops=int(flops), bytes_accessed=int(size), transcendentals=0)


def on_device(queries, keys, values, out_grad, level_codes):
    count, heads, width = queries.shape
    scale = width ** (-0.5)
    local_bits = bits_of(count)
    blocks = lax.axis_size("seq")
    tree_bits = bits_of(blocks)
    groups = lax.axis_size("head")
    here = lax.axis_index("seq")
    tile = min(256, count)
    chunks = count // tile
    half = heads // 2
    rows = local_bits + 1 + tree_bits

    def permute(x, apart):
        return lax.ppermute(x, "seq", [(i, i ^ apart) for i in range(blocks)])

    def in_hbm(*arrays):
        return [pltpu.with_memory_space_constraint(x, pltpu.HBM) for x in arrays]

    def near(*arrays):
        return [pltpu.with_memory_space_constraint(x, pltpu.VMEM) for x in arrays]

    token_block = pl.BlockSpec((tile, heads, width), lambda c: (c, 0, 0))
    in_vmem = pl.BlockSpec(memory_space=pltpu.VMEM)
    anywhere = pl.BlockSpec(memory_space=pl.ANY)

    def chunk_block(*dims):
        return pl.BlockSpec((1,) + dims, lambda c: (c,) + (0,) * len(dims))

    def whole(*dims):
        return pl.BlockSpec(dims, lambda c: (0,) * len(dims))

    head_block = chunk_block(heads, tile, width)
    natural = pltpu.VMEM((chunks, heads, tile, width), BF16)
    square = (width, width)
    size = count * heads * width
    groups_in = len(level_sources(chunks))
    queries, keys, values, out_grad = in_hbm(queries, keys, values, out_grad)

    kh, vh, gh, qt, level_state, state = pl.pallas_call(
        states_kernel,
        grid=(chunks,),
        in_specs=[token_block] * 4,
        out_specs=[
            *[head_block] * 3, chunk_block(heads, width, tile),
            whole(groups_in, heads, *square), whole(heads, *square),
        ],
        out_shape=[
            *[natural] * 3, pltpu.VMEM((chunks, heads, width, tile), BF16),
            pltpu.VMEM((groups_in, heads, *square), BF16), pltpu.VMEM((heads, *square), F32),
        ],
        scratch_shapes=[pltpu.VMEM((chunks, heads, *square), F32)],
        compiler_params=params(8),
        cost_estimate=cost(2 * size * width, 8 * size),
        name="states",
    )(keys, values, queries, out_grad)

    group = lax.axis_index("head")
    pieces = [
        lax.ppermute(level_codes, "head", [(i, (i + r) % groups) for i in range(groups)])
        for r in range(1, groups)
    ]
    pieces, state = lax.optimization_barrier((pieces, state))
    pieces = jnp.stack([level_codes, *pieces])
    codes = jnp.concatenate(
        [
            lax.dynamic_index_in_dim(pieces, (group - j) % groups, 0, keepdims=False)[:rows]
            for j in range(groups)
        ],
        axis=1,
    )
    order = jnp.arange(rows)
    factor = jnp.exp2(-0.5 * jnp.maximum(order.astype(F32) - 1.0, 0.0)) / 16.0
    on_bit = jnp.bitwise_and(jnp.right_shift(here, jnp.maximum(order - local_bits - 1, 0)), 1)
    factor = jnp.where(order > local_bits, factor * on_bit.astype(F32), factor)
    lam = codes.astype(F32) * (scale * factor)[:, None]

    wide = tree_bits * half
    send, keep = pl.pallas_call(
        functools.partial(grads_kernel, local_bits + 1),
        in_specs=[in_vmem] * 4,
        out_specs=[in_vmem] * 2,
        out_shape=[
            pltpu.VMEM((heads + wide, *square), F32), pltpu.VMEM((wide, *square), F32),
        ],
        compiler_params=params(4),
        cost_estimate=cost(2 * tree_bits * size * width, 2 * size),
        name="level_grads",
    )(lam, *near(qt, gh, state))
    found = permute(send, 1)
    kh, vh, qt, gh, level_state, keep = near(kh, vh, qt, gh, level_state, keep)

    dqt, *parts = pl.pallas_call(
        first_tile_kernel,
        in_specs=[in_vmem] * 5,
        out_specs=[in_vmem] * 4,
        out_shape=[pltpu.VMEM((heads, width, tile), F32)] + [natural] * 3,
        scratch_shapes=[pltpu.VMEM((tile, tile), F32)],
        compiler_params=params(3),
        cost_estimate=cost(14 * size * tile / chunks, 4 * size),
        name="first_tile",
    )(lam, kh, vh, qt, gh)
    hops = [1 << b | m for b in range(1, tree_bits) for m in range(0, 1 << b, 2)]
    hops.sort(key=lambda hop: (hop & hop - 1) == 0)
    messages = pl.pallas_call(
        functools.partial(pair_kernel, [bits_of(hop) for hop in hops]),
        in_specs=[in_vmem] * 2,
        out_specs=[in_vmem] * len(hops),
        out_shape=[pltpu.VMEM((half, *square), F32)] * len(hops),
        compiler_params=params(2),
        cost_estimate=cost(size, size),
        name="pair",
    )(keep, found)
    *messages, parts = lax.optimization_barrier((*messages, parts))
    arrived = [permute(x, hop) for hop, x in zip(hops, messages)]
    *parts, gin = pl.pallas_call(
        local_kernel,
        in_specs=[in_vmem] * 8 + [anywhere] * 3,
        out_specs=[in_vmem] * 4,
        out_shape=[natural] * 3 + [pltpu.VMEM((chunks, heads, *square), F32)],
        input_output_aliases={8: 0, 9: 1, 10: 2},
        scratch_shapes=[pltpu.VMEM((tile, tile), F32), pltpu.VMEM((heads, *square), BF16)],
        compiler_params=params(3),
        cost_estimate=cost(14 * size * tile, 4 * size),
        name="local",
    )(lam, kh, vh, qt, gh, level_state, found, *near(dqt, *parts))
    arrived, parts = lax.optimization_barrier((arrived, parts))
    sums_shape = (tree_bits - 1, half, *square)
    mine = pl.pallas_call(
        functools.partial(sum_kernel, [bits_of(hop) for hop in hops]),
        in_specs=[in_vmem] * len(hops),
        out_specs=in_vmem,
        out_shape=pltpu.VMEM(sums_shape, F32),
        compiler_params=params(2),
        cost_estimate=cost(size, size),
        name="sums",
    )(*arrived)
    others = permute(mine, 1)

    kept = [
        pltpu.VMEM((tree_bits - 1, tile, width), F32),
        pltpu.VMEM((half, (tree_bits - 1) * width, width), BF16),
        pltpu.VMEM((half, *square), F32),
    ]
    gin, mine = near(gin, mine)
    parts = pl.pallas_call(
        functools.partial(own_half_kernel, local_bits + 2),
        in_specs=[in_vmem] * 9,
        out_specs=[in_vmem] * 3,
        out_shape=[natural] * 3,
        input_output_aliases={6: 0, 7: 1, 8: 2},
        scratch_shapes=kept,
        compiler_params=params(3),
        cost_estimate=cost((tree_bits + 2) * size * width, 8 * size),
        name="own_half",
    )(lam, kh, vh, gh, gin, mine, *near(*parts))
    others, parts = lax.optimization_barrier((others, parts))
    return pl.pallas_call(
        functools.partial(final_kernel, local_bits + 2),
        in_specs=[in_vmem] * 9,
        out_specs=[anywhere] * 3,
        out_shape=[pltpu.HBM((count, heads, width), BF16)] * 3,
        scratch_shapes=[
            pltpu.VMEM((3, chunks, tile, heads, width), BF16), *kept,
            pltpu.SemaphoreType.DMA((3, chunks)),
        ],
        compiler_params=params(10),
        cost_estimate=cost((tree_bits + 2) * size * width, 16 * size),
        name="final",
    )(lam, kh, vh, gh, *near(*parts), gin, others)


def solution(mesh):
    tokens = P("seq", "head", None)
    return jax.shard_map(
        on_device,
        mesh=mesh,
        in_specs=(tokens, tokens, tokens, tokens, P(None, ("seq", "head"))),
        out_specs=(tokens, tokens, tokens),
        check_vma=False,
    )
```

```python
import functools

import jax
import jax.numpy as jnp
from jax import lax
from jax.experimental import pallas as pl
from jax.experimental.pallas import tpu as pltpu
from jax.sharding import PartitionSpec as P

F32 = jnp.float32
BF16 = jnp.bfloat16
MIB = 1 << 20


def bits_of(size):
    return size.bit_length() - 1


def dot(a, b):
    return jnp.dot(a, b, preferred_element_type=F32)


def dot_nt(a, b):
    return lax.dot_general(a, b, (((1,), (1,)), ((), ())), preferred_element_type=F32)


def scaled(row, x):
    return (row * x.astype(F32)).astype(BF16)


def stack_levels(parts, axis):
    return parts[0] if len(parts) == 1 else jnp.concatenate(parts, axis=axis)


def level_sources(chunks):
    found = []
    for j in range(bits_of(chunks)):
        for first in range(0, chunks, 2 << j):
            found.append(range(first, first + (1 << j)))
    return found


def bit_of_block(b):
    return jnp.bitwise_and(jnp.right_shift(lax.axis_index("seq"), b), 1)


def states_kernel(pieces, *refs):
    inputs = [refs[n * pieces : (n + 1) * pieces] for n in range(4)]
    kh_ref, vh_ref, gh_ref, qt_ref, level_ref, total_ref, chunk_ref = refs[4 * pieces :]
    heads = kh_ref.shape[1]
    size = kh_ref.shape[2] // pieces
    chunks = chunk_ref.shape[0]
    step = pl.program_id(0)
    for n, (k_ref, v_ref, q_ref, g_ref) in enumerate(zip(*inputs)):
        span = slice(n * size, (n + 1) * size)
        kh_ref[0, :, span] = jnp.swapaxes(k_ref[...], 0, 1)
        vh_ref[0, :, span] = jnp.swapaxes(v_ref[...], 0, 1)
        gh_ref[0, :, span] = jnp.swapaxes(g_ref[...], 0, 1)
        queries = jnp.swapaxes(q_ref[...], 0, 1)
        for h in range(heads):
            qt_ref[0, h, :, span] = queries[h].T
    for h in range(heads):
        chunk_ref[step, h] = dot(kh_ref[0, h].T, vh_ref[0, h])

    @pl.when(step == chunks - 1)
    def _():
        for h in range(heads):
            tiles = [chunk_ref[i, h] for i in range(chunks)]
            total_ref[h] = functools.reduce(jnp.add, tiles)
            for n, sources in enumerate(level_sources(chunks)):
                state = functools.reduce(jnp.add, [tiles[i] for i in sources])
                level_ref[n, h] = state.astype(BF16)


def grads_kernel(first_row, lam_ref, qt_ref, g_ref, state_ref, send_ref, keep_ref, whole_ref):
    chunks, heads, tile, width = g_ref.shape
    half = heads // 2
    levels = lam_ref.shape[0] - first_row

    for core in range(2):

        @pl.when(bit_of_block(0) == core)
        def _():
            for h in range(heads):
                weighted = [
                    stack_levels(
                        [
                            scaled(
                                lam_ref[first_row + b : first_row + b + 1, c * tile : (c + 1) * tile],
                                qt_ref[c, h],
                            )
                            for b in range(levels)
                        ],
                        0,
                    )
                    for c in range(chunks)
                ]
                grad = dot(stack_levels(weighted, 1), g_ref[:, h].reshape(chunks * tile, width))
                parts = [grad[b * width : (b + 1) * width] for b in range(levels)]
                state = state_ref[h]
                whole_ref[h] = state if core == 0 else parts[0]
                for b, part in enumerate([state, *parts[1:]]):
                    spot = b * half + h % half
                    if h // half == core:
                        keep_ref[spot] = part
                    else:
                        send_ref[spot] = part


def make_mask(lam_ref, span, mask_ref):
    tile = mask_ref.shape[0]
    part = min(128, tile)
    source = lax.broadcasted_iota(jnp.int32, (part, part), 0)
    target = lax.broadcasted_iota(jnp.int32, (part, part), 1)
    differ = jnp.where(source <= target, jnp.bitwise_xor(source, target), -1)
    for to in range(0, tile, part):
        lanes = slice(span.start + to, span.start + to + part)
        mask = jnp.where(differ >= 0, lam_ref[0:1, lanes], 0.0)
        for power in range(bits_of(part)):
            mask = jnp.where(differ >= 1 << power, lam_ref[power + 1 : power + 2, lanes], mask)
        mask_ref[to : to + part, to : to + part] = mask
        for at in range(0, tile, part):
            if at < to:
                level = bits_of(at ^ to) + 1
                row = lam_ref[level : level + 1, lanes]
                mask_ref[at : at + part, to : to + part] = jnp.broadcast_to(row, (part, part))
            elif at > to:
                mask_ref[at : at + part, to : to + part] = jnp.zeros((part, part), F32)


def diagonal_tile(key, value, query_t, grad, mask):
    weight_q = (mask * dot_nt(value, grad)).astype(BF16)
    weight_v = (mask * dot(key, query_t)).astype(BF16)
    dk = dot_nt(weight_q, query_t).astype(BF16)
    dv = dot(weight_v, grad).astype(BF16)
    return dot(key.T, weight_q), dk, dv


def first_tile_kernel(
    lam_ref, k_ref, v_ref, qt_ref, g_ref, dqt_ref, dq_ref, dk_ref, dv_ref, mask_ref
):
    del dq_ref
    make_mask(lam_ref, slice(0, mask_ref.shape[0]), mask_ref)

    @pl.loop(0, k_ref.shape[1], unroll=4)
    def _(h):
        dqt_ref[h], dk_ref[0, h], dv_ref[0, h] = diagonal_tile(
            k_ref[0, h], v_ref[0, h], qt_ref[0, h], g_ref[0, h], mask_ref[...]
        )


def local_kernel(
    lam_ref, k_ref, v_ref, qt_ref, g_ref, level_ref, found_ref, dqt_ref,
    dq_in, dk_in, dv_in,
    dq_ref, dk_ref, dv_ref, gin_ref, mask_ref, half_ref,
):
    del dq_in, dk_in, dv_in
    chunks, heads, tile, width = k_ref.shape
    tile_bits = bits_of(tile)
    first_row = tile_bits + bits_of(chunks) + 1
    groups = level_sources(chunks)
    off = (1 - bit_of_block(0)).astype(F32)

    @pl.loop(0, heads, unroll=4)
    def _(h):
        found = found_ref[h]
        half_ref[h] = found.astype(BF16)
        for i in range(chunks):
            gin_ref[i, h] = off * found
        row = lam_ref[first_row : first_row + 1, :tile]
        dqt = dqt_ref[h] + row * dot_nt(half_ref[h], g_ref[0, h])
        dq_ref[0, h] = dqt.astype(BF16).T

    for c in range(1, chunks):
        span = slice(c * tile, (c + 1) * tile)
        make_mask(lam_ref, span, mask_ref)

        @pl.loop(0, heads, unroll=4)
        def _(h):
            query_t, grad = qt_ref[c, h], g_ref[c, h]
            dqt, dk_ref[c, h], dv_ref[c, h] = diagonal_tile(
                k_ref[c, h], v_ref[c, h], query_t, grad, mask_ref[...]
            )
            dqt = dqt + lam_ref[first_row : first_row + 1, span] * dot_nt(half_ref[h], grad)
            for j in range(bits_of(chunks)):
                if c >> j & 1:
                    row = lam_ref[tile_bits + 1 + j : tile_bits + 2 + j, span]
                    first = (c >> j ^ 1) << j
                    sources = range(first, first + (1 << j))
                    dqt = dqt + row * dot_nt(level_ref[groups.index(sources), h], grad)
                    part = dot(scaled(row, query_t), grad)
                    for i in sources:
                        gin_ref[i, h] = gin_ref[i, h] + part
            dq_ref[c, h] = dqt.astype(BF16).T


def pair_kernel(levels, keep_ref, found_ref, *out_refs):
    half = out_refs[0].shape[0]
    for b, out_ref in zip(levels, out_refs):
        for on in range(2):

            @pl.when(bit_of_block(b) == on)
            def _():
                for i in range(half):
                    spot = b * on * half + i
                    out_ref[i] = keep_ref[spot] + found_ref[spot]


def sum_kernel(levels, *refs):
    out_ref = refs[-1]
    for n in range(out_ref.shape[0]):
        for i in range(out_ref.shape[1]):
            parts = [ref[i] for b, ref in zip(levels, refs) if b == n + 1]
            out_ref[n, i] = functools.reduce(jnp.add, parts)


def widen(lam_ref, first_row, lanes, wide_ref):
    for b in range(wide_ref.shape[0]):
        row = lam_ref[first_row + b : first_row + b + 1, lanes]
        wide_ref[b] = jnp.broadcast_to(row, wide_ref.shape[:0:-1]).T


def received(sums_ref, i):
    parts = [sums_ref[b, i] for b in range(sums_ref.shape[0])]
    off = [(1 - bit_of_block(b + 1)).astype(F32) for b in range(len(parts))]
    state = functools.reduce(jnp.add, [w * part for w, part in zip(off, parts)])
    return stack_levels([part.astype(BF16) for part in parts], 0), state


def add_to_query(half, wide_ref, grad, dq):
    width = grad.shape[1]
    dq = dq.astype(F32)
    projected = dot_nt(grad, half)
    for b in range(wide_ref.shape[0]):
        dq = dq + wide_ref[b] * projected[:, b * width : (b + 1) * width]
    return dq.astype(BF16)


def add_to_key_value(state, key, value, dk, dv):
    width = key.shape[1]
    state = state.astype(BF16)
    none = jnp.zeros((width, width), BF16)
    right = jnp.concatenate(
        [
            jnp.concatenate([state.T, none], axis=1),
            jnp.concatenate([none, state], axis=1),
        ],
        axis=0,
    )
    product = dot(jnp.concatenate([value, key], axis=1), right)
    dk = dk.astype(F32) + product[:, :width]
    dv = dv.astype(F32) + product[:, width:]
    return dk.astype(BF16), dv.astype(BF16)


def own_half_kernel(
    first_row, lam_ref, k_ref, v_ref, g_ref, gin_ref, sums_ref, dq_in, dk_in, dv_in,
    dq_ref, dk_ref, dv_ref, wide_ref, half_ref, state_ref,
):
    chunks, _, tile, _ = k_ref.shape
    half = half_ref.shape[0]
    start = bit_of_block(0) * half
    for i in range(half):
        half_ref[i], state_ref[i] = received(sums_ref, i)
    for c in range(chunks):
        widen(lam_ref, first_row, slice(c * tile, (c + 1) * tile), wide_ref)
        for i in range(half):
            h = start + i
            dq_ref[c, h] = add_to_query(half_ref[i], wide_ref, g_ref[c, h], dq_in[c, h])
            dk_ref[c, h], dv_ref[c, h] = add_to_key_value(
                gin_ref[c, h] + state_ref[i], k_ref[c, h], v_ref[c, h], dk_in[c, h], dv_in[c, h]
            )


def final_kernel(
    first_row, lam_ref, k_ref, v_ref, g_ref, dq_in, dk_in, dv_in, gin_ref, sums_ref,
    dq_out, dk_out, dv_out, done_ref, wide_ref, half_ref, state_ref, sems,
):
    chunks, heads, tile, _ = k_ref.shape
    half = half_ref.shape[0]
    outs = (dq_out, dk_out, dv_out)

    pieces = sems.shape[2]
    size = tile // pieces

    def ship(n, c):
        return [
            pltpu.make_async_copy(
                done_ref.at[n, c, pl.ds(i * size, size)],
                outs[n].at[pl.ds(c * tile + i * size, size)],
                sems.at[n, c, i],
            )
            for i in range(pieces)
        ]

    for i in range(half):
        half_ref[i], state_ref[i] = received(sums_ref, i)
    for core in range(2):

        @pl.when(bit_of_block(0) == core)
        def _():
            for c in range(chunks):
                widen(lam_ref, first_row, slice(c * tile, (c + 1) * tile), wide_ref)
                queries, keys, values = [], [], []
                for h in range(heads):
                    query, key, value = dq_in[c, h], dk_in[c, h], dv_in[c, h]
                    if h // half != core:
                        i = h % half
                        query = add_to_query(half_ref[i], wide_ref, g_ref[c, h], query)
                        key, value = add_to_key_value(
                            gin_ref[c, h] + state_ref[i], k_ref[c, h], v_ref[c, h], key, value
                        )
                    queries.append(query)
                    keys.append(key)
                    values.append(value)
                for n, parts in enumerate((queries, keys, values)):
                    done_ref[n, c] = jnp.swapaxes(jnp.stack(parts), 0, 1)
                    for copy in ship(n, c):
                        copy.start()

    for c in range(chunks):
        for n in range(3):
            for copy in ship(n, c):
                copy.wait()


def shape(dims, dtype):
    return jax.ShapeDtypeStruct(dims, dtype)


def params(limit):
    return pltpu.CompilerParams(vmem_limit_bytes=limit * MIB)


def cost(flops, size):
    return pl.CostEstimate(flops=int(flops), bytes_accessed=int(size), transcendentals=0)


def on_device(queries, keys, values, out_grad, level_codes):
    count, heads, width = queries.shape
    scale = width ** (-0.5)
    local_bits = bits_of(count)
    blocks = lax.axis_size("seq")
    tree_bits = bits_of(blocks)
    groups = lax.axis_size("head")
    here = lax.axis_index("seq")
    tile = min(256, count)
    chunks = count // tile
    half = heads // 2
    rows = local_bits + 1 + tree_bits

    def permute(x, apart):
        return lax.ppermute(x, "seq", [(i, i ^ apart) for i in range(blocks)])

    def in_hbm(*arrays):
        return [pltpu.with_memory_space_constraint(x, pltpu.HBM) for x in arrays]

    def near(*arrays):
        return [pltpu.with_memory_space_constraint(x, pltpu.VMEM) for x in arrays]

    pieces = 2 if tile % 256 == 0 else 1
    in_vmem = pl.BlockSpec(memory_space=pltpu.VMEM)
    anywhere = pl.BlockSpec(memory_space=pl.ANY)

    def chunk_block(*dims):
        return pl.BlockSpec((1,) + dims, lambda c: (c,) + (0,) * len(dims))

    def whole(*dims):
        return pl.BlockSpec(dims, lambda c: (0,) * len(dims))

    head_block = chunk_block(heads, tile, width)
    natural = pltpu.VMEM((chunks, heads, tile, width), BF16)
    square = (width, width)
    size = count * heads * width
    groups_in = len(level_sources(chunks))
    queries, keys, values, out_grad = in_hbm(queries, keys, values, out_grad)

    kh, vh, gh, qt, level_state, state = pl.pallas_call(
        functools.partial(states_kernel, pieces),
        grid=(chunks,),
        in_specs=[
            pl.BlockSpec((tile // pieces, heads, width), lambda c, n=n: (pieces * c + n, 0, 0))
            for _ in range(4)
            for n in range(pieces)
        ],
        out_specs=[
            *[head_block] * 3, chunk_block(heads, width, tile),
            whole(groups_in, heads, *square), whole(heads, *square),
        ],
        out_shape=[
            *[natural] * 3, pltpu.VMEM((chunks, heads, width, tile), BF16),
            pltpu.VMEM((groups_in, heads, *square), BF16), pltpu.VMEM((heads, *square), F32),
        ],
        scratch_shapes=[pltpu.VMEM((chunks, heads, *square), F32)],
        compiler_params=params(8),
        cost_estimate=cost(2 * size * width, 8 * size),
        name="states",
    )(*[x for x in (keys, values, queries, out_grad) for _ in range(pieces)])

    group = lax.axis_index("head")
    parts = [
        lax.ppermute(level_codes, "head", [(i, (i + r) % groups) for i in range(groups)])
        for r in range(1, groups)
    ]
    parts, state = lax.optimization_barrier((parts, state))
    parts = jnp.stack([level_codes, *parts])
    codes = jnp.concatenate(
        [
            lax.dynamic_index_in_dim(parts, (group - j) % groups, 0, keepdims=False)[:rows]
            for j in range(groups)
        ],
        axis=1,
    )
    order = jnp.arange(rows)
    factor = jnp.exp2(-0.5 * jnp.maximum(order.astype(F32) - 1.0, 0.0)) / 16.0
    on_bit = jnp.bitwise_and(jnp.right_shift(here, jnp.maximum(order - local_bits - 1, 0)), 1)
    factor = jnp.where(order > local_bits, factor * on_bit.astype(F32), factor)
    lam = codes.astype(F32) * (scale * factor)[:, None]

    wide = tree_bits * half
    send, keep, everything = pl.pallas_call(
        functools.partial(grads_kernel, local_bits + 1),
        in_specs=[in_vmem] * 4,
        out_specs=[in_vmem] * 3,
        out_shape=[pltpu.VMEM((n, *square), F32) for n in (wide, wide, heads)],
        compiler_params=params(4),
        cost_estimate=cost(2 * tree_bits * size * width, 2 * size),
        name="level_grads",
    )(lam, *near(qt, gh, state))
    found = permute(send, 1)
    kh, vh, qt, gh, level_state, keep = near(kh, vh, qt, gh, level_state, keep)

    dqt, *parts = pl.pallas_call(
        first_tile_kernel,
        in_specs=[in_vmem] * 5,
        out_specs=[in_vmem] * 4,
        out_shape=[pltpu.VMEM((heads, width, tile), F32)] + [natural] * 3,
        scratch_shapes=[pltpu.VMEM((tile, tile), F32)],
        compiler_params=params(3),
        cost_estimate=cost(14 * size * tile / chunks, 4 * size),
        name="first_tile",
    )(lam, kh, vh, qt, gh)
    hops = [1 << b | m for b in range(1, tree_bits) for m in range(0, 1 << b, 2)]
    hops.sort(key=lambda hop: (hop & hop - 1) == 0)
    messages = pl.pallas_call(
        functools.partial(pair_kernel, [bits_of(hop) for hop in hops]),
        in_specs=[in_vmem] * 2,
        out_specs=[in_vmem] * len(hops),
        out_shape=[pltpu.VMEM((half, *square), F32)] * len(hops),
        compiler_params=params(2),
        cost_estimate=cost(size, size),
        name="pair",
    )(keep, found)
    *messages, parts, everything = lax.optimization_barrier((*messages, parts, everything))
    arrived = [permute(x, hop) for hop, x in zip(hops, messages)]
    first = permute(everything, 1)
    *parts, gin = pl.pallas_call(
        local_kernel,
        in_specs=[in_vmem] * 8 + [anywhere] * 3,
        out_specs=[in_vmem] * 4,
        out_shape=[natural] * 3 + [pltpu.VMEM((chunks, heads, *square), F32)],
        input_output_aliases={8: 0, 9: 1, 10: 2},
        scratch_shapes=[pltpu.VMEM((tile, tile), F32), pltpu.VMEM((heads, *square), BF16)],
        compiler_params=params(3),
        cost_estimate=cost(14 * size * tile, 4 * size),
        name="local",
    )(lam, kh, vh, qt, gh, level_state, first, *near(dqt, *parts))
    arrived, parts = lax.optimization_barrier((arrived, parts))
    sums_shape = (tree_bits - 1, half, *square)
    mine = pl.pallas_call(
        functools.partial(sum_kernel, [bits_of(hop) for hop in hops]),
        in_specs=[in_vmem] * len(hops),
        out_specs=in_vmem,
        out_shape=pltpu.VMEM(sums_shape, F32),
        compiler_params=params(2),
        cost_estimate=cost(size, size),
        name="sums",
    )(*arrived)
    others = permute(mine, 1)

    kept = [
        pltpu.VMEM((tree_bits - 1, tile, width), F32),
        pltpu.VMEM((half, (tree_bits - 1) * width, width), BF16),
        pltpu.VMEM((half, *square), F32),
    ]
    gin, mine = near(gin, mine)
    parts = pl.pallas_call(
        functools.partial(own_half_kernel, local_bits + 2),
        in_specs=[in_vmem] * 9,
        out_specs=[in_vmem] * 3,
        out_shape=[natural] * 3,
        input_output_aliases={6: 0, 7: 1, 8: 2},
        scratch_shapes=kept,
        compiler_params=params(3),
        cost_estimate=cost((tree_bits + 2) * size * width, 8 * size),
        name="own_half",
    )(lam, kh, vh, gh, gin, mine, *near(*parts))
    others, parts = lax.optimization_barrier((others, parts))
    return pl.pallas_call(
        functools.partial(final_kernel, local_bits + 2),
        in_specs=[in_vmem] * 9,
        out_specs=[anywhere] * 3,
        out_shape=[pltpu.HBM((count, heads, width), BF16)] * 3,
        scratch_shapes=[
            pltpu.VMEM((3, chunks, tile, heads, width), BF16), *kept,
            pltpu.SemaphoreType.DMA((3, chunks, pieces)),
        ],
        compiler_params=params(10),
        cost_estimate=cost((tree_bits + 2) * size * width, 16 * size),
        name="final",
    )(lam, kh, vh, gh, *near(*parts), gin, others)


def solution(mesh):
    tokens = P("seq", "head", None)
    return jax.shard_map(
        on_device,
        mesh=mesh,
        in_specs=(tokens, tokens, tokens, tokens, P(None, ("seq", "head"))),
        out_specs=(tokens, tokens, tokens),
        check_vma=False,
    )
```

```python
import functools

import jax
import jax.numpy as jnp
from jax import lax
from jax.experimental import pallas as pl
from jax.experimental.pallas import tpu as pltpu
from jax.sharding import PartitionSpec as P

F32 = jnp.float32
BF16 = jnp.bfloat16
MIB = 1 << 20


def bits_of(size):
    return size.bit_length() - 1


def dot(a, b):
    return jnp.dot(a, b, preferred_element_type=F32)


def dot_nt(a, b):
    return lax.dot_general(a, b, (((1,), (1,)), ((), ())), preferred_element_type=F32)


def scaled(row, x):
    return (row * x.astype(F32)).astype(BF16)


def stack_levels(parts, axis):
    return parts[0] if len(parts) == 1 else jnp.concatenate(parts, axis=axis)


def level_sources(chunks):
    found = []
    for j in range(bits_of(chunks)):
        for first in range(0, chunks, 2 << j):
            found.append(range(first, first + (1 << j)))
    return found


def bit_of_block(b):
    return jnp.bitwise_and(jnp.right_shift(lax.axis_index("seq"), b), 1)


def states_kernel(pieces, *refs):
    inputs = [refs[n * pieces : (n + 1) * pieces] for n in range(4)]
    kh_ref, vh_ref, gh_ref, qt_ref, level_ref, total_ref, chunk_ref = refs[4 * pieces :]
    heads = kh_ref.shape[1]
    size = kh_ref.shape[2] // pieces
    chunks = chunk_ref.shape[0]
    step = pl.program_id(0)
    for n, (k_ref, v_ref, q_ref, g_ref) in enumerate(zip(*inputs)):
        span = slice(n * size, (n + 1) * size)
        kh_ref[0, :, span] = jnp.swapaxes(k_ref[...], 0, 1)
        vh_ref[0, :, span] = jnp.swapaxes(v_ref[...], 0, 1)
        gh_ref[0, :, span] = jnp.swapaxes(g_ref[...], 0, 1)
        queries = jnp.swapaxes(q_ref[...], 0, 1)
        for h in range(heads):
            qt_ref[0, h, :, span] = queries[h].T
    for h in range(heads):
        chunk_ref[step, h] = dot(kh_ref[0, h].T, vh_ref[0, h])

    @pl.when(step == chunks - 1)
    def _():
        for h in range(heads):
            tiles = [chunk_ref[i, h] for i in range(chunks)]
            total_ref[h] = functools.reduce(jnp.add, tiles)
            for n, sources in enumerate(level_sources(chunks)):
                state = functools.reduce(jnp.add, [tiles[i] for i in sources])
                level_ref[n, h] = state.astype(BF16)


def grads_kernel(first_row, own, lam_ref, qt_ref, g_ref, state_ref, *refs):
    sums_ref, whole_ref = refs[-2:]
    chunks, heads, tile, width = g_ref.shape
    half = heads // 2
    levels = lam_ref.shape[0] - first_row

    for core in range(2):

        @pl.when(bit_of_block(0) == core)
        def _():
            for h in range(heads):
                if (h // half == core) != own:
                    continue
                weighted = [
                    stack_levels(
                        [
                            scaled(
                                lam_ref[first_row + b : first_row + b + 1, c * tile : (c + 1) * tile],
                                qt_ref[c, h],
                            )
                            for b in range(levels)
                        ],
                        0,
                    )
                    for c in range(chunks)
                ]
                grad = dot(stack_levels(weighted, 1), g_ref[:, h].reshape(chunks * tile, width))
                parts = [grad[b * width : (b + 1) * width] for b in range(levels)]
                state = state_ref[h]
                whole_ref[h] = state if core == 0 else parts[0]
                for b, part in enumerate([state, *parts[1:]]):
                    sums_ref[b * half + h % half] = part


def make_mask(lam_ref, span, mask_ref):
    tile = mask_ref.shape[0]
    part = min(128, tile)
    source = lax.broadcasted_iota(jnp.int32, (part, part), 0)
    target = lax.broadcasted_iota(jnp.int32, (part, part), 1)
    differ = jnp.where(source <= target, jnp.bitwise_xor(source, target), -1)
    for to in range(0, tile, part):
        lanes = slice(span.start + to, span.start + to + part)
        mask = jnp.where(differ >= 0, lam_ref[0:1, lanes], 0.0)
        for power in range(bits_of(part)):
            mask = jnp.where(differ >= 1 << power, lam_ref[power + 1 : power + 2, lanes], mask)
        mask_ref[to : to + part, to : to + part] = mask
        for at in range(0, tile, part):
            if at < to:
                level = bits_of(at ^ to) + 1
                row = lam_ref[level : level + 1, lanes]
                mask_ref[at : at + part, to : to + part] = jnp.broadcast_to(row, (part, part))
            elif at > to:
                mask_ref[at : at + part, to : to + part] = jnp.zeros((part, part), F32)


def diagonal_tile(key, value, query_t, grad, mask):
    weight_q = (mask * dot_nt(value, grad)).astype(BF16)
    weight_v = (mask * dot(key, query_t)).astype(BF16)
    dk = dot_nt(weight_q, query_t).astype(BF16)
    dv = dot(weight_v, grad).astype(BF16)
    return dot(key.T, weight_q), dk, dv


def local_kernel(
    lam_ref, k_ref, v_ref, qt_ref, g_ref, level_ref, found_ref,
    dq_ref, dk_ref, dv_ref, gin_ref, mask_ref, half_ref,
):
    chunks, heads, tile, width = k_ref.shape
    tile_bits = bits_of(tile)
    first_row = tile_bits + bits_of(chunks) + 1
    groups = level_sources(chunks)
    off = (1 - bit_of_block(0)).astype(F32)

    @pl.loop(0, heads, unroll=4)
    def _(h):
        found = found_ref[h]
        half_ref[h] = found.astype(BF16)
        for i in range(chunks):
            gin_ref[i, h] = off * found

    for c in range(chunks):
        span = slice(c * tile, (c + 1) * tile)
        make_mask(lam_ref, span, mask_ref)

        @pl.loop(0, heads, unroll=4)
        def _(h):
            query_t, grad = qt_ref[c, h], g_ref[c, h]
            dqt, dk_ref[c, h], dv_ref[c, h] = diagonal_tile(
                k_ref[c, h], v_ref[c, h], query_t, grad, mask_ref[...]
            )
            dqt = dqt + lam_ref[first_row : first_row + 1, span] * dot_nt(half_ref[h], grad)
            for j in range(bits_of(chunks)):
                if c >> j & 1:
                    row = lam_ref[tile_bits + 1 + j : tile_bits + 2 + j, span]
                    first = (c >> j ^ 1) << j
                    sources = range(first, first + (1 << j))
                    dqt = dqt + row * dot_nt(level_ref[groups.index(sources), h], grad)
                    part = dot(scaled(row, query_t), grad)
                    for i in sources:
                        gin_ref[i, h] = gin_ref[i, h] + part
            dq_ref[c, h] = dqt.astype(BF16).T


def pair_kernel(levels, keep_ref, found_ref, *out_refs):
    half = out_refs[0].shape[0]
    for b, out_ref in zip(levels, out_refs):
        for on in range(2):

            @pl.when(bit_of_block(b) == on)
            def _():
                for i in range(half):
                    spot = b * on * half + i
                    out_ref[i] = keep_ref[spot] + found_ref[spot]


def sum_kernel(levels, *refs):
    out_ref = refs[-1]
    for n in range(out_ref.shape[0]):
        for i in range(out_ref.shape[1]):
            parts = [ref[i] for b, ref in zip(levels, refs) if b == n + 1]
            out_ref[n, i] = functools.reduce(jnp.add, parts)


def widen(lam_ref, first_row, lanes, wide_ref):
    for b in range(wide_ref.shape[0]):
        row = lam_ref[first_row + b : first_row + b + 1, lanes]
        wide_ref[b] = jnp.broadcast_to(row, wide_ref.shape[:0:-1]).T


def received(sums_ref, i):
    parts = [sums_ref[b, i] for b in range(sums_ref.shape[0])]
    off = [(1 - bit_of_block(b + 1)).astype(F32) for b in range(len(parts))]
    state = functools.reduce(jnp.add, [w * part for w, part in zip(off, parts)])
    return stack_levels([part.astype(BF16) for part in parts], 0), state


def add_to_query(half, wide_ref, grad, dq):
    width = grad.shape[1]
    dq = dq.astype(F32)
    projected = dot_nt(grad, half)
    for b in range(wide_ref.shape[0]):
        dq = dq + wide_ref[b] * projected[:, b * width : (b + 1) * width]
    return dq.astype(BF16)


def add_to_key_value(state, key, value, dk, dv):
    width = key.shape[1]
    state = state.astype(BF16)
    none = jnp.zeros((width, width), BF16)
    right = jnp.concatenate(
        [
            jnp.concatenate([state.T, none], axis=1),
            jnp.concatenate([none, state], axis=1),
        ],
        axis=0,
    )
    product = dot(jnp.concatenate([value, key], axis=1), right)
    dk = dk.astype(F32) + product[:, :width]
    dv = dv.astype(F32) + product[:, width:]
    return dk.astype(BF16), dv.astype(BF16)


def own_half_kernel(
    first_row, lam_ref, k_ref, v_ref, g_ref, gin_ref, sums_ref, dq_in, dk_in, dv_in,
    dq_ref, dk_ref, dv_ref, wide_ref, half_ref, state_ref,
):
    chunks, _, tile, _ = k_ref.shape
    half = half_ref.shape[0]
    start = bit_of_block(0) * half
    for i in range(half):
        half_ref[i], state_ref[i] = received(sums_ref, i)
    for c in range(chunks):
        widen(lam_ref, first_row, slice(c * tile, (c + 1) * tile), wide_ref)
        for i in range(half):
            h = start + i
            dq_ref[c, h] = add_to_query(half_ref[i], wide_ref, g_ref[c, h], dq_in[c, h])
            dk_ref[c, h], dv_ref[c, h] = add_to_key_value(
                gin_ref[c, h] + state_ref[i], k_ref[c, h], v_ref[c, h], dk_in[c, h], dv_in[c, h]
            )


def final_kernel(
    first_row, lam_ref, k_ref, v_ref, g_ref, dq_in, dk_in, dv_in, gin_ref, sums_ref,
    dq_out, dk_out, dv_out, done_ref, wide_ref, half_ref, state_ref, sems,
):
    chunks, heads, tile, _ = k_ref.shape
    half = half_ref.shape[0]
    outs = (dq_out, dk_out, dv_out)

    pieces = sems.shape[2]
    size = tile // pieces

    def ship(n, c):
        return [
            pltpu.make_async_copy(
                done_ref.at[n, c, pl.ds(i * size, size)],
                outs[n].at[pl.ds(c * tile + i * size, size)],
                sems.at[n, c, i],
            )
            for i in range(pieces)
        ]

    for i in range(half):
        half_ref[i], state_ref[i] = received(sums_ref, i)
    for core in range(2):

        @pl.when(bit_of_block(0) == core)
        def _():
            for c in range(chunks):
                widen(lam_ref, first_row, slice(c * tile, (c + 1) * tile), wide_ref)
                queries, keys, values = [], [], []
                for h in range(heads):
                    query, key, value = dq_in[c, h], dk_in[c, h], dv_in[c, h]
                    if h // half != core:
                        i = h % half
                        query = add_to_query(half_ref[i], wide_ref, g_ref[c, h], query)
                        key, value = add_to_key_value(
                            gin_ref[c, h] + state_ref[i], k_ref[c, h], v_ref[c, h], key, value
                        )
                    queries.append(query)
                    keys.append(key)
                    values.append(value)
                for n, parts in enumerate((queries, keys, values)):
                    done_ref[n, c] = jnp.swapaxes(jnp.stack(parts), 0, 1)
                    for copy in ship(n, c):
                        copy.start()

    for c in range(chunks):
        for n in range(3):
            for copy in ship(n, c):
                copy.wait()


def shape(dims, dtype):
    return jax.ShapeDtypeStruct(dims, dtype)


def params(limit):
    return pltpu.CompilerParams(vmem_limit_bytes=limit * MIB)


def cost(flops, size):
    return pl.CostEstimate(flops=int(flops), bytes_accessed=int(size), transcendentals=0)


def on_device(queries, keys, values, out_grad, level_codes):
    count, heads, width = queries.shape
    scale = width ** (-0.5)
    local_bits = bits_of(count)
    blocks = lax.axis_size("seq")
    tree_bits = bits_of(blocks)
    groups = lax.axis_size("head")
    here = lax.axis_index("seq")
    tile = min(256, count)
    chunks = count // tile
    half = heads // 2
    rows = local_bits + 1 + tree_bits

    def permute(x, apart):
        return lax.ppermute(x, "seq", [(i, i ^ apart) for i in range(blocks)])

    def in_hbm(*arrays):
        return [pltpu.with_memory_space_constraint(x, pltpu.HBM) for x in arrays]

    def near(*arrays):
        return [pltpu.with_memory_space_constraint(x, pltpu.VMEM) for x in arrays]

    pieces = 2 if tile % 256 == 0 else 1
    in_vmem = pl.BlockSpec(memory_space=pltpu.VMEM)
    anywhere = pl.BlockSpec(memory_space=pl.ANY)

    def chunk_block(*dims):
        return pl.BlockSpec((1,) + dims, lambda c: (c,) + (0,) * len(dims))

    def whole(*dims):
        return pl.BlockSpec(dims, lambda c: (0,) * len(dims))

    head_block = chunk_block(heads, tile, width)
    natural = pltpu.VMEM((chunks, heads, tile, width), BF16)
    square = (width, width)
    size = count * heads * width
    groups_in = len(level_sources(chunks))
    queries, keys, values, out_grad = in_hbm(queries, keys, values, out_grad)

    kh, vh, gh, qt, level_state, state = pl.pallas_call(
        functools.partial(states_kernel, pieces),
        grid=(chunks,),
        in_specs=[
            pl.BlockSpec((tile // pieces, heads, width), lambda c, n=n: (pieces * c + n, 0, 0))
            for _ in range(4)
            for n in range(pieces)
        ],
        out_specs=[
            *[head_block] * 3, chunk_block(heads, width, tile),
            whole(groups_in, heads, *square), whole(heads, *square),
        ],
        out_shape=[
            *[natural] * 3, pltpu.VMEM((chunks, heads, width, tile), BF16),
            pltpu.VMEM((groups_in, heads, *square), BF16), pltpu.VMEM((heads, *square), F32),
        ],
        scratch_shapes=[pltpu.VMEM((chunks, heads, *square), F32)],
        compiler_params=params(8),
        cost_estimate=cost(2 * size * width, 8 * size),
        name="states",
    )(*[x for x in (keys, values, queries, out_grad) for _ in range(pieces)])

    group = lax.axis_index("head")
    parts = [
        lax.ppermute(level_codes, "head", [(i, (i + r) % groups) for i in range(groups)])
        for r in range(1, groups)
    ]
    parts, state = lax.optimization_barrier((parts, state))
    parts = jnp.stack([level_codes, *parts])
    codes = jnp.concatenate(
        [
            lax.dynamic_index_in_dim(parts, (group - j) % groups, 0, keepdims=False)[:rows]
            for j in range(groups)
        ],
        axis=1,
    )
    order = jnp.arange(rows)
    factor = jnp.exp2(-0.5 * jnp.maximum(order.astype(F32) - 1.0, 0.0)) / 16.0
    on_bit = jnp.bitwise_and(jnp.right_shift(here, jnp.maximum(order - local_bits - 1, 0)), 1)
    factor = jnp.where(order > local_bits, factor * on_bit.astype(F32), factor)
    lam = codes.astype(F32) * (scale * factor)[:, None]

    kh, vh, qt, gh, level_state, state = near(kh, vh, qt, gh, level_state, state)

    def level_grads(own, before):
        inputs = [lam, qt, gh, state]
        return pl.pallas_call(
            functools.partial(grads_kernel, local_bits + 1, own),
            in_specs=[in_vmem] * len(inputs) + [anywhere] * len(before),
            out_specs=[in_vmem] * 2,
            out_shape=[pltpu.VMEM((n, *square), F32) for n in (tree_bits * half, heads)],
            input_output_aliases={len(inputs): 1} if before else {},
            compiler_params=params(4),
            cost_estimate=cost(tree_bits * size * width, size),
            name="level_grads",
        )(*inputs, *before)

    send, everything = level_grads(False, [])
    found = permute(send, 1)
    keep, everything = level_grads(True, near(everything))
    (keep,) = near(keep)
    hops = [1 << b | m for b in range(1, tree_bits) for m in range(0, 1 << b, 2)]
    hops.sort(key=lambda hop: (hop & hop - 1) == 0)
    messages = pl.pallas_call(
        functools.partial(pair_kernel, [bits_of(hop) for hop in hops]),
        in_specs=[in_vmem] * 2,
        out_specs=[in_vmem] * len(hops),
        out_shape=[pltpu.VMEM((half, *square), F32)] * len(hops),
        compiler_params=params(2),
        cost_estimate=cost(size, size),
        name="pair",
    )(keep, found)
    *messages, everything = lax.optimization_barrier((*messages, everything))
    arrived = [permute(x, hop) for hop, x in zip(hops, messages)]
    first = permute(everything, 1)
    *parts, gin = pl.pallas_call(
        local_kernel,
        in_specs=[in_vmem] * 7,
        out_specs=[in_vmem] * 4,
        out_shape=[natural] * 3 + [pltpu.VMEM((chunks, heads, *square), F32)],
        scratch_shapes=[pltpu.VMEM((tile, tile), F32), pltpu.VMEM((heads, *square), BF16)],
        compiler_params=params(3),
        cost_estimate=cost(14 * size * tile, 4 * size),
        name="local",
    )(lam, kh, vh, qt, gh, level_state, first)
    arrived, parts = lax.optimization_barrier((arrived, parts))
    sums_shape = (tree_bits - 1, half, *square)
    mine = pl.pallas_call(
        functools.partial(sum_kernel, [bits_of(hop) for hop in hops]),
        in_specs=[in_vmem] * len(hops),
        out_specs=in_vmem,
        out_shape=pltpu.VMEM(sums_shape, F32),
        compiler_params=params(2),
        cost_estimate=cost(size, size),
        name="sums",
    )(*arrived)
    others = permute(mine, 1)

    kept = [
        pltpu.VMEM((tree_bits - 1, tile, width), F32),
        pltpu.VMEM((half, (tree_bits - 1) * width, width), BF16),
        pltpu.VMEM((half, *square), F32),
    ]
    gin, mine = near(gin, mine)
    parts = pl.pallas_call(
        functools.partial(own_half_kernel, local_bits + 2),
        in_specs=[in_vmem] * 9,
        out_specs=[in_vmem] * 3,
        out_shape=[natural] * 3,
        input_output_aliases={6: 0, 7: 1, 8: 2},
        scratch_shapes=kept,
        compiler_params=params(3),
        cost_estimate=cost((tree_bits + 2) * size * width, 8 * size),
        name="own_half",
    )(lam, kh, vh, gh, gin, mine, *near(*parts))
    others, parts = lax.optimization_barrier((others, parts))
    return pl.pallas_call(
        functools.partial(final_kernel, local_bits + 2),
        in_specs=[in_vmem] * 9,
        out_specs=[anywhere] * 3,
        out_shape=[pltpu.HBM((count, heads, width), BF16)] * 3,
        scratch_shapes=[
            pltpu.VMEM((3, chunks, tile, heads, width), BF16), *kept,
            pltpu.SemaphoreType.DMA((3, chunks, pieces)),
        ],
        compiler_params=params(10),
        cost_estimate=cost((tree_bits + 2) * size * width, 16 * size),
        name="final",
    )(lam, kh, vh, gh, *near(*parts), gin, others)


def solution(mesh):
    tokens = P("seq", "head", None)
    return jax.shard_map(
        on_device,
        mesh=mesh,
        in_specs=(tokens, tokens, tokens, tokens, P(None, ("seq", "head"))),
        out_specs=(tokens, tokens, tokens),
        check_vma=False,
    )
```

```python
import functools

import jax
import jax.numpy as jnp
from jax import lax
from jax.experimental import pallas as pl
from jax.experimental.pallas import tpu as pltpu
from jax.sharding import PartitionSpec as P

F32 = jnp.float32
BF16 = jnp.bfloat16
MIB = 1 << 20


def bits_of(size):
    return size.bit_length() - 1


def dot(a, b):
    return jnp.dot(a, b, preferred_element_type=F32)


def dot_nt(a, b):
    return lax.dot_general(a, b, (((1,), (1,)), ((), ())), preferred_element_type=F32)


def scaled(row, x):
    return (row * x.astype(F32)).astype(BF16)


def stack_levels(parts, axis):
    return parts[0] if len(parts) == 1 else jnp.concatenate(parts, axis=axis)


def level_sources(chunks):
    found = []
    for j in range(bits_of(chunks)):
        for first in range(0, chunks, 2 << j):
            found.append(range(first, first + (1 << j)))
    return found


def bit_of_block(b):
    return jnp.bitwise_and(jnp.right_shift(lax.axis_index("seq"), b), 1)


def states_kernel(pieces, *refs):
    inputs = [refs[n * pieces : (n + 1) * pieces] for n in range(4)]
    kh_ref, vh_ref, gh_ref, qt_ref, level_ref, total_ref, chunk_ref = refs[4 * pieces :]
    heads = kh_ref.shape[1]
    size = kh_ref.shape[2] // pieces
    chunks = chunk_ref.shape[0]
    step = pl.program_id(0)
    for n, (k_ref, v_ref, q_ref, g_ref) in enumerate(zip(*inputs)):
        span = slice(n * size, (n + 1) * size)
        kh_ref[0, :, span] = jnp.swapaxes(k_ref[...], 0, 1)
        vh_ref[0, :, span] = jnp.swapaxes(v_ref[...], 0, 1)
        gh_ref[0, :, span] = jnp.swapaxes(g_ref[...], 0, 1)
        queries = jnp.swapaxes(q_ref[...], 0, 1)
        for h in range(heads):
            qt_ref[0, h, :, span] = queries[h].T
    for h in range(heads):
        chunk_ref[step, h] = dot(kh_ref[0, h].T, vh_ref[0, h])

    @pl.when(step == chunks - 1)
    def _():
        for h in range(heads):
            tiles = [chunk_ref[i, h] for i in range(chunks)]
            total_ref[h] = functools.reduce(jnp.add, tiles)
            for n, sources in enumerate(level_sources(chunks)):
                state = functools.reduce(jnp.add, [tiles[i] for i in sources])
                level_ref[n, h] = state.astype(BF16)


def grads_kernel(first_row, own, lam_ref, qt_ref, g_ref, state_ref, *refs):
    sums_ref, whole_ref = refs[-2:]
    chunks, heads, tile, width = g_ref.shape
    half = heads // 2
    levels = lam_ref.shape[0] - first_row

    for core in range(2):

        @pl.when(bit_of_block(0) == core)
        def _():
            for h in range(heads):
                if (h // half == core) != own:
                    continue
                weighted = [
                    stack_levels(
                        [
                            scaled(
                                lam_ref[first_row + b : first_row + b + 1, c * tile : (c + 1) * tile],
                                qt_ref[c, h],
                            )
                            for b in range(levels)
                        ],
                        0,
                    )
                    for c in range(chunks)
                ]
                grad = dot(stack_levels(weighted, 1), g_ref[:, h].reshape(chunks * tile, width))
                parts = [grad[b * width : (b + 1) * width] for b in range(levels)]
                state = state_ref[h]
                whole_ref[h] = state if core == 0 else parts[0]
                for b, part in enumerate([state, *parts[1:]]):
                    sums_ref[b * half + h % half] = part


def make_mask(lam_ref, span, mask_ref):
    tile = mask_ref.shape[0]
    part = min(128, tile)
    source = lax.broadcasted_iota(jnp.int32, (part, part), 0)
    target = lax.broadcasted_iota(jnp.int32, (part, part), 1)
    differ = jnp.where(source <= target, jnp.bitwise_xor(source, target), -1)
    for to in range(0, tile, part):
        lanes = slice(span.start + to, span.start + to + part)
        mask = jnp.where(differ >= 0, lam_ref[0:1, lanes], 0.0)
        for power in range(bits_of(part)):
            mask = jnp.where(differ >= 1 << power, lam_ref[power + 1 : power + 2, lanes], mask)
        mask_ref[to : to + part, to : to + part] = mask
        for at in range(0, tile, part):
            if at < to:
                level = bits_of(at ^ to) + 1
                row = lam_ref[level : level + 1, lanes]
                mask_ref[at : at + part, to : to + part] = jnp.broadcast_to(row, (part, part))
            elif at > to:
                mask_ref[at : at + part, to : to + part] = jnp.zeros((part, part), F32)


def diagonal_tile(key, value, query_t, grad, mask):
    weight_q = (mask * dot_nt(value, grad)).astype(BF16)
    weight_v = (mask * dot(key, query_t)).astype(BF16)
    dk = dot_nt(weight_q, query_t).astype(BF16)
    dv = dot(weight_v, grad).astype(BF16)
    return dot(key.T, weight_q), dk, dv


def local_kernel(
    lam_ref, k_ref, v_ref, qt_ref, g_ref, level_ref, found_ref,
    dq_ref, dk_ref, dv_ref, gin_ref, mask_ref, half_ref,
):
    chunks, heads, tile, width = k_ref.shape
    tile_bits = bits_of(tile)
    first_row = tile_bits + bits_of(chunks) + 1
    groups = level_sources(chunks)
    off = (1 - bit_of_block(0)).astype(F32)

    @pl.loop(0, heads, unroll=4)
    def _(h):
        found = found_ref[h]
        half_ref[h] = found.astype(BF16)
        for i in range(chunks):
            gin_ref[i, h] = off * found

    for c in range(chunks):
        span = slice(c * tile, (c + 1) * tile)
        make_mask(lam_ref, span, mask_ref)

        @pl.loop(0, heads, unroll=4)
        def _(h):
            query_t, grad = qt_ref[c, h], g_ref[c, h]
            dqt, dk_ref[c, h], dv_ref[c, h] = diagonal_tile(
                k_ref[c, h], v_ref[c, h], query_t, grad, mask_ref[...]
            )
            dqt = dqt + lam_ref[first_row : first_row + 1, span] * dot_nt(half_ref[h], grad)
            for j in range(bits_of(chunks)):
                if c >> j & 1:
                    row = lam_ref[tile_bits + 1 + j : tile_bits + 2 + j, span]
                    first = (c >> j ^ 1) << j
                    sources = range(first, first + (1 << j))
                    dqt = dqt + row * dot_nt(level_ref[groups.index(sources), h], grad)
                    part = dot(scaled(row, query_t), grad)
                    for i in sources:
                        gin_ref[i, h] = gin_ref[i, h] + part
            dq_ref[c, h] = dqt.astype(BF16).T


def pair_kernel(levels, keep_ref, found_ref, *out_refs):
    half = out_refs[0].shape[0]
    for b, out_ref in zip(levels, out_refs):
        for on in range(2):

            @pl.when(bit_of_block(b) == on)
            def _():
                for i in range(half):
                    spot = b * on * half + i
                    out_ref[i] = keep_ref[spot] + found_ref[spot]


def sum_kernel(levels, *refs):
    out_ref = refs[-1]
    for n in range(out_ref.shape[0]):
        for i in range(out_ref.shape[1]):
            parts = [ref[i] for b, ref in zip(levels, refs) if b == n + 1]
            out_ref[n, i] = functools.reduce(jnp.add, parts)


def widen(lam_ref, first_row, lanes, wide_ref):
    for b in range(wide_ref.shape[0]):
        row = lam_ref[first_row + b : first_row + b + 1, lanes]
        wide_ref[b] = jnp.broadcast_to(row, wide_ref.shape[:0:-1]).T


def received(sums_ref, i):
    parts = [sums_ref[b, i] for b in range(sums_ref.shape[0])]
    off = [(1 - bit_of_block(b + 1)).astype(F32) for b in range(len(parts))]
    state = functools.reduce(jnp.add, [w * part for w, part in zip(off, parts)])
    return stack_levels([part.astype(BF16) for part in parts], 0), state


def add_to_query(half, wide_ref, grad, dq):
    width = grad.shape[1]
    dq = dq.astype(F32)
    projected = dot_nt(grad, half)
    for b in range(wide_ref.shape[0]):
        dq = dq + wide_ref[b] * projected[:, b * width : (b + 1) * width]
    return dq.astype(BF16)


def add_to_key_value(state, key, value, dk, dv):
    width = key.shape[1]
    state = state.astype(BF16)
    none = jnp.zeros((width, width), BF16)
    right = jnp.concatenate(
        [
            jnp.concatenate([state.T, none], axis=1),
            jnp.concatenate([none, state], axis=1),
        ],
        axis=0,
    )
    product = dot(jnp.concatenate([value, key], axis=1), right)
    dk = dk.astype(F32) + product[:, :width]
    dv = dv.astype(F32) + product[:, width:]
    return dk.astype(BF16), dv.astype(BF16)


def own_half_kernel(
    first_row, lam_ref, k_ref, v_ref, g_ref, gin_ref, sums_ref, dq_in, dk_in, dv_in,
    dq_ref, dk_ref, dv_ref, wide_ref, half_ref, state_ref,
):
    chunks, _, tile, _ = k_ref.shape
    half = half_ref.shape[0]
    start = bit_of_block(0) * half
    for i in range(half):
        half_ref[i], state_ref[i] = received(sums_ref, i)
    for c in range(chunks):
        widen(lam_ref, first_row, slice(c * tile, (c + 1) * tile), wide_ref)
        for i in range(half):
            h = start + i
            dq_ref[c, h] = add_to_query(half_ref[i], wide_ref, g_ref[c, h], dq_in[c, h])
            dk_ref[c, h], dv_ref[c, h] = add_to_key_value(
                gin_ref[c, h] + state_ref[i], k_ref[c, h], v_ref[c, h], dk_in[c, h], dv_in[c, h]
            )


def final_kernel(
    first_row, lam_ref, k_ref, v_ref, g_ref, dq_in, dk_in, dv_in, gin_ref, sums_ref,
    dq_out, dk_out, dv_out, done_ref, wide_ref, half_ref, state_ref, sems,
):
    chunks, heads, tile, _ = k_ref.shape
    half = half_ref.shape[0]
    outs = (dq_out, dk_out, dv_out)

    pieces = sems.shape[2]
    size = tile // pieces

    def ship(n, c):
        return [
            pltpu.make_async_copy(
                done_ref.at[n, c, pl.ds(i * size, size)],
                outs[n].at[pl.ds(c * tile + i * size, size)],
                sems.at[n, c, i],
            )
            for i in range(pieces)
        ]

    for i in range(half):
        half_ref[i], state_ref[i] = received(sums_ref, i)
    for core in range(2):

        @pl.when(bit_of_block(0) == core)
        def _():
            for c in range(chunks):
                widen(lam_ref, first_row, slice(c * tile, (c + 1) * tile), wide_ref)

                def send_out(n, parts):
                    done_ref[n, c] = jnp.swapaxes(jnp.stack(parts), 0, 1)
                    for copy in ship(n, c):
                        copy.start()

                queries, keys, values = [], [], []
                for h in range(heads):
                    query = dq_in[c, h]
                    if h // half != core:
                        query = add_to_query(half_ref[h % half], wide_ref, g_ref[c, h], query)
                    queries.append(query)
                send_out(0, queries)
                for h in range(heads):
                    key, value = dk_in[c, h], dv_in[c, h]
                    if h // half != core:
                        key, value = add_to_key_value(
                            gin_ref[c, h] + state_ref[h % half],
                            k_ref[c, h], v_ref[c, h], key, value,
                        )
                    keys.append(key)
                    values.append(value)
                send_out(1, keys)
                send_out(2, values)

    for c in range(chunks):
        for n in range(3):
            for copy in ship(n, c):
                copy.wait()


def shape(dims, dtype):
    return jax.ShapeDtypeStruct(dims, dtype)


def params(limit):
    return pltpu.CompilerParams(vmem_limit_bytes=limit * MIB)


def cost(flops, size):
    return pl.CostEstimate(flops=int(flops), bytes_accessed=int(size), transcendentals=0)


def on_device(queries, keys, values, out_grad, level_codes):
    count, heads, width = queries.shape
    scale = width ** (-0.5)
    local_bits = bits_of(count)
    blocks = lax.axis_size("seq")
    tree_bits = bits_of(blocks)
    groups = lax.axis_size("head")
    here = lax.axis_index("seq")
    tile = min(256, count)
    chunks = count // tile
    half = heads // 2
    rows = local_bits + 1 + tree_bits

    def permute(x, apart):
        return lax.ppermute(x, "seq", [(i, i ^ apart) for i in range(blocks)])

    def in_hbm(*arrays):
        return [pltpu.with_memory_space_constraint(x, pltpu.HBM) for x in arrays]

    def near(*arrays):
        return [pltpu.with_memory_space_constraint(x, pltpu.VMEM) for x in arrays]

    pieces = 2 if tile % 256 == 0 else 1
    in_vmem = pl.BlockSpec(memory_space=pltpu.VMEM)
    anywhere = pl.BlockSpec(memory_space=pl.ANY)

    def chunk_block(*dims):
        return pl.BlockSpec((1,) + dims, lambda c: (c,) + (0,) * len(dims))

    def whole(*dims):
        return pl.BlockSpec(dims, lambda c: (0,) * len(dims))

    head_block = chunk_block(heads, tile, width)
    natural = pltpu.VMEM((chunks, heads, tile, width), BF16)
    square = (width, width)
    size = count * heads * width
    groups_in = len(level_sources(chunks))
    queries, keys, values, out_grad = in_hbm(queries, keys, values, out_grad)

    kh, vh, gh, qt, level_state, state = pl.pallas_call(
        functools.partial(states_kernel, pieces),
        grid=(chunks,),
        in_specs=[
            pl.BlockSpec((tile // pieces, heads, width), lambda c, n=n: (pieces * c + n, 0, 0))
            for _ in range(4)
            for n in range(pieces)
        ],
        out_specs=[
            *[head_block] * 3, chunk_block(heads, width, tile),
            whole(groups_in, heads, *square), whole(heads, *square),
        ],
        out_shape=[
            *[natural] * 3, pltpu.VMEM((chunks, heads, width, tile), BF16),
            pltpu.VMEM((groups_in, heads, *square), BF16), pltpu.VMEM((heads, *square), F32),
        ],
        scratch_shapes=[pltpu.VMEM((chunks, heads, *square), F32)],
        compiler_params=params(8),
        cost_estimate=cost(2 * size * width, 8 * size),
        name="states",
    )(*[x for x in (keys, values, queries, out_grad) for _ in range(pieces)])

    group = lax.axis_index("head")
    parts = [
        lax.ppermute(level_codes, "head", [(i, (i + r) % groups) for i in range(groups)])
        for r in range(1, groups)
    ]
    parts, state = lax.optimization_barrier((parts, state))
    parts = jnp.stack([level_codes, *parts])
    codes = jnp.concatenate(
        [
            lax.dynamic_index_in_dim(parts, (group - j) % groups, 0, keepdims=False)[:rows]
            for j in range(groups)
        ],
        axis=1,
    )
    order = jnp.arange(rows)
    factor = jnp.exp2(-0.5 * jnp.maximum(order.astype(F32) - 1.0, 0.0)) / 16.0
    on_bit = jnp.bitwise_and(jnp.right_shift(here, jnp.maximum(order - local_bits - 1, 0)), 1)
    factor = jnp.where(order > local_bits, factor * on_bit.astype(F32), factor)
    lam = codes.astype(F32) * (scale * factor)[:, None]

    kh, vh, qt, gh, level_state, state = near(kh, vh, qt, gh, level_state, state)

    def level_grads(own, before):
        inputs = [lam, qt, gh, state]
        return pl.pallas_call(
            functools.partial(grads_kernel, local_bits + 1, own),
            in_specs=[in_vmem] * len(inputs) + [anywhere] * len(before),
            out_specs=[in_vmem] * 2,
            out_shape=[pltpu.VMEM((n, *square), F32) for n in (tree_bits * half, heads)],
            input_output_aliases={len(inputs): 1} if before else {},
            compiler_params=params(4),
            cost_estimate=cost(tree_bits * size * width, size),
            name="level_grads",
        )(*inputs, *before)

    send, everything = level_grads(False, [])
    found = permute(send, 1)
    keep, everything = level_grads(True, near(everything))
    (keep,) = near(keep)
    hops = [1 << b | m for b in range(1, tree_bits) for m in range(0, 1 << b, 2)]
    hops.sort(key=lambda hop: (bits_of(hop), -hop))
    messages = pl.pallas_call(
        functools.partial(pair_kernel, [bits_of(hop) for hop in hops]),
        in_specs=[in_vmem] * 2,
        out_specs=[in_vmem] * len(hops),
        out_shape=[pltpu.VMEM((half, *square), F32)] * len(hops),
        compiler_params=params(2),
        cost_estimate=cost(size, size),
        name="pair",
    )(keep, found)
    *messages, everything = lax.optimization_barrier((*messages, everything))
    arrived = [permute(x, hop) for hop, x in zip(hops, messages)]
    first = permute(everything, 1)
    *parts, gin = pl.pallas_call(
        local_kernel,
        in_specs=[in_vmem] * 7,
        out_specs=[in_vmem] * 4,
        out_shape=[natural] * 3 + [pltpu.VMEM((chunks, heads, *square), F32)],
        scratch_shapes=[pltpu.VMEM((tile, tile), F32), pltpu.VMEM((heads, *square), BF16)],
        compiler_params=params(3),
        cost_estimate=cost(14 * size * tile, 4 * size),
        name="local",
    )(lam, kh, vh, qt, gh, level_state, first)
    arrived, parts = lax.optimization_barrier((arrived, parts))
    sums_shape = (tree_bits - 1, half, *square)
    mine = pl.pallas_call(
        functools.partial(sum_kernel, [bits_of(hop) for hop in hops]),
        in_specs=[in_vmem] * len(hops),
        out_specs=in_vmem,
        out_shape=pltpu.VMEM(sums_shape, F32),
        compiler_params=params(2),
        cost_estimate=cost(size, size),
        name="sums",
    )(*arrived)
    others = permute(mine, 1)

    kept = [
        pltpu.VMEM((tree_bits - 1, tile, width), F32),
        pltpu.VMEM((half, (tree_bits - 1) * width, width), BF16),
        pltpu.VMEM((half, *square), F32),
    ]
    gin, mine = near(gin, mine)
    parts = pl.pallas_call(
        functools.partial(own_half_kernel, local_bits + 2),
        in_specs=[in_vmem] * 9,
        out_specs=[in_vmem] * 3,
        out_shape=[natural] * 3,
        input_output_aliases={6: 0, 7: 1, 8: 2},
        scratch_shapes=kept,
        compiler_params=params(3),
        cost_estimate=cost((tree_bits + 2) * size * width, 8 * size),
        name="own_half",
    )(lam, kh, vh, gh, gin, mine, *near(*parts))
    others, parts = lax.optimization_barrier((others, parts))
    return pl.pallas_call(
        functools.partial(final_kernel, local_bits + 2),
        in_specs=[in_vmem] * 9,
        out_specs=[anywhere] * 3,
        out_shape=[pltpu.HBM((count, heads, width), BF16)] * 3,
        scratch_shapes=[
            pltpu.VMEM((3, chunks, tile, heads, width), BF16), *kept,
            pltpu.SemaphoreType.DMA((3, chunks, pieces)),
        ],
        compiler_params=params(10),
        cost_estimate=cost((tree_bits + 2) * size * width, 16 * size),
        name="final",
    )(lam, kh, vh, gh, *near(*parts), gin, others)


def solution(mesh):
    tokens = P("seq", "head", None)
    return jax.shard_map(
        on_device,
        mesh=mesh,
        in_specs=(tokens, tokens, tokens, tokens, P(None, ("seq", "head"))),
        out_specs=(tokens, tokens, tokens),
        check_vma=False,
    )
```

```python
import functools

import jax
import jax.numpy as jnp
from jax import lax
from jax.experimental import pallas as pl
from jax.experimental.pallas import tpu as pltpu
from jax.sharding import PartitionSpec as P

F32 = jnp.float32
BF16 = jnp.bfloat16
MIB = 1 << 20


def bits_of(size):
    return size.bit_length() - 1


def dot(a, b):
    return jnp.dot(a, b, preferred_element_type=F32)


def dot_nt(a, b):
    return lax.dot_general(a, b, (((1,), (1,)), ((), ())), preferred_element_type=F32)


def scaled(row, x):
    return (row * x.astype(F32)).astype(BF16)


def stack_levels(parts, axis):
    return parts[0] if len(parts) == 1 else jnp.concatenate(parts, axis=axis)


def level_sources(chunks):
    found = []
    for j in range(bits_of(chunks)):
        for first in range(0, chunks, 2 << j):
            found.append(range(first, first + (1 << j)))
    return found


def bit_of_block(b):
    return jnp.bitwise_and(jnp.right_shift(lax.axis_index("seq"), b), 1)


def states_kernel(pieces, *refs):
    inputs = [refs[n * pieces : (n + 1) * pieces] for n in range(4)]
    kh_ref, vh_ref, gh_ref, qt_ref, level_ref, total_ref, chunk_ref = refs[4 * pieces :]
    heads = kh_ref.shape[1]
    size = kh_ref.shape[2] // pieces
    chunks = chunk_ref.shape[0]
    step = pl.program_id(0)
    for n, (k_ref, v_ref, q_ref, g_ref) in enumerate(zip(*inputs)):
        span = slice(n * size, (n + 1) * size)
        kh_ref[0, :, span] = jnp.swapaxes(k_ref[...], 0, 1)
        vh_ref[0, :, span] = jnp.swapaxes(v_ref[...], 0, 1)
        gh_ref[0, :, span] = jnp.swapaxes(g_ref[...], 0, 1)
        queries = jnp.swapaxes(q_ref[...], 0, 1)
        for h in range(heads):
            qt_ref[0, h, :, span] = queries[h].T
    for h in range(heads):
        chunk_ref[step, h] = dot(kh_ref[0, h].T, vh_ref[0, h])

    @pl.when(step == chunks - 1)
    def _():
        for h in range(heads):
            tiles = [chunk_ref[i, h] for i in range(chunks)]
            total_ref[h] = functools.reduce(jnp.add, tiles)
            for n, sources in enumerate(level_sources(chunks)):
                state = functools.reduce(jnp.add, [tiles[i] for i in sources])
                level_ref[n, h] = state.astype(BF16)


def grads_kernel(first_row, own, lam_ref, qt_ref, g_ref, state_ref, *refs):
    sums_ref, whole_ref = refs[-2:]
    chunks, heads, tile, width = g_ref.shape
    half = heads // 2
    levels = lam_ref.shape[0] - first_row

    for core in range(2):

        @pl.when(bit_of_block(0) == core)
        def _():
            for h in range(heads):
                if (h // half == core) != own:
                    continue
                weighted = [
                    stack_levels(
                        [
                            scaled(
                                lam_ref[first_row + b : first_row + b + 1, c * tile : (c + 1) * tile],
                                qt_ref[c, h],
                            )
                            for b in range(levels)
                        ],
                        0,
                    )
                    for c in range(chunks)
                ]
                grad = dot(stack_levels(weighted, 1), g_ref[:, h].reshape(chunks * tile, width))
                parts = [grad[b * width : (b + 1) * width] for b in range(levels)]
                state = state_ref[h]
                whole_ref[h] = state if core == 0 else parts[0]
                for b, part in enumerate([state, *parts[1:]]):
                    sums_ref[b * half + h % half] = part


def make_mask(lam_ref, span, mask_ref):
    tile = mask_ref.shape[0]
    part = min(128, tile)
    source = lax.broadcasted_iota(jnp.int32, (part, part), 0)
    target = lax.broadcasted_iota(jnp.int32, (part, part), 1)
    differ = jnp.where(source <= target, jnp.bitwise_xor(source, target), -1)
    for to in range(0, tile, part):
        lanes = slice(span.start + to, span.start + to + part)
        mask = jnp.where(differ >= 0, lam_ref[0:1, lanes], 0.0)
        for power in range(bits_of(part)):
            mask = jnp.where(differ >= 1 << power, lam_ref[power + 1 : power + 2, lanes], mask)
        mask_ref[to : to + part, to : to + part] = mask
        for at in range(0, tile, part):
            if at < to:
                level = bits_of(at ^ to) + 1
                row = lam_ref[level : level + 1, lanes]
                mask_ref[at : at + part, to : to + part] = jnp.broadcast_to(row, (part, part))
            elif at > to:
                mask_ref[at : at + part, to : to + part] = jnp.zeros((part, part), F32)


def diagonal_tile(key, value, query_t, grad, mask):
    weight_q = (mask * dot_nt(value, grad)).astype(BF16)
    weight_v = (mask * dot(key, query_t)).astype(BF16)
    dk = dot_nt(weight_q, query_t).astype(BF16)
    dv = dot(weight_v, grad).astype(BF16)
    return dot(key.T, weight_q), dk, dv


def local_kernel(
    lam_ref, k_ref, v_ref, qt_ref, g_ref, level_ref, found_ref,
    dq_ref, dk_ref, dv_ref, gin_ref, mask_ref, half_ref,
):
    chunks, heads, tile, width = k_ref.shape
    tile_bits = bits_of(tile)
    first_row = tile_bits + bits_of(chunks) + 1
    groups = level_sources(chunks)
    off = (1 - bit_of_block(0)).astype(F32)

    @pl.loop(0, heads, unroll=4)
    def _(h):
        found = found_ref[h]
        half_ref[h] = found.astype(BF16)
        for i in range(chunks):
            gin_ref[i, h] = off * found

    for c in range(chunks):
        span = slice(c * tile, (c + 1) * tile)
        make_mask(lam_ref, span, mask_ref)

        @pl.loop(0, heads, unroll=4)
        def _(h):
            query_t, grad = qt_ref[c, h], g_ref[c, h]
            dqt, dk_ref[c, h], dv_ref[c, h] = diagonal_tile(
                k_ref[c, h], v_ref[c, h], query_t, grad, mask_ref[...]
            )
            dqt = dqt + lam_ref[first_row : first_row + 1, span] * dot_nt(half_ref[h], grad)
            for j in range(bits_of(chunks)):
                if c >> j & 1:
                    row = lam_ref[tile_bits + 1 + j : tile_bits + 2 + j, span]
                    first = (c >> j ^ 1) << j
                    sources = range(first, first + (1 << j))
                    dqt = dqt + row * dot_nt(level_ref[groups.index(sources), h], grad)
                    part = dot(scaled(row, query_t), grad)
                    for i in sources:
                        gin_ref[i, h] = gin_ref[i, h] + part
            dq_ref[c, h] = dqt.astype(BF16).T


def pair_kernel(levels, keep_ref, found_ref, *out_refs):
    half = out_refs[0].shape[0]
    for b, out_ref in zip(levels, out_refs):
        for on in range(2):

            @pl.when(bit_of_block(b) == on)
            def _():
                for i in range(half):
                    spot = b * on * half + i
                    out_ref[i] = keep_ref[spot] + found_ref[spot]


def sum_kernel(levels, *refs):
    out_ref = refs[-1]
    for n in range(out_ref.shape[0]):
        for i in range(out_ref.shape[1]):
            parts = [ref[i] for b, ref in zip(levels, refs) if b == n + 1]
            out_ref[n, i] = functools.reduce(jnp.add, parts)


def widen(lam_ref, first_row, lanes, wide_ref):
    for b in range(wide_ref.shape[0]):
        row = lam_ref[first_row + b : first_row + b + 1, lanes]
        wide_ref[b] = jnp.broadcast_to(row, wide_ref.shape[:0:-1]).T


def received(sums_ref, i):
    parts = [sums_ref[b, i] for b in range(sums_ref.shape[0])]
    off = [(1 - bit_of_block(b + 1)).astype(F32) for b in range(len(parts))]
    state = functools.reduce(jnp.add, [w * part for w, part in zip(off, parts)])
    return stack_levels([part.astype(BF16) for part in parts], 0), state


def add_to_query(half, wide_ref, grad, dq):
    width = grad.shape[1]
    dq = dq.astype(F32)
    projected = dot_nt(grad, half)
    for b in range(wide_ref.shape[0]):
        dq = dq + wide_ref[b] * projected[:, b * width : (b + 1) * width]
    return dq.astype(BF16)


def add_to_key_value(state, key, value, dk, dv):
    width = key.shape[1]
    state = state.astype(BF16)
    none = jnp.zeros((width, width), BF16)
    right = jnp.concatenate(
        [
            jnp.concatenate([state.T, none], axis=1),
            jnp.concatenate([none, state], axis=1),
        ],
        axis=0,
    )
    product = dot(jnp.concatenate([value, key], axis=1), right)
    dk = dk.astype(F32) + product[:, :width]
    dv = dv.astype(F32) + product[:, width:]
    return dk.astype(BF16), dv.astype(BF16)


def own_half_kernel(
    first_row, lam_ref, k_ref, v_ref, g_ref, gin_ref, sums_ref, dq_in, dk_in, dv_in,
    dq_ref, dk_ref, dv_ref, wide_ref, half_ref, state_ref,
):
    chunks, _, tile, _ = k_ref.shape
    half = half_ref.shape[0]
    start = bit_of_block(0) * half
    for i in range(half):
        half_ref[i], state_ref[i] = received(sums_ref, i)
    for c in range(chunks):
        widen(lam_ref, first_row, slice(c * tile, (c + 1) * tile), wide_ref)
        for i in range(half):
            h = start + i
            dq_ref[c, h] = add_to_query(half_ref[i], wide_ref, g_ref[c, h], dq_in[c, h])
            dk_ref[c, h], dv_ref[c, h] = add_to_key_value(
                gin_ref[c, h] + state_ref[i], k_ref[c, h], v_ref[c, h], dk_in[c, h], dv_in[c, h]
            )


def final_kernel(
    first_row, lam_ref, k_ref, v_ref, g_ref, dq_in, dk_in, dv_in, gin_ref, sums_ref,
    dq_out, dk_out, dv_out, done_ref, heads_ref, wide_ref, half_ref, state_ref, sems,
):
    chunks, heads, tile, _ = k_ref.shape
    half = half_ref.shape[0]
    outs = (dq_out, dk_out, dv_out)

    pieces = sems.shape[2]
    size = tile // pieces

    def ship(n, c):
        return [
            pltpu.make_async_copy(
                done_ref.at[n, c, pl.ds(i * size, size)],
                outs[n].at[pl.ds(c * tile + i * size, size)],
                sems.at[n, c, i],
            )
            for i in range(pieces)
        ]

    for i in range(half):
        half_ref[i], state_ref[i] = received(sums_ref, i)
    for core in range(2):

        @pl.when(bit_of_block(0) == core)
        def _():
            for c in range(chunks):
                widen(lam_ref, first_row, slice(c * tile, (c + 1) * tile), wide_ref)
                slot = c % 2
                for h in range(heads):
                    query, key, value = dq_in[c, h], dk_in[c, h], dv_in[c, h]
                    if h // half != core:
                        i = h % half
                        query = add_to_query(half_ref[i], wide_ref, g_ref[c, h], query)
                        key, value = add_to_key_value(
                            gin_ref[c, h] + state_ref[i], k_ref[c, h], v_ref[c, h], key, value
                        )
                    for n, part in enumerate((query, key, value)):
                        heads_ref[slot, n, h] = part
                for n in range(3):
                    done_ref[n, c] = jnp.swapaxes(heads_ref[slot, n], 0, 1)
                    for copy in ship(n, c):
                        copy.start()

    for c in range(chunks):
        for n in range(3):
            for copy in ship(n, c):
                copy.wait()


def shape(dims, dtype):
    return jax.ShapeDtypeStruct(dims, dtype)


def params(limit):
    return pltpu.CompilerParams(vmem_limit_bytes=limit * MIB)


def cost(flops, size):
    return pl.CostEstimate(flops=int(flops), bytes_accessed=int(size), transcendentals=0)


def on_device(queries, keys, values, out_grad, level_codes):
    count, heads, width = queries.shape
    scale = width ** (-0.5)
    local_bits = bits_of(count)
    blocks = lax.axis_size("seq")
    tree_bits = bits_of(blocks)
    groups = lax.axis_size("head")
    here = lax.axis_index("seq")
    tile = min(256, count)
    chunks = count // tile
    half = heads // 2
    rows = local_bits + 1 + tree_bits

    def permute(x, apart):
        return lax.ppermute(x, "seq", [(i, i ^ apart) for i in range(blocks)])

    def in_hbm(*arrays):
        return [pltpu.with_memory_space_constraint(x, pltpu.HBM) for x in arrays]

    def near(*arrays):
        return [pltpu.with_memory_space_constraint(x, pltpu.VMEM) for x in arrays]

    pieces = 2 if tile % 256 == 0 else 1
    in_vmem = pl.BlockSpec(memory_space=pltpu.VMEM)
    anywhere = pl.BlockSpec(memory_space=pl.ANY)

    def chunk_block(*dims):
        return pl.BlockSpec((1,) + dims, lambda c: (c,) + (0,) * len(dims))

    def whole(*dims):
        return pl.BlockSpec(dims, lambda c: (0,) * len(dims))

    head_block = chunk_block(heads, tile, width)
    natural = pltpu.VMEM((chunks, heads, tile, width), BF16)
    square = (width, width)
    size = count * heads * width
    groups_in = len(level_sources(chunks))
    queries, keys, values, out_grad = in_hbm(queries, keys, values, out_grad)

    kh, vh, gh, qt, level_state, state = pl.pallas_call(
        functools.partial(states_kernel, pieces),
        grid=(chunks,),
        in_specs=[
            pl.BlockSpec((tile // pieces, heads, width), lambda c, n=n: (pieces * c + n, 0, 0))
            for _ in range(4)
            for n in range(pieces)
        ],
        out_specs=[
            *[head_block] * 3, chunk_block(heads, width, tile),
            whole(groups_in, heads, *square), whole(heads, *square),
        ],
        out_shape=[
            *[natural] * 3, pltpu.VMEM((chunks, heads, width, tile), BF16),
            pltpu.VMEM((groups_in, heads, *square), BF16), pltpu.VMEM((heads, *square), F32),
        ],
        scratch_shapes=[pltpu.VMEM((chunks, heads, *square), F32)],
        compiler_params=params(8),
        cost_estimate=cost(2 * size * width, 8 * size),
        name="states",
    )(*[x for x in (keys, values, queries, out_grad) for _ in range(pieces)])

    group = lax.axis_index("head")
    parts = [
        lax.ppermute(level_codes, "head", [(i, (i + r) % groups) for i in range(groups)])
        for r in range(1, groups)
    ]
    parts, state = lax.optimization_barrier((parts, state))
    parts = jnp.stack([level_codes, *parts])
    codes = jnp.concatenate(
        [
            lax.dynamic_index_in_dim(parts, (group - j) % groups, 0, keepdims=False)[:rows]
            for j in range(groups)
        ],
        axis=1,
    )
    order = jnp.arange(rows)
    factor = jnp.exp2(-0.5 * jnp.maximum(order.astype(F32) - 1.0, 0.0)) / 16.0
    on_bit = jnp.bitwise_and(jnp.right_shift(here, jnp.maximum(order - local_bits - 1, 0)), 1)
    factor = jnp.where(order > local_bits, factor * on_bit.astype(F32), factor)
    lam = codes.astype(F32) * (scale * factor)[:, None]

    kh, vh, qt, gh, level_state, state = near(kh, vh, qt, gh, level_state, state)

    def level_grads(own, before):
        inputs = [lam, qt, gh, state]
        return pl.pallas_call(
            functools.partial(grads_kernel, local_bits + 1, own),
            in_specs=[in_vmem] * len(inputs) + [anywhere] * len(before),
            out_specs=[in_vmem] * 2,
            out_shape=[pltpu.VMEM((n, *square), F32) for n in (tree_bits * half, heads)],
            input_output_aliases={len(inputs): 1} if before else {},
            compiler_params=params(4),
            cost_estimate=cost(tree_bits * size * width, size),
            name="level_grads",
        )(*inputs, *before)

    send, everything = level_grads(False, [])
    found = permute(send, 1)
    keep, everything = level_grads(True, near(everything))
    (keep,) = near(keep)
    hops = [1 << b | m for b in range(1, tree_bits) for m in range(0, 1 << b, 2)]
    hops.sort(key=lambda hop: (hop & hop - 1) == 0)
    messages = pl.pallas_call(
        functools.partial(pair_kernel, [bits_of(hop) for hop in hops]),
        in_specs=[in_vmem] * 2,
        out_specs=[in_vmem] * len(hops),
        out_shape=[pltpu.VMEM((half, *square), F32)] * len(hops),
        compiler_params=params(2),
        cost_estimate=cost(size, size),
        name="pair",
    )(keep, found)
    *messages, everything = lax.optimization_barrier((*messages, everything))
    arrived = [permute(x, hop) for hop, x in zip(hops, messages)]
    first = permute(everything, 1)
    *parts, gin = pl.pallas_call(
        local_kernel,
        in_specs=[in_vmem] * 7,
        out_specs=[in_vmem] * 4,
        out_shape=[natural] * 3 + [pltpu.VMEM((chunks, heads, *square), F32)],
        scratch_shapes=[pltpu.VMEM((tile, tile), F32), pltpu.VMEM((heads, *square), BF16)],
        compiler_params=params(3),
        cost_estimate=cost(14 * size * tile, 4 * size),
        name="local",
    )(lam, kh, vh, qt, gh, level_state, first)
    arrived, parts = lax.optimization_barrier((arrived, parts))
    sums_shape = (tree_bits - 1, half, *square)
    mine = pl.pallas_call(
        functools.partial(sum_kernel, [bits_of(hop) for hop in hops]),
        in_specs=[in_vmem] * len(hops),
        out_specs=in_vmem,
        out_shape=pltpu.VMEM(sums_shape, F32),
        compiler_params=params(2),
        cost_estimate=cost(size, size),
        name="sums",
    )(*arrived)
    others = permute(mine, 1)

    kept = [
        pltpu.VMEM((tree_bits - 1, tile, width), F32),
        pltpu.VMEM((half, (tree_bits - 1) * width, width), BF16),
        pltpu.VMEM((half, *square), F32),
    ]
    gin, mine = near(gin, mine)
    parts = pl.pallas_call(
        functools.partial(own_half_kernel, local_bits + 2),
        in_specs=[in_vmem] * 9,
        out_specs=[in_vmem] * 3,
        out_shape=[natural] * 3,
        input_output_aliases={6: 0, 7: 1, 8: 2},
        scratch_shapes=kept,
        compiler_params=params(3),
        cost_estimate=cost((tree_bits + 2) * size * width, 8 * size),
        name="own_half",
    )(lam, kh, vh, gh, gin, mine, *near(*parts))
    others, parts = lax.optimization_barrier((others, parts))
    return pl.pallas_call(
        functools.partial(final_kernel, local_bits + 2),
        in_specs=[in_vmem] * 9,
        out_specs=[anywhere] * 3,
        out_shape=[pltpu.HBM((count, heads, width), BF16)] * 3,
        scratch_shapes=[
            pltpu.VMEM((3, chunks, tile, heads, width), BF16),
            pltpu.VMEM((2, 3, heads, tile, width), BF16), *kept,
            pltpu.SemaphoreType.DMA((3, chunks, pieces)),
        ],
        compiler_params=params(14),
        cost_estimate=cost((tree_bits + 2) * size * width, 16 * size),
        name="final",
    )(lam, kh, vh, gh, *near(*parts), gin, others)


def solution(mesh):
    tokens = P("seq", "head", None)
    return jax.shard_map(
        on_device,
        mesh=mesh,
        in_specs=(tokens, tokens, tokens, tokens, P(None, ("seq", "head"))),
        out_specs=(tokens, tokens, tokens),
        check_vma=False,
    )
```

```python
import functools

import jax
import jax.numpy as jnp
from jax import lax
from jax.experimental import pallas as pl
from jax.experimental.pallas import tpu as pltpu
from jax.sharding import PartitionSpec as P

F32 = jnp.float32
BF16 = jnp.bfloat16
MIB = 1 << 20


def bits_of(size):
    return size.bit_length() - 1


def dot(a, b):
    return jnp.dot(a, b, preferred_element_type=F32)


def dot_nt(a, b):
    return lax.dot_general(a, b, (((1,), (1,)), ((), ())), preferred_element_type=F32)


def scaled(row, x):
    return (row * x.astype(F32)).astype(BF16)


def stack_levels(parts, axis):
    return parts[0] if len(parts) == 1 else jnp.concatenate(parts, axis=axis)


def level_sources(chunks):
    found = []
    for j in range(bits_of(chunks)):
        for first in range(0, chunks, 2 << j):
            found.append(range(first, first + (1 << j)))
    return found


def bit_of_block(b):
    return jnp.bitwise_and(jnp.right_shift(lax.axis_index("seq"), b), 1)


def states_kernel(pieces, *refs):
    inputs = [refs[n * pieces : (n + 1) * pieces] for n in range(4)]
    kh_ref, vh_ref, gh_ref, qt_ref, level_ref, total_ref, send_ref, chunk_ref = refs[4 * pieces :]
    half = send_ref.shape[0]
    heads = kh_ref.shape[1]
    size = kh_ref.shape[2] // pieces
    chunks = chunk_ref.shape[0]
    step = pl.program_id(0)
    for n, (k_ref, v_ref, q_ref, g_ref) in enumerate(zip(*inputs)):
        span = slice(n * size, (n + 1) * size)
        kh_ref[0, :, span] = jnp.swapaxes(k_ref[...], 0, 1)
        vh_ref[0, :, span] = jnp.swapaxes(v_ref[...], 0, 1)
        gh_ref[0, :, span] = jnp.swapaxes(g_ref[...], 0, 1)
        queries = jnp.swapaxes(q_ref[...], 0, 1)
        for h in range(heads):
            qt_ref[0, h, :, span] = queries[h].T
    for h in range(heads):
        chunk_ref[step, h] = dot(kh_ref[0, h].T, vh_ref[0, h])

    @pl.when(step == chunks - 1)
    def _():
        for h in range(heads):
            tiles = [chunk_ref[i, h] for i in range(chunks)]
            total_ref[h] = functools.reduce(jnp.add, tiles)
            for n, sources in enumerate(level_sources(chunks)):
                state = functools.reduce(jnp.add, [tiles[i] for i in sources])
                level_ref[n, h] = state.astype(BF16)
        for core in range(2):

            @pl.when(bit_of_block(0) == core)
            def _():
                for i in range(half):
                    send_ref[i] = total_ref[(1 - core) * half + i]


def grads_kernel(first_row, own, lam_ref, qt_ref, g_ref, state_ref, *refs):
    sums_ref, whole_ref = refs[-2:]
    chunks, heads, tile, width = g_ref.shape
    half = heads // 2
    levels = lam_ref.shape[0] - first_row

    for core in range(2):

        @pl.when(bit_of_block(0) == core)
        def _():
            for h in range(heads):
                if (h // half == core) != own:
                    continue
                weighted = [
                    stack_levels(
                        [
                            scaled(
                                lam_ref[first_row + b : first_row + b + 1, c * tile : (c + 1) * tile],
                                qt_ref[c, h],
                            )
                            for b in range(levels)
                        ],
                        0,
                    )
                    for c in range(chunks)
                ]
                grad = dot(stack_levels(weighted, 1), g_ref[:, h].reshape(chunks * tile, width))
                parts = [grad[b * width : (b + 1) * width] for b in range(levels)]
                whole_ref[h] = state_ref[h] if core == 0 else parts[0]
                for b, part in enumerate(parts[1:]):
                    sums_ref[b * half + h % half] = part


def make_mask(lam_ref, span, mask_ref):
    tile = mask_ref.shape[0]
    part = min(128, tile)
    source = lax.broadcasted_iota(jnp.int32, (part, part), 0)
    target = lax.broadcasted_iota(jnp.int32, (part, part), 1)
    differ = jnp.where(source <= target, jnp.bitwise_xor(source, target), -1)
    for to in range(0, tile, part):
        lanes = slice(span.start + to, span.start + to + part)
        mask = jnp.where(differ >= 0, lam_ref[0:1, lanes], 0.0)
        for power in range(bits_of(part)):
            mask = jnp.where(differ >= 1 << power, lam_ref[power + 1 : power + 2, lanes], mask)
        mask_ref[to : to + part, to : to + part] = mask
        for at in range(0, tile, part):
            if at < to:
                level = bits_of(at ^ to) + 1
                row = lam_ref[level : level + 1, lanes]
                mask_ref[at : at + part, to : to + part] = jnp.broadcast_to(row, (part, part))
            elif at > to:
                mask_ref[at : at + part, to : to + part] = jnp.zeros((part, part), F32)


def diagonal_tile(key, value, query_t, grad, mask):
    weight_q = (mask * dot_nt(value, grad)).astype(BF16)
    weight_v = (mask * dot(key, query_t)).astype(BF16)
    dk = dot_nt(weight_q, query_t).astype(BF16)
    dv = dot(weight_v, grad).astype(BF16)
    return dot(key.T, weight_q), dk, dv


def local_kernel(
    lam_ref, k_ref, v_ref, qt_ref, g_ref, level_ref, found_ref,
    dq_ref, dk_ref, dv_ref, gin_ref, mask_ref, half_ref,
):
    chunks, heads, tile, width = k_ref.shape
    tile_bits = bits_of(tile)
    first_row = tile_bits + bits_of(chunks) + 1
    groups = level_sources(chunks)
    off = (1 - bit_of_block(0)).astype(F32)

    @pl.loop(0, heads, unroll=4)
    def _(h):
        found = found_ref[h]
        half_ref[h] = found.astype(BF16)
        for i in range(chunks):
            gin_ref[i, h] = off * found

    for c in range(chunks):
        span = slice(c * tile, (c + 1) * tile)
        make_mask(lam_ref, span, mask_ref)

        @pl.loop(0, heads, unroll=4)
        def _(h):
            query_t, grad = qt_ref[c, h], g_ref[c, h]
            dqt, dk_ref[c, h], dv_ref[c, h] = diagonal_tile(
                k_ref[c, h], v_ref[c, h], query_t, grad, mask_ref[...]
            )
            dqt = dqt + lam_ref[first_row : first_row + 1, span] * dot_nt(half_ref[h], grad)
            for j in range(bits_of(chunks)):
                if c >> j & 1:
                    row = lam_ref[tile_bits + 1 + j : tile_bits + 2 + j, span]
                    first = (c >> j ^ 1) << j
                    sources = range(first, first + (1 << j))
                    dqt = dqt + row * dot_nt(level_ref[groups.index(sources), h], grad)
                    part = dot(scaled(row, query_t), grad)
                    for i in sources:
                        gin_ref[i, h] = gin_ref[i, h] + part
            dq_ref[c, h] = dqt.astype(BF16).T


def pair_kernel(levels, state_ref, other_ref, keep_ref, found_ref, *out_refs):
    half = out_refs[0].shape[0]
    start = bit_of_block(0) * half
    for b, out_ref in zip(levels, out_refs):
        for on in range(2):

            @pl.when(bit_of_block(b) == on)
            def _():
                for i in range(half):
                    if on:
                        spot = (b - 1) * half + i
                        out_ref[i] = keep_ref[spot] + found_ref[spot]
                    else:
                        out_ref[i] = state_ref[start + i] + other_ref[i]


def sum_kernel(levels, *refs):
    out_ref = refs[-1]
    for n in range(out_ref.shape[0]):
        for i in range(out_ref.shape[1]):
            parts = [ref[i] for b, ref in zip(levels, refs) if b == n + 1]
            out_ref[n, i] = functools.reduce(jnp.add, parts)


def widen(lam_ref, first_row, lanes, wide_ref):
    for b in range(wide_ref.shape[0]):
        row = lam_ref[first_row + b : first_row + b + 1, lanes]
        wide_ref[b] = jnp.broadcast_to(row, wide_ref.shape[:0:-1]).T


def received(sums_ref, i):
    parts = [sums_ref[b, i] for b in range(sums_ref.shape[0])]
    off = [(1 - bit_of_block(b + 1)).astype(F32) for b in range(len(parts))]
    state = functools.reduce(jnp.add, [w * part for w, part in zip(off, parts)])
    return stack_levels([part.astype(BF16) for part in parts], 0), state


def add_to_query(half, wide_ref, grad, dq):
    width = grad.shape[1]
    dq = dq.astype(F32)
    projected = dot_nt(grad, half)
    for b in range(wide_ref.shape[0]):
        dq = dq + wide_ref[b] * projected[:, b * width : (b + 1) * width]
    return dq.astype(BF16)


def add_to_key_value(state, key, value, dk, dv):
    width = key.shape[1]
    state = state.astype(BF16)
    none = jnp.zeros((width, width), BF16)
    right = jnp.concatenate(
        [
            jnp.concatenate([state.T, none], axis=1),
            jnp.concatenate([none, state], axis=1),
        ],
        axis=0,
    )
    product = dot(jnp.concatenate([value, key], axis=1), right)
    dk = dk.astype(F32) + product[:, :width]
    dv = dv.astype(F32) + product[:, width:]
    return dk.astype(BF16), dv.astype(BF16)


def own_half_kernel(
    first_row, lam_ref, k_ref, v_ref, g_ref, gin_ref, sums_ref, dq_in, dk_in, dv_in,
    dq_ref, dk_ref, dv_ref, wide_ref, half_ref, state_ref,
):
    chunks, _, tile, _ = k_ref.shape
    half = half_ref.shape[0]
    start = bit_of_block(0) * half
    for i in range(half):
        half_ref[i], state_ref[i] = received(sums_ref, i)
    for c in range(chunks):
        widen(lam_ref, first_row, slice(c * tile, (c + 1) * tile), wide_ref)
        for i in range(half):
            h = start + i
            dq_ref[c, h] = add_to_query(half_ref[i], wide_ref, g_ref[c, h], dq_in[c, h])
            dk_ref[c, h], dv_ref[c, h] = add_to_key_value(
                gin_ref[c, h] + state_ref[i], k_ref[c, h], v_ref[c, h], dk_in[c, h], dv_in[c, h]
            )


def final_kernel(
    first_row, lam_ref, k_ref, v_ref, g_ref, dq_in, dk_in, dv_in, gin_ref, sums_ref,
    dq_out, dk_out, dv_out, done_ref, wide_ref, half_ref, state_ref, sems,
):
    chunks, heads, tile, _ = k_ref.shape
    half = half_ref.shape[0]
    outs = (dq_out, dk_out, dv_out)

    pieces = sems.shape[2]
    size = tile // pieces

    def ship(n, c):
        return [
            pltpu.make_async_copy(
                done_ref.at[n, c, pl.ds(i * size, size)],
                outs[n].at[pl.ds(c * tile + i * size, size)],
                sems.at[n, c, i],
            )
            for i in range(pieces)
        ]

    for i in range(half):
        half_ref[i], state_ref[i] = received(sums_ref, i)
    for core in range(2):

        @pl.when(bit_of_block(0) == core)
        def _():
            for c in range(chunks):
                widen(lam_ref, first_row, slice(c * tile, (c + 1) * tile), wide_ref)
                queries, keys, values = [], [], []
                for h in range(heads):
                    query, key, value = dq_in[c, h], dk_in[c, h], dv_in[c, h]
                    if h // half != core:
                        i = h % half
                        query = add_to_query(half_ref[i], wide_ref, g_ref[c, h], query)
                        key, value = add_to_key_value(
                            gin_ref[c, h] + state_ref[i], k_ref[c, h], v_ref[c, h], key, value
                        )
                    queries.append(query)
                    keys.append(key)
                    values.append(value)
                for n, parts in enumerate((queries, keys, values)):
                    done_ref[n, c] = jnp.swapaxes(jnp.stack(parts), 0, 1)
                    for copy in ship(n, c):
                        copy.start()

    for c in range(chunks):
        for n in range(3):
            for copy in ship(n, c):
                copy.wait()


def shape(dims, dtype):
    return jax.ShapeDtypeStruct(dims, dtype)


def params(limit):
    return pltpu.CompilerParams(vmem_limit_bytes=limit * MIB)


def cost(flops, size):
    return pl.CostEstimate(flops=int(flops), bytes_accessed=int(size), transcendentals=0)


def on_device(queries, keys, values, out_grad, level_codes):
    count, heads, width = queries.shape
    scale = width ** (-0.5)
    local_bits = bits_of(count)
    blocks = lax.axis_size("seq")
    tree_bits = bits_of(blocks)
    groups = lax.axis_size("head")
    here = lax.axis_index("seq")
    tile = min(256, count)
    chunks = count // tile
    half = heads // 2
    rows = local_bits + 1 + tree_bits

    def permute(x, apart):
        return lax.ppermute(x, "seq", [(i, i ^ apart) for i in range(blocks)])

    def in_hbm(*arrays):
        return [pltpu.with_memory_space_constraint(x, pltpu.HBM) for x in arrays]

    def near(*arrays):
        return [pltpu.with_memory_space_constraint(x, pltpu.VMEM) for x in arrays]

    pieces = 2 if tile % 256 == 0 else 1
    in_vmem = pl.BlockSpec(memory_space=pltpu.VMEM)
    anywhere = pl.BlockSpec(memory_space=pl.ANY)

    def chunk_block(*dims):
        return pl.BlockSpec((1,) + dims, lambda c: (c,) + (0,) * len(dims))

    def whole(*dims):
        return pl.BlockSpec(dims, lambda c: (0,) * len(dims))

    head_block = chunk_block(heads, tile, width)
    natural = pltpu.VMEM((chunks, heads, tile, width), BF16)
    square = (width, width)
    size = count * heads * width
    groups_in = len(level_sources(chunks))
    queries, keys, values, out_grad = in_hbm(queries, keys, values, out_grad)

    kh, vh, gh, qt, level_state, state, send_state = pl.pallas_call(
        functools.partial(states_kernel, pieces),
        grid=(chunks,),
        in_specs=[
            pl.BlockSpec((tile // pieces, heads, width), lambda c, n=n: (pieces * c + n, 0, 0))
            for _ in range(4)
            for n in range(pieces)
        ],
        out_specs=[
            *[head_block] * 3, chunk_block(heads, width, tile),
            whole(groups_in, heads, *square), whole(heads, *square), whole(half, *square),
        ],
        out_shape=[
            *[natural] * 3, pltpu.VMEM((chunks, heads, width, tile), BF16),
            pltpu.VMEM((groups_in, heads, *square), BF16), pltpu.VMEM((heads, *square), F32),
            pltpu.VMEM((half, *square), F32),
        ],
        scratch_shapes=[pltpu.VMEM((chunks, heads, *square), F32)],
        compiler_params=params(8),
        cost_estimate=cost(2 * size * width, 8 * size),
        name="states",
    )(*[x for x in (keys, values, queries, out_grad) for _ in range(pieces)])

    other_state = permute(send_state, 1)

    group = lax.axis_index("head")
    parts = [
        lax.ppermute(level_codes, "head", [(i, (i + r) % groups) for i in range(groups)])
        for r in range(1, groups)
    ]
    parts, state = lax.optimization_barrier((parts, state))
    parts = jnp.stack([level_codes, *parts])
    codes = jnp.concatenate(
        [
            lax.dynamic_index_in_dim(parts, (group - j) % groups, 0, keepdims=False)[:rows]
            for j in range(groups)
        ],
        axis=1,
    )
    order = jnp.arange(rows)
    factor = jnp.exp2(-0.5 * jnp.maximum(order.astype(F32) - 1.0, 0.0)) / 16.0
    on_bit = jnp.bitwise_and(jnp.right_shift(here, jnp.maximum(order - local_bits - 1, 0)), 1)
    factor = jnp.where(order > local_bits, factor * on_bit.astype(F32), factor)
    lam = codes.astype(F32) * (scale * factor)[:, None]

    kh, vh, qt, gh, level_state, state = near(kh, vh, qt, gh, level_state, state)

    def level_grads(own, before):
        inputs = [lam, qt, gh, state]
        return pl.pallas_call(
            functools.partial(grads_kernel, local_bits + 1, own),
            in_specs=[in_vmem] * len(inputs) + [anywhere] * len(before),
            out_specs=[in_vmem] * 2,
            out_shape=[pltpu.VMEM((n, *square), F32) for n in ((tree_bits - 1) * half, heads)],
            input_output_aliases={len(inputs): 1} if before else {},
            compiler_params=params(4),
            cost_estimate=cost(tree_bits * size * width, size),
            name="level_grads",
        )(*inputs, *before)

    send, everything = level_grads(False, [])
    send, other_state = lax.optimization_barrier((send, other_state))
    found = permute(send, 1)
    keep, everything = level_grads(True, near(everything))
    (keep,) = near(keep)
    hops = [1 << b | m for b in range(1, tree_bits) for m in range(0, 1 << b, 2)]
    hops.sort(key=lambda hop: (hop & hop - 1) == 0)
    messages = pl.pallas_call(
        functools.partial(pair_kernel, [bits_of(hop) for hop in hops]),
        in_specs=[in_vmem] * 4,
        out_specs=[in_vmem] * len(hops),
        out_shape=[pltpu.VMEM((half, *square), F32)] * len(hops),
        compiler_params=params(2),
        cost_estimate=cost(size, size),
        name="pair",
    )(state, other_state, keep, found)
    *messages, everything = lax.optimization_barrier((*messages, everything))
    arrived = [permute(x, hop) for hop, x in zip(hops, messages)]
    first = permute(everything, 1)
    *parts, gin = pl.pallas_call(
        local_kernel,
        in_specs=[in_vmem] * 7,
        out_specs=[in_vmem] * 4,
        out_shape=[natural] * 3 + [pltpu.VMEM((chunks, heads, *square), F32)],
        scratch_shapes=[pltpu.VMEM((tile, tile), F32), pltpu.VMEM((heads, *square), BF16)],
        compiler_params=params(3),
        cost_estimate=cost(14 * size * tile, 4 * size),
        name="local",
    )(lam, kh, vh, qt, gh, level_state, first)
    arrived, parts = lax.optimization_barrier((arrived, parts))
    sums_shape = (tree_bits - 1, half, *square)
    mine = pl.pallas_call(
        functools.partial(sum_kernel, [bits_of(hop) for hop in hops]),
        in_specs=[in_vmem] * len(hops),
        out_specs=in_vmem,
        out_shape=pltpu.VMEM(sums_shape, F32),
        compiler_params=params(2),
        cost_estimate=cost(size, size),
        name="sums",
    )(*arrived)
    others = permute(mine, 1)

    kept = [
        pltpu.VMEM((tree_bits - 1, tile, width), F32),
        pltpu.VMEM((half, (tree_bits - 1) * width, width), BF16),
        pltpu.VMEM((half, *square), F32),
    ]
    gin, mine = near(gin, mine)
    parts = pl.pallas_call(
        functools.partial(own_half_kernel, local_bits + 2),
        in_specs=[in_vmem] * 9,
        out_specs=[in_vmem] * 3,
        out_shape=[natural] * 3,
        input_output_aliases={6: 0, 7: 1, 8: 2},
        scratch_shapes=kept,
        compiler_params=params(3),
        cost_estimate=cost((tree_bits + 2) * size * width, 8 * size),
        name="own_half",
    )(lam, kh, vh, gh, gin, mine, *near(*parts))
    others, parts = lax.optimization_barrier((others, parts))
    return pl.pallas_call(
        functools.partial(final_kernel, local_bits + 2),
        in_specs=[in_vmem] * 9,
        out_specs=[anywhere] * 3,
        out_shape=[pltpu.HBM((count, heads, width), BF16)] * 3,
        scratch_shapes=[
            pltpu.VMEM((3, chunks, tile, heads, width), BF16), *kept,
            pltpu.SemaphoreType.DMA((3, chunks, pieces)),
        ],
        compiler_params=params(10),
        cost_estimate=cost((tree_bits + 2) * size * width, 16 * size),
        name="final",
    )(lam, kh, vh, gh, *near(*parts), gin, others)


def solution(mesh):
    tokens = P("seq", "head", None)
    return jax.shard_map(
        on_device,
        mesh=mesh,
        in_specs=(tokens, tokens, tokens, tokens, P(None, ("seq", "head"))),
        out_specs=(tokens, tokens, tokens),
        check_vma=False,
    )
```

```python
import functools

import jax
import jax.numpy as jnp
from jax import lax
from jax.experimental import pallas as pl
from jax.experimental.pallas import tpu as pltpu
from jax.sharding import PartitionSpec as P

F32 = jnp.float32
BF16 = jnp.bfloat16
MIB = 1 << 20


def bits_of(size):
    return size.bit_length() - 1


def dot(a, b):
    return jnp.dot(a, b, preferred_element_type=F32)


def dot_nt(a, b):
    return lax.dot_general(a, b, (((1,), (1,)), ((), ())), preferred_element_type=F32)


def scaled(row, x):
    return (row * x.astype(F32)).astype(BF16)


def stack_levels(parts, axis):
    return parts[0] if len(parts) == 1 else jnp.concatenate(parts, axis=axis)


def level_sources(chunks):
    found = []
    for j in range(bits_of(chunks)):
        for first in range(0, chunks, 2 << j):
            found.append(range(first, first + (1 << j)))
    return found


def bit_of_block(b):
    return jnp.bitwise_and(jnp.right_shift(lax.axis_index("seq"), b), 1)


def states_kernel(pieces, *refs):
    inputs = [refs[n * pieces : (n + 1) * pieces] for n in range(4)]
    kh_ref, vh_ref, gh_ref, qt_ref, level_ref, total_ref, chunk_ref = refs[4 * pieces :]
    heads = kh_ref.shape[1]
    size = kh_ref.shape[2] // pieces
    chunks = chunk_ref.shape[0]
    step = pl.program_id(0)
    for n, (k_ref, v_ref, q_ref, g_ref) in enumerate(zip(*inputs)):
        span = slice(n * size, (n + 1) * size)
        kh_ref[0, :, span] = jnp.swapaxes(k_ref[...], 0, 1)
        vh_ref[0, :, span] = jnp.swapaxes(v_ref[...], 0, 1)
        gh_ref[0, :, span] = jnp.swapaxes(g_ref[...], 0, 1)
        queries = jnp.swapaxes(q_ref[...], 0, 1)
        for h in range(heads):
            qt_ref[0, h, :, span] = queries[h].T
    for h in range(heads):
        chunk_ref[step, h] = dot(kh_ref[0, h].T, vh_ref[0, h])

    @pl.when(step == chunks - 1)
    def _():
        for h in range(heads):
            tiles = [chunk_ref[i, h] for i in range(chunks)]
            total_ref[h] = functools.reduce(jnp.add, tiles)
            for n, sources in enumerate(level_sources(chunks)):
                state = functools.reduce(jnp.add, [tiles[i] for i in sources])
                level_ref[n, h] = state.astype(BF16)


def grads_kernel(first_row, own, lam_ref, qt_ref, g_ref, state_ref, sums_ref, *whole_refs):
    chunks, heads, tile, width = g_ref.shape
    half = heads // 2
    levels = lam_ref.shape[0] - first_row

    def level_grad(h, low, high):
        weighted = [
            stack_levels(
                [
                    scaled(
                        lam_ref[first_row + b : first_row + b + 1, c * tile : (c + 1) * tile],
                        qt_ref[c, h],
                    )
                    for b in range(low, high)
                ],
                0,
            )
            for c in range(chunks)
        ]
        grad = dot(stack_levels(weighted, 1), g_ref[:, h].reshape(chunks * tile, width))
        return [grad[i * width : (i + 1) * width] for i in range(high - low)]

    for core in range(2):

        @pl.when(bit_of_block(0) == core)
        def _():
            for h in range(heads):
                chosen = (h // half == core) == own
                low = 0 if own and core == 1 else 1
                parts = level_grad(h, low, levels if chosen else 1) if chosen or low == 0 else []
                if own:
                    whole_refs[0][h] = state_ref[h] if core == 0 else parts[0]
                if chosen:
                    for b, part in enumerate([state_ref[h], *parts[1 - low :]]):
                        sums_ref[b * half + h % half] = part


def make_mask(lam_ref, span, mask_ref):
    tile = mask_ref.shape[0]
    part = min(128, tile)
    source = lax.broadcasted_iota(jnp.int32, (part, part), 0)
    target = lax.broadcasted_iota(jnp.int32, (part, part), 1)
    differ = jnp.where(source <= target, jnp.bitwise_xor(source, target), -1)
    for to in range(0, tile, part):
        lanes = slice(span.start + to, span.start + to + part)
        mask = jnp.where(differ >= 0, lam_ref[0:1, lanes], 0.0)
        for power in range(bits_of(part)):
            mask = jnp.where(differ >= 1 << power, lam_ref[power + 1 : power + 2, lanes], mask)
        mask_ref[to : to + part, to : to + part] = mask
        for at in range(0, tile, part):
            if at < to:
                level = bits_of(at ^ to) + 1
                row = lam_ref[level : level + 1, lanes]
                mask_ref[at : at + part, to : to + part] = jnp.broadcast_to(row, (part, part))
            elif at > to:
                mask_ref[at : at + part, to : to + part] = jnp.zeros((part, part), F32)


def diagonal_tile(key, value, query_t, grad, mask):
    weight_q = (mask * dot_nt(value, grad)).astype(BF16)
    weight_v = (mask * dot(key, query_t)).astype(BF16)
    dk = dot_nt(weight_q, query_t).astype(BF16)
    dv = dot(weight_v, grad).astype(BF16)
    return dot(key.T, weight_q), dk, dv


def local_kernel(
    lam_ref, k_ref, v_ref, qt_ref, g_ref, level_ref, found_ref,
    dq_ref, dk_ref, dv_ref, gin_ref, mask_ref, half_ref,
):
    chunks, heads, tile, width = k_ref.shape
    tile_bits = bits_of(tile)
    first_row = tile_bits + bits_of(chunks) + 1
    groups = level_sources(chunks)
    off = (1 - bit_of_block(0)).astype(F32)

    @pl.loop(0, heads, unroll=4)
    def _(h):
        found = found_ref[h]
        half_ref[h] = found.astype(BF16)
        for i in range(chunks):
            gin_ref[i, h] = off * found

    for c in range(chunks):
        span = slice(c * tile, (c + 1) * tile)
        make_mask(lam_ref, span, mask_ref)

        @pl.loop(0, heads, unroll=4)
        def _(h):
            query_t, grad = qt_ref[c, h], g_ref[c, h]
            dqt, dk_ref[c, h], dv_ref[c, h] = diagonal_tile(
                k_ref[c, h], v_ref[c, h], query_t, grad, mask_ref[...]
            )
            dqt = dqt + lam_ref[first_row : first_row + 1, span] * dot_nt(half_ref[h], grad)
            for j in range(bits_of(chunks)):
                if c >> j & 1:
                    row = lam_ref[tile_bits + 1 + j : tile_bits + 2 + j, span]
                    first = (c >> j ^ 1) << j
                    sources = range(first, first + (1 << j))
                    dqt = dqt + row * dot_nt(level_ref[groups.index(sources), h], grad)
                    part = dot(scaled(row, query_t), grad)
                    for i in sources:
                        gin_ref[i, h] = gin_ref[i, h] + part
            dq_ref[c, h] = dqt.astype(BF16).T


def pair_kernel(levels, keep_ref, found_ref, *out_refs):
    half = out_refs[0].shape[0]
    for b, out_ref in zip(levels, out_refs):
        for on in range(2):

            @pl.when(bit_of_block(b) == on)
            def _():
                for i in range(half):
                    spot = b * on * half + i
                    out_ref[i] = keep_ref[spot] + found_ref[spot]


def sum_kernel(levels, *refs):
    out_ref = refs[-1]
    for n in range(out_ref.shape[0]):
        for i in range(out_ref.shape[1]):
            parts = [ref[i] for b, ref in zip(levels, refs) if b == n + 1]
            out_ref[n, i] = functools.reduce(jnp.add, parts)


def widen(lam_ref, first_row, lanes, wide_ref):
    for b in range(wide_ref.shape[0]):
        row = lam_ref[first_row + b : first_row + b + 1, lanes]
        wide_ref[b] = jnp.broadcast_to(row, wide_ref.shape[:0:-1]).T


def received(sums_ref, i):
    parts = [sums_ref[b, i] for b in range(sums_ref.shape[0])]
    off = [(1 - bit_of_block(b + 1)).astype(F32) for b in range(len(parts))]
    state = functools.reduce(jnp.add, [w * part for w, part in zip(off, parts)])
    return stack_levels([part.astype(BF16) for part in parts], 0), state


def add_to_query(half, wide_ref, grad, dq):
    width = grad.shape[1]
    dq = dq.astype(F32)
    projected = dot_nt(grad, half)
    for b in range(wide_ref.shape[0]):
        dq = dq + wide_ref[b] * projected[:, b * width : (b + 1) * width]
    return dq.astype(BF16)


def add_to_key_value(state, key, value, dk, dv):
    width = key.shape[1]
    state = state.astype(BF16)
    none = jnp.zeros((width, width), BF16)
    right = jnp.concatenate(
        [
            jnp.concatenate([state.T, none], axis=1),
            jnp.concatenate([none, state], axis=1),
        ],
        axis=0,
    )
    product = dot(jnp.concatenate([value, key], axis=1), right)
    dk = dk.astype(F32) + product[:, :width]
    dv = dv.astype(F32) + product[:, width:]
    return dk.astype(BF16), dv.astype(BF16)


def own_half_kernel(
    first_row, lam_ref, k_ref, v_ref, g_ref, gin_ref, sums_ref, dq_in, dk_in, dv_in,
    dq_ref, dk_ref, dv_ref, wide_ref, half_ref, state_ref,
):
    chunks, _, tile, _ = k_ref.shape
    half = half_ref.shape[0]
    start = bit_of_block(0) * half
    for i in range(half):
        half_ref[i], state_ref[i] = received(sums_ref, i)
    for c in range(chunks):
        widen(lam_ref, first_row, slice(c * tile, (c + 1) * tile), wide_ref)
        for i in range(half):
            h = start + i
            dq_ref[c, h] = add_to_query(half_ref[i], wide_ref, g_ref[c, h], dq_in[c, h])
            dk_ref[c, h], dv_ref[c, h] = add_to_key_value(
                gin_ref[c, h] + state_ref[i], k_ref[c, h], v_ref[c, h], dk_in[c, h], dv_in[c, h]
            )


def final_kernel(
    first_row, lam_ref, k_ref, v_ref, g_ref, dq_in, dk_in, dv_in, gin_ref, sums_ref,
    dq_out, dk_out, dv_out, done_ref, wide_ref, half_ref, state_ref, sems,
):
    chunks, heads, tile, _ = k_ref.shape
    half = half_ref.shape[0]
    outs = (dq_out, dk_out, dv_out)

    pieces = sems.shape[2]
    size = tile // pieces

    def ship(n, c):
        return [
            pltpu.make_async_copy(
                done_ref.at[n, c, pl.ds(i * size, size)],
                outs[n].at[pl.ds(c * tile + i * size, size)],
                sems.at[n, c, i],
            )
            for i in range(pieces)
        ]

    for i in range(half):
        half_ref[i], state_ref[i] = received(sums_ref, i)
    for core in range(2):

        @pl.when(bit_of_block(0) == core)
        def _():
            for c in range(chunks):
                widen(lam_ref, first_row, slice(c * tile, (c + 1) * tile), wide_ref)
                queries, keys, values = [], [], []
                for h in range(heads):
                    query, key, value = dq_in[c, h], dk_in[c, h], dv_in[c, h]
                    if h // half != core:
                        i = h % half
                        query = add_to_query(half_ref[i], wide_ref, g_ref[c, h], query)
                        key, value = add_to_key_value(
                            gin_ref[c, h] + state_ref[i], k_ref[c, h], v_ref[c, h], key, value
                        )
                    queries.append(query)
                    keys.append(key)
                    values.append(value)
                for n, parts in enumerate((queries, keys, values)):
                    done_ref[n, c] = jnp.swapaxes(jnp.stack(parts), 0, 1)
                    for copy in ship(n, c):
                        copy.start()

    for c in range(chunks):
        for n in range(3):
            for copy in ship(n, c):
                copy.wait()


def shape(dims, dtype):
    return jax.ShapeDtypeStruct(dims, dtype)


def params(limit):
    return pltpu.CompilerParams(vmem_limit_bytes=limit * MIB)


def cost(flops, size):
    return pl.CostEstimate(flops=int(flops), bytes_accessed=int(size), transcendentals=0)


def on_device(queries, keys, values, out_grad, level_codes):
    count, heads, width = queries.shape
    scale = width ** (-0.5)
    local_bits = bits_of(count)
    blocks = lax.axis_size("seq")
    tree_bits = bits_of(blocks)
    groups = lax.axis_size("head")
    here = lax.axis_index("seq")
    tile = min(256, count)
    chunks = count // tile
    half = heads // 2
    rows = local_bits + 1 + tree_bits

    def permute(x, apart):
        return lax.ppermute(x, "seq", [(i, i ^ apart) for i in range(blocks)])

    def in_hbm(*arrays):
        return [pltpu.with_memory_space_constraint(x, pltpu.HBM) for x in arrays]

    def near(*arrays):
        return [pltpu.with_memory_space_constraint(x, pltpu.VMEM) for x in arrays]

    pieces = 2 if tile % 256 == 0 else 1
    in_vmem = pl.BlockSpec(memory_space=pltpu.VMEM)
    anywhere = pl.BlockSpec(memory_space=pl.ANY)

    def chunk_block(*dims):
        return pl.BlockSpec((1,) + dims, lambda c: (c,) + (0,) * len(dims))

    def whole(*dims):
        return pl.BlockSpec(dims, lambda c: (0,) * len(dims))

    head_block = chunk_block(heads, tile, width)
    natural = pltpu.VMEM((chunks, heads, tile, width), BF16)
    square = (width, width)
    size = count * heads * width
    groups_in = len(level_sources(chunks))
    queries, keys, values, out_grad = in_hbm(queries, keys, values, out_grad)

    kh, vh, gh, qt, level_state, state = pl.pallas_call(
        functools.partial(states_kernel, pieces),
        grid=(chunks,),
        in_specs=[
            pl.BlockSpec((tile // pieces, heads, width), lambda c, n=n: (pieces * c + n, 0, 0))
            for _ in range(4)
            for n in range(pieces)
        ],
        out_specs=[
            *[head_block] * 3, chunk_block(heads, width, tile),
            whole(groups_in, heads, *square), whole(heads, *square),
        ],
        out_shape=[
            *[natural] * 3, pltpu.VMEM((chunks, heads, width, tile), BF16),
            pltpu.VMEM((groups_in, heads, *square), BF16), pltpu.VMEM((heads, *square), F32),
        ],
        scratch_shapes=[pltpu.VMEM((chunks, heads, *square), F32)],
        compiler_params=params(8),
        cost_estimate=cost(2 * size * width, 8 * size),
        name="states",
    )(*[x for x in (keys, values, queries, out_grad) for _ in range(pieces)])

    group = lax.axis_index("head")
    parts = [
        lax.ppermute(level_codes, "head", [(i, (i + r) % groups) for i in range(groups)])
        for r in range(1, groups)
    ]
    parts, state = lax.optimization_barrier((parts, state))
    parts = jnp.stack([level_codes, *parts])
    codes = jnp.concatenate(
        [
            lax.dynamic_index_in_dim(parts, (group - j) % groups, 0, keepdims=False)[:rows]
            for j in range(groups)
        ],
        axis=1,
    )
    order = jnp.arange(rows)
    factor = jnp.exp2(-0.5 * jnp.maximum(order.astype(F32) - 1.0, 0.0)) / 16.0
    on_bit = jnp.bitwise_and(jnp.right_shift(here, jnp.maximum(order - local_bits - 1, 0)), 1)
    factor = jnp.where(order > local_bits, factor * on_bit.astype(F32), factor)
    lam = codes.astype(F32) * (scale * factor)[:, None]

    kh, vh, qt, gh, level_state, state = near(kh, vh, qt, gh, level_state, state)

    def level_grads(own):
        inputs = [lam, qt, gh, state]
        sizes = (tree_bits * half, heads) if own else (tree_bits * half,)
        return pl.pallas_call(
            functools.partial(grads_kernel, local_bits + 1, own),
            in_specs=[in_vmem] * len(inputs),
            out_specs=[in_vmem] * len(sizes),
            out_shape=[pltpu.VMEM((n, *square), F32) for n in sizes],
            compiler_params=params(4),
            cost_estimate=cost(tree_bits * size * width, size),
            name="level_grads",
        )(*inputs)

    (send,) = level_grads(False)
    found = permute(send, 1)
    keep, everything = level_grads(True)
    (keep,) = near(keep)
    hops = [1 << b | m for b in range(1, tree_bits) for m in range(0, 1 << b, 2)]
    hops.sort(key=lambda hop: (hop & hop - 1) == 0)
    messages = pl.pallas_call(
        functools.partial(pair_kernel, [bits_of(hop) for hop in hops]),
        in_specs=[in_vmem] * 2,
        out_specs=[in_vmem] * len(hops),
        out_shape=[pltpu.VMEM((half, *square), F32)] * len(hops),
        compiler_params=params(2),
        cost_estimate=cost(size, size),
        name="pair",
    )(keep, found)
    *messages, everything = lax.optimization_barrier((*messages, everything))
    arrived = [permute(x, hop) for hop, x in zip(hops, messages)]
    first = permute(everything, 1)
    *parts, gin = pl.pallas_call(
        local_kernel,
        in_specs=[in_vmem] * 7,
        out_specs=[in_vmem] * 4,
        out_shape=[natural] * 3 + [pltpu.VMEM((chunks, heads, *square), F32)],
        scratch_shapes=[pltpu.VMEM((tile, tile), F32), pltpu.VMEM((heads, *square), BF16)],
        compiler_params=params(3),
        cost_estimate=cost(14 * size * tile, 4 * size),
        name="local",
    )(lam, kh, vh, qt, gh, level_state, first)
    arrived, parts = lax.optimization_barrier((arrived, parts))
    sums_shape = (tree_bits - 1, half, *square)
    mine = pl.pallas_call(
        functools.partial(sum_kernel, [bits_of(hop) for hop in hops]),
        in_specs=[in_vmem] * len(hops),
        out_specs=in_vmem,
        out_shape=pltpu.VMEM(sums_shape, F32),
        compiler_params=params(2),
        cost_estimate=cost(size, size),
        name="sums",
    )(*arrived)
    others = permute(mine, 1)

    kept = [
        pltpu.VMEM((tree_bits - 1, tile, width), F32),
        pltpu.VMEM((half, (tree_bits - 1) * width, width), BF16),
        pltpu.VMEM((half, *square), F32),
    ]
    gin, mine = near(gin, mine)
    parts = pl.pallas_call(
        functools.partial(own_half_kernel, local_bits + 2),
        in_specs=[in_vmem] * 9,
        out_specs=[in_vmem] * 3,
        out_shape=[natural] * 3,
        input_output_aliases={6: 0, 7: 1, 8: 2},
        scratch_shapes=kept,
        compiler_params=params(3),
        cost_estimate=cost((tree_bits + 2) * size * width, 8 * size),
        name="own_half",
    )(lam, kh, vh, gh, gin, mine, *near(*parts))
    others, parts = lax.optimization_barrier((others, parts))
    return pl.pallas_call(
        functools.partial(final_kernel, local_bits + 2),
        in_specs=[in_vmem] * 9,
        out_specs=[anywhere] * 3,
        out_shape=[pltpu.HBM((count, heads, width), BF16)] * 3,
        scratch_shapes=[
            pltpu.VMEM((3, chunks, tile, heads, width), BF16), *kept,
            pltpu.SemaphoreType.DMA((3, chunks, pieces)),
        ],
        compiler_params=params(10),
        cost_estimate=cost((tree_bits + 2) * size * width, 16 * size),
        name="final",
    )(lam, kh, vh, gh, *near(*parts), gin, others)


def solution(mesh):
    tokens = P("seq", "head", None)
    return jax.shard_map(
        on_device,
        mesh=mesh,
        in_specs=(tokens, tokens, tokens, tokens, P(None, ("seq", "head"))),
        out_specs=(tokens, tokens, tokens),
        check_vma=False,
    )
```

```python
import functools

import jax
import jax.numpy as jnp
from jax import lax
from jax.experimental import pallas as pl
from jax.experimental.pallas import tpu as pltpu
from jax.sharding import PartitionSpec as P

F32 = jnp.float32
BF16 = jnp.bfloat16
MIB = 1 << 20


def bits_of(size):
    return size.bit_length() - 1


def dot(a, b):
    return jnp.dot(a, b, preferred_element_type=F32)


def dot_nt(a, b):
    return lax.dot_general(a, b, (((1,), (1,)), ((), ())), preferred_element_type=F32)


def scaled(row, x):
    return (row * x.astype(F32)).astype(BF16)


def stack_levels(parts, axis):
    return parts[0] if len(parts) == 1 else jnp.concatenate(parts, axis=axis)


def level_sources(chunks):
    found = []
    for j in range(bits_of(chunks)):
        for first in range(0, chunks, 2 << j):
            found.append(range(first, first + (1 << j)))
    return found


def bit_of_block(b):
    return jnp.bitwise_and(jnp.right_shift(lax.axis_index("seq"), b), 1)


def states_kernel(pieces, *refs):
    inputs = [refs[n * pieces : (n + 1) * pieces] for n in range(4)]
    kh_ref, vh_ref, gh_ref, qt_ref, level_ref, total_ref, chunk_ref = refs[4 * pieces :]
    heads = kh_ref.shape[1]
    size = kh_ref.shape[2] // pieces
    chunks = chunk_ref.shape[0]
    step = pl.program_id(0)
    for n, (k_ref, v_ref, q_ref, g_ref) in enumerate(zip(*inputs)):
        span = slice(n * size, (n + 1) * size)
        kh_ref[0, :, span] = jnp.swapaxes(k_ref[...], 0, 1)
        vh_ref[0, :, span] = jnp.swapaxes(v_ref[...], 0, 1)
        gh_ref[0, :, span] = jnp.swapaxes(g_ref[...], 0, 1)
        queries = jnp.swapaxes(q_ref[...], 0, 1)
        for h in range(heads):
            qt_ref[0, h, :, span] = queries[h].T
    for h in range(heads):
        chunk_ref[step, h] = dot(kh_ref[0, h].T, vh_ref[0, h])

    @pl.when(step == chunks - 1)
    def _():
        for h in range(heads):
            tiles = [chunk_ref[i, h] for i in range(chunks)]
            total_ref[h] = functools.reduce(jnp.add, tiles)
            for n, sources in enumerate(level_sources(chunks)):
                state = functools.reduce(jnp.add, [tiles[i] for i in sources])
                level_ref[n, h] = state.astype(BF16)


def grads_kernel(first_row, own, lam_ref, qt_ref, g_ref, state_ref, sums_ref, *whole_refs):
    chunks, heads, tile, width = g_ref.shape
    half = heads // 2
    levels = lam_ref.shape[0] - first_row

    def level_grad(h, low, high):
        weighted = [
            stack_levels(
                [
                    scaled(
                        lam_ref[first_row + b : first_row + b + 1, c * tile : (c + 1) * tile],
                        qt_ref[c, h],
                    )
                    for b in range(low, high)
                ],
                0,
            )
            for c in range(chunks)
        ]
        grad = dot(stack_levels(weighted, 1), g_ref[:, h].reshape(chunks * tile, width))
        return [grad[i * width : (i + 1) * width] for i in range(high - low)]

    for core in range(2):

        @pl.when(bit_of_block(0) == core)
        def _():
            for h in range(heads):
                chosen = (h // half == core) == own
                low = 0 if own and core == 1 else 1
                parts = level_grad(h, low, levels if chosen else 1) if chosen or low == 0 else []
                if own:
                    whole_refs[0][h] = state_ref[h] if core == 0 else parts[0]
                if chosen:
                    for b, part in enumerate([state_ref[h], *parts[1 - low :]]):
                        sums_ref[b * half + h % half] = part


def make_mask(lam_ref, span, mask_ref):
    tile = mask_ref.shape[0]
    part = min(128, tile)
    source = lax.broadcasted_iota(jnp.int32, (part, part), 0)
    target = lax.broadcasted_iota(jnp.int32, (part, part), 1)
    differ = jnp.where(source <= target, jnp.bitwise_xor(source, target), -1)
    for to in range(0, tile, part):
        lanes = slice(span.start + to, span.start + to + part)
        mask = jnp.where(differ >= 0, lam_ref[0:1, lanes], 0.0)
        for power in range(bits_of(part)):
            mask = jnp.where(differ >= 1 << power, lam_ref[power + 1 : power + 2, lanes], mask)
        mask_ref[to : to + part, to : to + part] = mask
        for at in range(0, tile, part):
            if at < to:
                level = bits_of(at ^ to) + 1
                row = lam_ref[level : level + 1, lanes]
                mask_ref[at : at + part, to : to + part] = jnp.broadcast_to(row, (part, part))
            elif at > to:
                mask_ref[at : at + part, to : to + part] = jnp.zeros((part, part), F32)


def diagonal_tile(key, value, query_t, grad, mask):
    weight_q = (mask * dot_nt(value, grad)).astype(BF16)
    weight_v = (mask * dot(key, query_t)).astype(BF16)
    dk = dot_nt(weight_q, query_t).astype(BF16)
    dv = dot(weight_v, grad).astype(BF16)
    return dot(key.T, weight_q), dk, dv


def local_kernel(
    lam_ref, k_ref, v_ref, qt_ref, g_ref, level_ref, found_ref,
    dq_ref, dk_ref, dv_ref, gin_ref, mask_ref, half_ref,
):
    chunks, heads, tile, width = k_ref.shape
    tile_bits = bits_of(tile)
    first_row = tile_bits + bits_of(chunks) + 1
    groups = level_sources(chunks)
    off = (1 - bit_of_block(0)).astype(F32)

    @pl.loop(0, heads, unroll=4)
    def _(h):
        found = found_ref[h]
        half_ref[h] = found.astype(BF16)
        for i in range(chunks):
            gin_ref[i, h] = off * found

    for c in range(chunks):
        span = slice(c * tile, (c + 1) * tile)
        make_mask(lam_ref, span, mask_ref)

        @pl.loop(0, heads, unroll=4)
        def _(h):
            query_t, grad = qt_ref[c, h], g_ref[c, h]
            dqt, dk_ref[c, h], dv_ref[c, h] = diagonal_tile(
                k_ref[c, h], v_ref[c, h], query_t, grad, mask_ref[...]
            )
            dqt = dqt + lam_ref[first_row : first_row + 1, span] * dot_nt(half_ref[h], grad)
            for j in range(bits_of(chunks)):
                if c >> j & 1:
                    row = lam_ref[tile_bits + 1 + j : tile_bits + 2 + j, span]
                    first = (c >> j ^ 1) << j
                    sources = range(first, first + (1 << j))
                    dqt = dqt + row * dot_nt(level_ref[groups.index(sources), h], grad)
                    part = dot(scaled(row, query_t), grad)
                    for i in sources:
                        gin_ref[i, h] = gin_ref[i, h] + part
            dq_ref[c, h] = dqt.astype(BF16).T


def pair_kernel(levels, keep_ref, found_ref, *out_refs):
    half = out_refs[0].shape[0]
    for b, out_ref in zip(levels, out_refs):
        for on in range(2):

            @pl.when(bit_of_block(b) == on)
            def _():
                for i in range(half):
                    spot = b * on * half + i
                    out_ref[i] = keep_ref[spot] + found_ref[spot]


def sum_kernel(levels, *refs):
    out_ref = refs[-1]
    for n in range(out_ref.shape[0]):
        for i in range(out_ref.shape[1]):
            parts = [ref[i] for b, ref in zip(levels, refs) if b == n + 1]
            out_ref[n, i] = functools.reduce(jnp.add, parts)


def widen(lam_ref, first_row, lanes, wide_ref):
    for b in range(wide_ref.shape[0]):
        row = lam_ref[first_row + b : first_row + b + 1, lanes]
        wide_ref[b] = jnp.broadcast_to(row, wide_ref.shape[:0:-1]).T


def received(sums_ref, i):
    parts = [sums_ref[b, i] for b in range(sums_ref.shape[0])]
    off = [(1 - bit_of_block(b + 1)).astype(F32) for b in range(len(parts))]
    state = functools.reduce(jnp.add, [w * part for w, part in zip(off, parts)])
    return stack_levels([part.astype(BF16) for part in parts], 0), state


def add_to_query(half, wide_ref, grad, dq):
    width = grad.shape[1]
    dq = dq.astype(F32)
    projected = dot_nt(grad, half)
    for b in range(wide_ref.shape[0]):
        dq = dq + wide_ref[b] * projected[:, b * width : (b + 1) * width]
    return dq.astype(BF16)


def add_to_key_value(state, key, value, dk, dv):
    width = key.shape[1]
    state = state.astype(BF16)
    none = jnp.zeros((width, width), BF16)
    right = jnp.concatenate(
        [
            jnp.concatenate([state.T, none], axis=1),
            jnp.concatenate([none, state], axis=1),
        ],
        axis=0,
    )
    product = dot(jnp.concatenate([value, key], axis=1), right)
    dk = dk.astype(F32) + product[:, :width]
    dv = dv.astype(F32) + product[:, width:]
    return dk.astype(BF16), dv.astype(BF16)


def own_half_kernel(
    first_row, lam_ref, k_ref, v_ref, g_ref, gin_ref, sums_ref, dq_in, dk_in, dv_in,
    dq_ref, dk_ref, dv_ref, wide_ref, half_ref, state_ref,
):
    chunks, _, tile, _ = k_ref.shape
    half = half_ref.shape[0]
    start = bit_of_block(0) * half
    for i in range(half):
        half_ref[i], state_ref[i] = received(sums_ref, i)
    for c in range(chunks):
        widen(lam_ref, first_row, slice(c * tile, (c + 1) * tile), wide_ref.at[c])
        for i in range(half):
            h = start + i
            dq_ref[c, h] = add_to_query(half_ref[i], wide_ref.at[c], g_ref[c, h], dq_in[c, h])
            dk_ref[c, h], dv_ref[c, h] = add_to_key_value(
                gin_ref[c, h] + state_ref[i], k_ref[c, h], v_ref[c, h], dk_in[c, h], dv_in[c, h]
            )


def final_kernel(
    wide_ref, k_ref, v_ref, g_ref, dq_in, dk_in, dv_in, gin_ref, sums_ref,
    dq_out, dk_out, dv_out, done_ref, half_ref, state_ref, sems,
):
    chunks, heads, tile, _ = k_ref.shape
    half = half_ref.shape[0]
    outs = (dq_out, dk_out, dv_out)

    pieces = sems.shape[2]
    size = tile // pieces

    def ship(n, c):
        return [
            pltpu.make_async_copy(
                done_ref.at[n, c, pl.ds(i * size, size)],
                outs[n].at[pl.ds(c * tile + i * size, size)],
                sems.at[n, c, i],
            )
            for i in range(pieces)
        ]

    for i in range(half):
        half_ref[i], state_ref[i] = received(sums_ref, i)
    for core in range(2):

        @pl.when(bit_of_block(0) == core)
        def _():
            for c in range(chunks):
                queries, keys, values = [], [], []
                for h in range(heads):
                    query, key, value = dq_in[c, h], dk_in[c, h], dv_in[c, h]
                    if h // half != core:
                        i = h % half
                        query = add_to_query(half_ref[i], wide_ref.at[c], g_ref[c, h], query)
                        key, value = add_to_key_value(
                            gin_ref[c, h] + state_ref[i], k_ref[c, h], v_ref[c, h], key, value
                        )
                    queries.append(query)
                    keys.append(key)
                    values.append(value)
                for n, parts in enumerate((queries, keys, values)):
                    done_ref[n, c] = jnp.swapaxes(jnp.stack(parts), 0, 1)
                    for copy in ship(n, c):
                        copy.start()

    for c in range(chunks):
        for n in range(3):
            for copy in ship(n, c):
                copy.wait()


def shape(dims, dtype):
    return jax.ShapeDtypeStruct(dims, dtype)


def params(limit):
    return pltpu.CompilerParams(vmem_limit_bytes=limit * MIB)


def cost(flops, size):
    return pl.CostEstimate(flops=int(flops), bytes_accessed=int(size), transcendentals=0)


def on_device(queries, keys, values, out_grad, level_codes):
    count, heads, width = queries.shape
    scale = width ** (-0.5)
    local_bits = bits_of(count)
    blocks = lax.axis_size("seq")
    tree_bits = bits_of(blocks)
    groups = lax.axis_size("head")
    here = lax.axis_index("seq")
    tile = min(256, count)
    chunks = count // tile
    half = heads // 2
    rows = local_bits + 1 + tree_bits

    def permute(x, apart):
        return lax.ppermute(x, "seq", [(i, i ^ apart) for i in range(blocks)])

    def in_hbm(*arrays):
        return [pltpu.with_memory_space_constraint(x, pltpu.HBM) for x in arrays]

    def near(*arrays):
        return [pltpu.with_memory_space_constraint(x, pltpu.VMEM) for x in arrays]

    pieces = 2 if tile % 256 == 0 else 1
    in_vmem = pl.BlockSpec(memory_space=pltpu.VMEM)
    anywhere = pl.BlockSpec(memory_space=pl.ANY)

    def chunk_block(*dims):
        return pl.BlockSpec((1,) + dims, lambda c: (c,) + (0,) * len(dims))

    def whole(*dims):
        return pl.BlockSpec(dims, lambda c: (0,) * len(dims))

    head_block = chunk_block(heads, tile, width)
    natural = pltpu.VMEM((chunks, heads, tile, width), BF16)
    square = (width, width)
    size = count * heads * width
    groups_in = len(level_sources(chunks))
    queries, keys, values, out_grad = in_hbm(queries, keys, values, out_grad)

    kh, vh, gh, qt, level_state, state = pl.pallas_call(
        functools.partial(states_kernel, pieces),
        grid=(chunks,),
        in_specs=[
            pl.BlockSpec((tile // pieces, heads, width), lambda c, n=n: (pieces * c + n, 0, 0))
            for _ in range(4)
            for n in range(pieces)
        ],
        out_specs=[
            *[head_block] * 3, chunk_block(heads, width, tile),
            whole(groups_in, heads, *square), whole(heads, *square),
        ],
        out_shape=[
            *[natural] * 3, pltpu.VMEM((chunks, heads, width, tile), BF16),
            pltpu.VMEM((groups_in, heads, *square), BF16), pltpu.VMEM((heads, *square), F32),
        ],
        scratch_shapes=[pltpu.VMEM((chunks, heads, *square), F32)],
        compiler_params=params(8),
        cost_estimate=cost(2 * size * width, 8 * size),
        name="states",
    )(*[x for x in (keys, values, queries, out_grad) for _ in range(pieces)])

    group = lax.axis_index("head")
    parts = [
        lax.ppermute(level_codes, "head", [(i, (i + r) % groups) for i in range(groups)])
        for r in range(1, groups)
    ]
    parts, state = lax.optimization_barrier((parts, state))
    parts = jnp.stack([level_codes, *parts])
    codes = jnp.concatenate(
        [
            lax.dynamic_index_in_dim(parts, (group - j) % groups, 0, keepdims=False)[:rows]
            for j in range(groups)
        ],
        axis=1,
    )
    order = jnp.arange(rows)
    factor = jnp.exp2(-0.5 * jnp.maximum(order.astype(F32) - 1.0, 0.0)) / 16.0
    on_bit = jnp.bitwise_and(jnp.right_shift(here, jnp.maximum(order - local_bits - 1, 0)), 1)
    factor = jnp.where(order > local_bits, factor * on_bit.astype(F32), factor)
    lam = codes.astype(F32) * (scale * factor)[:, None]

    kh, vh, qt, gh, level_state, state = near(kh, vh, qt, gh, level_state, state)

    def level_grads(own):
        inputs = [lam, qt, gh, state]
        sizes = (tree_bits * half, heads) if own else (tree_bits * half,)
        return pl.pallas_call(
            functools.partial(grads_kernel, local_bits + 1, own),
            in_specs=[in_vmem] * len(inputs),
            out_specs=[in_vmem] * len(sizes),
            out_shape=[pltpu.VMEM((n, *square), F32) for n in sizes],
            compiler_params=params(4),
            cost_estimate=cost(tree_bits * size * width, size),
            name="level_grads",
        )(*inputs)

    (send,) = level_grads(False)
    found = permute(send, 1)
    keep, everything = level_grads(True)
    (keep,) = near(keep)
    hops = [1 << b | m for b in range(1, tree_bits) for m in range(0, 1 << b, 2)]
    hops.sort(key=lambda hop: (hop & hop - 1) == 0)
    messages = pl.pallas_call(
        functools.partial(pair_kernel, [bits_of(hop) for hop in hops]),
        in_specs=[in_vmem] * 2,
        out_specs=[in_vmem] * len(hops),
        out_shape=[pltpu.VMEM((half, *square), F32)] * len(hops),
        compiler_params=params(2),
        cost_estimate=cost(size, size),
        name="pair",
    )(keep, found)
    *messages, everything = lax.optimization_barrier((*messages, everything))
    arrived = [permute(x, hop) for hop, x in zip(hops, messages)]
    first = permute(everything, 1)
    *parts, gin = pl.pallas_call(
        local_kernel,
        in_specs=[in_vmem] * 7,
        out_specs=[in_vmem] * 4,
        out_shape=[natural] * 3 + [pltpu.VMEM((chunks, heads, *square), F32)],
        scratch_shapes=[pltpu.VMEM((tile, tile), F32), pltpu.VMEM((heads, *square), BF16)],
        compiler_params=params(3),
        cost_estimate=cost(14 * size * tile, 4 * size),
        name="local",
    )(lam, kh, vh, qt, gh, level_state, first)
    arrived, parts = lax.optimization_barrier((arrived, parts))
    sums_shape = (tree_bits - 1, half, *square)
    mine = pl.pallas_call(
        functools.partial(sum_kernel, [bits_of(hop) for hop in hops]),
        in_specs=[in_vmem] * len(hops),
        out_specs=in_vmem,
        out_shape=pltpu.VMEM(sums_shape, F32),
        compiler_params=params(2),
        cost_estimate=cost(size, size),
        name="sums",
    )(*arrived)
    others = permute(mine, 1)

    kept = [
        pltpu.VMEM((half, (tree_bits - 1) * width, width), BF16),
        pltpu.VMEM((half, *square), F32),
    ]
    gin, mine = near(gin, mine)
    *parts, wide = pl.pallas_call(
        functools.partial(own_half_kernel, local_bits + 2),
        in_specs=[in_vmem] * 9,
        out_specs=[in_vmem] * 4,
        out_shape=[natural] * 3 + [pltpu.VMEM((chunks, tree_bits - 1, tile, width), F32)],
        input_output_aliases={6: 0, 7: 1, 8: 2},
        scratch_shapes=kept,
        compiler_params=params(3),
        cost_estimate=cost((tree_bits + 2) * size * width, 8 * size),
        name="own_half",
    )(lam, kh, vh, gh, gin, mine, *near(*parts))
    others, parts = lax.optimization_barrier((others, parts))
    return pl.pallas_call(
        final_kernel,
        in_specs=[in_vmem] * 9,
        out_specs=[anywhere] * 3,
        out_shape=[pltpu.HBM((count, heads, width), BF16)] * 3,
        scratch_shapes=[
            pltpu.VMEM((3, chunks, tile, heads, width), BF16), *kept,
            pltpu.SemaphoreType.DMA((3, chunks, pieces)),
        ],
        compiler_params=params(10),
        cost_estimate=cost((tree_bits + 2) * size * width, 16 * size),
        name="final",
    )(*near(wide), kh, vh, gh, *near(*parts), gin, others)


def solution(mesh):
    tokens = P("seq", "head", None)
    return jax.shard_map(
        on_device,
        mesh=mesh,
        in_specs=(tokens, tokens, tokens, tokens, P(None, ("seq", "head"))),
        out_specs=(tokens, tokens, tokens),
        check_vma=False,
    )
```
